128 devices in a mesh: dp: 16 (over z, y), ctx: 8 (over x, core).
Axes of the slice: x: 4, y: 4, z: 4, core: 2. Of those that a mesh axis runs over, the one named last changes fastest.
Arguments:
- tokens: bfloat16 [16, 1024, 1024], P('dp', 'ctx'), may hold values from -6 to 6
- cotangent: bfloat16 [16, 1024, 1024], P('dp', 'ctx'), may hold values from -6 to 6
- gain_attn: bfloat16 [1, 1024], P(None, ('dp', 'ctx')), may hold values from 0.5 to 1.5
- gain_mlp: bfloat16 [1, 1024], P(None, ('dp', 'ctx')), may hold values from 0.5 to 1.5
- w_qkv: bfloat16 [1, 1024, 768], P(None, ('dp', 'ctx')), may hold values from -0.1875 to 0.1875
- w_o: bfloat16 [1, 512, 1024], P(None, ('dp', 'ctx')), may hold values from -2 to 2
- w_zx: bfloat16 [1, 1024, 3072], P(None, ('dp', 'ctx')), may hold values from -0.1875 to 0.1875
- w_side: bfloat16 [1, 1024, 280], P(None, ('dp', 'ctx')), may hold values from -0.1875 to 0.1875
- w_out: bfloat16 [1, 1536, 1024], P(None, ('dp', 'ctx')), may hold values from -0.078125 to 0.078125
- w_gu: bfloat16 [1, 1024, 4096], P(None, ('dp', 'ctx')), may hold values from -0.1875 to 0.1875
- w_down: bfloat16 [1, 2048, 1024], P(None, ('dp', 'ctx')), may hold values from -0.125 to 0.125
- conv_w: bfloat16 [1, 4, 1792], P(None, None, ('dp', 'ctx')), may hold values from -3 to 3
- conv_bias: bfloat16 [1, 1792], P(None, ('dp', 'ctx')), may hold values from -3 to 3
- a_log: float32 [1, 24], replicated, may hold values from -6.5 to 0
- dt_bias: float32 [1, 24], replicated, may hold values from -4 to -2
- d_skip: float32 [1, 24], replicated, may hold values from 0 to 2
Outputs:
- block_out: float32 [16, 1024, 1024], P('dp', 'ctx')
- grad_tokens: float32 [16, 1024, 1024], P('dp', 'ctx')
- grad_gain_attn: float32 [1, 1024], P(None, ('dp', 'ctx'))
- grad_gain_mlp: float32 [1, 1024], P(None, ('dp', 'ctx'))
- grad_qkv: float32 [1, 1024, 768], P(None, ('dp', 'ctx'))
- grad_o: float32 [1, 512, 1024], P(None, ('dp', 'ctx'))
- grad_zx: float32 [1, 1024, 3072], P(None, ('dp', 'ctx'))
- grad_side: float32 [1, 1024, 280], P(None, ('dp', 'ctx'))
- grad_out: float32 [1, 1536, 1024], P(None, ('dp', 'ctx'))
- grad_gu: float32 [1, 1024, 4096], P(None, ('dp', 'ctx'))
- grad_down: float32 [1, 2048, 1024], P(None, ('dp', 'ctx'))
- grad_conv_w: float32 [1, 4, 1792], P(None, None, ('dp', 'ctx'))
- grad_conv_bias: float32 [1, 1792], P(None, ('dp', 'ctx'))
- grad_a_log: float32 [1, 24], replicated
- grad_dt_bias: float32 [1, 24], replicated
- grad_d_skip: float32 [1, 24], replicated
The draws below stay inside these ranges and needn't reach their ends.
All inputs are finite; a program needn't handle non-finite values.
Results may differ from the reference program's by a relative error of at most 0.023.
Values may be sent and summed in bfloat16 or wider, within the bound.
No kernel may reach another device: no remote copies, remote signals or barrier semaphores. Data moves between devices by JAX's collectives and lax.ppermute only.
A program may use at most 192 MiB of HBM per device.

```python
import math
import jax
import jax.numpy as jnp
from jax import lax

D = 1024
QUERY_HEADS = 8
KEY_VALUE_HEADS = 2
HEAD_SIZE = 64
SH = 24
SP = 64
SN = 128
FF = 2048
KW = 4
LAYERS = 1
BLK = 128
QUERY_FEATURES = 512
KEY_FEATURES = 128
QKV = 768
INNER = 1536
SIDE = 280
CONV = 1792
SEQUENCE_LENGTH = 1024
SEQS = 16


def levels(key, dims, split, low, largest):
    def one(axis_at, blocks):
        heights = jax.random.uniform(jax.random.fold_in(jax.random.fold_in(key, 6), axis_at), (blocks,), jnp.float32, low / len(split), largest / len(split))
        return jnp.repeat(jnp.exp(heights), dims[axis_at] // blocks).reshape((-1,) + (1,) * (len(dims) - axis_at - 1))

    factor_of = one(*split[0])
    for cut in split[1:]:
        factor_of = factor_of * one(*cut)
    return factor_of


def noise(key, dims, deviation, most, pieces=(), kind=jnp.bfloat16):
    drawn = deviation * jax.random.normal(key, dims, jnp.float32)
    if pieces:
        drawn = drawn * levels(key, dims, pieces, -0.22, 0.18)
    return jnp.clip(drawn, -most, most).astype(kind)


def setup_inputs(seed: int = 0) -> dict:
    streams_of = jax.random.split(jax.random.key(seed), 17)
    tokens = noise(streams_of[0], (SEQS, SEQUENCE_LENGTH, D), 1.0, 6.0, ((0, 16), (1, 8)))
    cotangent = noise(streams_of[1], (SEQS, SEQUENCE_LENGTH, D), 1.0, 6.0, ((0, 16), (1, 8)))
    gain_attn = jnp.clip(1.0 + 0.1 * jax.random.normal(streams_of[2], (LAYERS, D), jnp.float32), 0.5, 1.5).astype(jnp.bfloat16)
    gain_mlp = jnp.clip(1.0 + 0.1 * jax.random.normal(streams_of[3], (LAYERS, D), jnp.float32), 0.5, 1.5).astype(jnp.bfloat16)
    w_qkv = noise(streams_of[4], (LAYERS, D, QKV), D ** -0.5, 0.1875, ((1, 128),))
    w_o = noise(streams_of[5], (LAYERS, QUERY_FEATURES, D), (HEAD_SIZE // 8) ** -0.5, 2.0, ((1, 128),))
    w_zx = noise(streams_of[6], (LAYERS, D, 2 * INNER), D ** -0.5, 0.1875, ((1, 128),))
    w_side = noise(streams_of[7], (LAYERS, D, SIDE), D ** -0.5, 0.1875, ((1, 128),))
    w_out = noise(streams_of[8], (LAYERS, INNER, D), (4 * INNER) ** -0.5, 0.078125, ((1, 128),))
    w_gu = noise(streams_of[9], (LAYERS, D, 2 * FF), D ** -0.5, 0.1875, ((1, 128),))
    w_down = noise(streams_of[10], (LAYERS, FF, D), FF ** -0.5, 0.125, ((1, 128),))
    conv_w = noise(streams_of[11], (LAYERS, KW, CONV), KW ** -0.5, 3.0, ((2, 128),))
    conv_bias = noise(streams_of[12], (LAYERS, CONV), 0.5, 3.0, ((1, 128),))
    a_log = jnp.clip(jax.random.uniform(streams_of[13], (LAYERS, SH), jnp.float32, -6.5, 0.0), -6.5, 0.0)
    dt_bias = jnp.clip(jax.random.uniform(streams_of[14], (LAYERS, SH), jnp.float32, -4.0, -2.0), -4.0, -2.0)
    d_skip = jnp.clip(jax.random.uniform(streams_of[15], (LAYERS, SH), jnp.float32, 0.0, 2.0), 0.0, 2.0)
    return dict(tokens=tokens, cotangent=cotangent, gain_attn=gain_attn, gain_mlp=gain_mlp, w_qkv=w_qkv, w_o=w_o, w_zx=w_zx, w_side=w_side, w_out=w_out, w_gu=w_gu, w_down=w_down, conv_w=conv_w, conv_bias=conv_bias, a_log=a_log, dt_bias=dt_bias, d_skip=d_skip)


HIGHEST = lax.Precision.HIGHEST
EPSILON = 1e-05
ROPE_BASE = 100000000000.0

@jax.custom_vjp
def low(v):
    return lax.optimization_barrier(v.astype(jnp.bfloat16)).astype(jnp.float32)

@jax.custom_vjp
def low_back(v):
    return v

def low_keep(v):
    return (low(v), None)

def low_pass(kept, grad):
    return (grad,)

def back_keep(v):
    return (v, None)

def back_low(kept, grad):
    return (low(grad),)
low.defvjp(low_keep, low_pass)
low_back.defvjp(back_keep, back_low)

def round_both(value_heads_rows):
    return low(low_back(value_heads_rows))

def matmul_high(left, right):
    return jnp.dot(left, right, precision=HIGHEST)

def rms_norm(hidden_in, gain):
    factor = lax.rsqrt(lax.optimization_barrier(jnp.mean(hidden_in * hidden_in, axis=-1, keepdims=True)) + EPSILON)
    return hidden_in * factor * gain

def rope_tables(positions):
    exponent = -(2.0 * jnp.arange(HEAD_SIZE // 2, dtype=jnp.float32)) / HEAD_SIZE
    inverse = jnp.power(jnp.float32(ROPE_BASE), exponent)
    angles = positions.astype(jnp.float32)[:, None] * inverse[None, :]
    cosine_table = jnp.concatenate([jnp.cos(angles), jnp.cos(angles)], axis=1)
    sine_lookup = jnp.concatenate([jnp.sin(angles), jnp.sin(angles)], axis=1)
    return (cosine_table, sine_lookup)

def apply_rotary(values, cosine_table, sine_lookup):
    half_width = values.shape[-1] // 2
    turned = jnp.concatenate([-values[..., half_width:], values[..., :half_width]], axis=-1)
    return values * cosine_table + turned * sine_lookup

def conv_part(extended, taps, conv_bias):
    number_of_rows = extended.shape[0] - (KW - 1)
    total = conv_bias[None, :] + jnp.zeros((number_of_rows, extended.shape[1]), jnp.float32)
    for offset in range(KW):
        total = total + taps[offset][None, :] * extended[offset:offset + number_of_rows]
    return jax.nn.silu(total)

def ssd_block(carried, block_in):
    inputs_x, input_b, input_c, log_decay, dt_step = block_in
    block_length = log_decay.shape[0]
    cumulative = jnp.cumsum(log_decay, axis=0)
    places = jnp.arange(block_length, dtype=jnp.int32)
    causal = places[:, None] >= places[None, :]
    log_gap = jnp.where(causal[:, :, None], cumulative[:, None, :] - cumulative[None, :, :], -jnp.inf)
    intersection = jnp.dot(input_c, input_b.T, precision=HIGHEST)
    mixing = intersection[:, :, None] * jnp.exp(log_gap) * dt_step[None, :, :]
    output = jnp.einsum('tsh,shp->thp', mixing, inputs_x, precision=HIGHEST)
    output = output + jnp.einsum('tn,hpn->thp', input_c, carried, precision=HIGHEST) * jnp.exp(cumulative)[:, :, None]
    to_end = jnp.exp(cumulative[-1][None, :] - cumulative) * dt_step
    leaving = carried * jnp.exp(cumulative[-1])[:, None, None] + jnp.einsum('sh,shp,sn->hpn', to_end, inputs_x, input_b, precision=HIGHEST)
    return (leaving, output)

def ssd_core(inputs_x, input_b, input_c, log_decay, dt_step, entering):
    number_of_blocks = inputs_x.shape[0] // BLK
    blocks = (inputs_x.reshape(number_of_blocks, BLK, SH, SP), input_b.reshape(number_of_blocks, BLK, SN), input_c.reshape(number_of_blocks, BLK, SN), log_decay.reshape(number_of_blocks, BLK, SH), dt_step.reshape(number_of_blocks, BLK, SH))
    leaving, outputs = lax.scan(jax.checkpoint(ssd_block), entering, blocks)
    return (leaving, outputs.reshape(number_of_blocks * BLK, SH, SP))

def attention(query_heads_rows, key, value_heads_rows):
    query_group_size = QUERY_HEADS // KEY_VALUE_HEADS
    block_length = min(512, SEQUENCE_LENGTH)
    number_of_blocks = SEQUENCE_LENGTH // block_length
    score_scale = 1.0 / math.sqrt(HEAD_SIZE)
    query_block_list = query_heads_rows.reshape(number_of_blocks, block_length, KEY_VALUE_HEADS, query_group_size, HEAD_SIZE)
    key_pos = jnp.arange(SEQUENCE_LENGTH, dtype=jnp.int32)

    def one_block(pair):
        block_in, block_index = pair
        raw_scores = low_back(jnp.einsum('tgqd,sgd->gqts', block_in, key, precision=HIGHEST))
        query_pos = block_index * block_length + jnp.arange(block_length, dtype=jnp.int32)
        allowed = query_pos[:, None] >= key_pos[None, :]
        scores = jnp.where(allowed, raw_scores * score_scale, -jnp.inf)
        probabilities = low(jax.nn.softmax(scores, axis=-1))
        result = jnp.einsum('gqts,sgd->tgqd', probabilities, value_heads_rows, precision=HIGHEST)
        return result.reshape(block_length, QUERY_FEATURES)
    outputs = lax.map(jax.checkpoint(one_block), (query_block_list, jnp.arange(number_of_blocks, dtype=jnp.int32)))
    return outputs.reshape(SEQUENCE_LENGTH, QUERY_FEATURES)

def layer(residual, params):
    gain_attn, gain_mlp, w_qkv, w_o, w_zx, w_side, w_out, w_gu, w_down, conv_w, conv_bias, a_log, dt_bias, d_skip = params
    normed = low(rms_norm(residual, gain_attn))
    query_key_value_weight = low_back(matmul_high(normed, w_qkv))
    cosine_table, sine_lookup = rope_tables(jnp.arange(SEQUENCE_LENGTH, dtype=jnp.int32))
    query_heads_rows = low(apply_rotary(query_key_value_weight[:, :QUERY_FEATURES].reshape(SEQUENCE_LENGTH, KEY_VALUE_HEADS, QUERY_HEADS // KEY_VALUE_HEADS, HEAD_SIZE), cosine_table[:, None, None, :], sine_lookup[:, None, None, :]))
    key = low(apply_rotary(query_key_value_weight[:, QUERY_FEATURES:QUERY_FEATURES + KEY_FEATURES].reshape(SEQUENCE_LENGTH, KEY_VALUE_HEADS, HEAD_SIZE), cosine_table[:, None, :], sine_lookup[:, None, :]))
    value_heads_rows = low(query_key_value_weight[:, QUERY_FEATURES + KEY_FEATURES:]).reshape(SEQUENCE_LENGTH, KEY_VALUE_HEADS, HEAD_SIZE)
    attention_output = round_both(attention(query_heads_rows, key, value_heads_rows))
    branch_attn = low_back(matmul_high(attention_output, w_o))
    mixed_proj = low_back(matmul_high(normed, w_zx))
    gate_z = mixed_proj[:, :INNER]
    side_proj = low_back(matmul_high(normed, w_side))
    conv_in = low(jnp.concatenate([mixed_proj[:, INNER:], side_proj[:, :2 * SN]], axis=1))
    extended = jnp.concatenate([jnp.zeros((KW - 1, CONV), conv_in.dtype), conv_in], axis=0)
    activated = conv_part(extended, conv_w, conv_bias)
    inputs_x = low(activated[:, :INNER]).reshape(SEQUENCE_LENGTH, SH, SP)
    input_b = low(activated[:, INNER:INNER + SN])
    input_c = low(activated[:, INNER + SN:])
    dt_step = jax.nn.softplus(side_proj[:, 2 * SN:] + dt_bias)
    log_decay = -jnp.exp(a_log) * dt_step
    _, ssm_y = ssd_core(inputs_x, input_b, input_c, log_decay, dt_step, jnp.zeros((SH, SP, SN), jnp.float32))
    ssm_y = ssm_y + d_skip[None, :, None] * inputs_x
    gated = low(ssm_y.reshape(SEQUENCE_LENGTH, INNER) * jax.nn.silu(gate_z))
    middle = residual + branch_attn + low_back(matmul_high(gated, w_out))
    normed2 = low(rms_norm(middle, gain_mlp))
    gate_up = low_back(matmul_high(normed2, w_gu))
    hidden = low(jax.nn.silu(gate_up[:, :FF]) * gate_up[:, FF:])
    return middle + low_back(matmul_high(hidden, w_down))

def reference(tokens, cotangent, gain_attn, gain_mlp, w_qkv, w_o, w_zx, w_side, w_out, w_gu, w_down, conv_w, conv_bias, a_log, dt_bias, d_skip):
    weights = tuple((weight.astype(jnp.float32) for weight in (gain_attn, gain_mlp, w_qkv, w_o, w_zx, w_side, w_out, w_gu, w_down, conv_w, conv_bias, a_log, dt_bias, d_skip)))

    def forward(seq_tokens, params):
        residual = seq_tokens
        for layer_index in range(LAYERS):
            residual = layer(residual, tuple((weight[layer_index] for weight in params)))
        return residual

    def per_sequence(totals, pair):
        seq_tokens, seq_cot = pair
        result, pull = jax.vjp(forward, seq_tokens, weights)
        input_gradient, grad_weights = pull(seq_cot)
        totals = jax.tree.map(jnp.add, totals, grad_weights)
        return (totals, (result, input_gradient))
    zeros = jax.tree.map(jnp.zeros_like, weights)
    totals, (block_out, grad_tokens) = lax.scan(per_sequence, zeros, (tokens.astype(jnp.float32), cotangent.astype(jnp.float32)))
    return (block_out, grad_tokens, totals[0], totals[1], totals[2], totals[3], totals[4], totals[5], totals[6], totals[7], totals[8], totals[9], totals[10], totals[11], totals[12], totals[13])
```

```python
import math

import jax
import jax.numpy as jnp
from jax import lax
from jax.sharding import PartitionSpec as P

D = 1024
HEAD_SIZE = 64
SH = 24
SP = 64
SN = 128
FF = 2048
KW = 4
BLK = 128
INNER = 1536
CONV = 1792
QUERY_FEATURES = 512
KEY_FEATURES = 128
NDP = 16
NCTX = 8
CHIPS = 4
HPD = SH // NCTX
XC = INNER // NCTX
HID = FF // NCTX
GA = 2 * XC + 2 * SN + 3 * HEAD_SIZE + 64
X0, B0, Q0, K0, V0, T0 = XC, 2 * XC, 2 * XC + 2 * SN, 2 * XC + 2 * SN + 64, 2 * XC + 2 * SN + 128, 2 * XC + 2 * SN + 192

EPSILON = 1e-05
ROPE_BASE = 100000000000.0
F32 = jnp.float32
BF16 = jnp.bfloat16
HIGHEST = lax.Precision.HIGHEST


def dot(a, b, dims):
    return lax.dot_general(a, b, (dims, ((), ())), preferred_element_type=F32)


def mm(a, b):
    return dot(a, b, ((1,), (0,)))


def mm_nt(a, b):
    return dot(a, b, ((1,), (1,)))


def mm_tn(a, b):
    return dot(a, b, ((0,), (0,)))


def chip_shift(array, by):
    return lax.ppermute(array, "ctx", [(i, (i + 2 * by) % NCTX) for i in range(NCTX)])


def core_swap(array):
    return lax.ppermute(array, "ctx", [(i, i ^ 1) for i in range(NCTX)])


def gather_rows(own):
    half = own.shape[0] // 2
    after = chip_shift(own, -1)
    before = chip_shift(own, 1)
    far_top = chip_shift(after[:half], -1)
    far_low = chip_shift(before[half:], 1)
    far = jnp.concatenate([far_top, far_low], axis=0)
    blocks = []
    for block in (own, after, far, before):
        blocks += [block, core_swap(block)]
    return jnp.concatenate(blocks, axis=0)


def scatter_rows(partial):
    rows = partial.shape[0] // NCTX
    half = rows // 2
    block = lambda r: partial[r * rows : (r + 1) * rows]
    both = [None] * CHIPS
    for k in (2, 1, 3, 0):
        both[k] = block(2 * k) + core_swap(block(2 * k + 1).astype(BF16)).astype(F32)
    far = both[2].astype(BF16)
    from_before = chip_shift(far[:half], 1).astype(F32)
    from_after = chip_shift(far[half:], -1).astype(F32)
    low_next = chip_shift(both[1][half:].astype(BF16), 1)
    top_prev = chip_shift(both[3][:half].astype(BF16), -1)
    top_next = chip_shift((both[1][:half] + from_before).astype(BF16), 1)
    low_prev = chip_shift((both[3][half:] + from_after).astype(BF16), -1)
    next_part = jnp.concatenate([top_next, low_next], axis=0).astype(F32)
    prev_part = jnp.concatenate([top_prev, low_prev], axis=0).astype(F32)
    return both[0] + next_part + prev_part


def dp_gather(own):
    return lax.all_to_all(jnp.broadcast_to(own[None], (NDP,) + own.shape), "dp", 0, 0)


def dp_sum(parts):
    return jnp.sum(lax.all_to_all(parts.astype(BF16), "dp", 0, 0).astype(F32), axis=0)


def rms_factor(hidden_in):
    return lax.rsqrt(jnp.mean(hidden_in * hidden_in, axis=-1, keepdims=True) + EPSILON)


def norm_back(hidden_in, factor, gain, upstream):
    scaled = upstream * gain
    inner = jnp.mean(scaled * hidden_in, axis=-1, keepdims=True)
    return factor * scaled - hidden_in * (factor * factor * factor) * inner


def rope_tables(positions):
    exponent = -(2.0 * jnp.arange(HEAD_SIZE // 2, dtype=F32)) / HEAD_SIZE
    inverse = jnp.power(jnp.float32(ROPE_BASE), exponent)
    angles = positions.astype(F32)[:, None] * inverse[None, :]
    cosine, sine = jnp.cos(angles), jnp.sin(angles)
    return (jnp.concatenate([cosine, cosine], axis=1), jnp.concatenate([sine, sine], axis=1))


def apply_rotary(values, cosine, sine):
    half = HEAD_SIZE // 2
    turned = jnp.concatenate([-values[:, half:], values[:, :half]], axis=1)
    return values * cosine + turned * sine


def unrotate(grads, cosine, sine):
    half = HEAD_SIZE // 2
    product = grads * sine
    return grads * cosine + jnp.concatenate([product[:, half:], -product[:, :half]], axis=1)


def conv_act(conv_in, taps, bias, previous):
    blocks = conv_in.reshape(NCTX, BLK, conv_in.shape[1])
    rims = blocks[:, BLK - (KW - 1) :]
    rims = jnp.sum(previous[:, :, None, None] * rims[None], axis=1)
    extended = jnp.concatenate([rims, blocks], axis=1)
    total = bias[None, None, :]
    for offset in range(KW):
        total = total + taps[offset][None, None, :] * extended[:, offset : offset + BLK]
    return jax.nn.silu(total).reshape(conv_in.shape)


def mixer(inputs_x, input_b, input_c, gate, dt_raw, a_log, dt_bias, d_skip, order):
    step = jax.nn.softplus(dt_raw + dt_bias)
    decay = -jnp.exp(a_log) * step
    per_head = lambda v: v.reshape(NCTX, BLK, HPD).transpose(0, 2, 1)
    step, decay = per_head(step), per_head(decay)
    x = inputs_x.reshape(NCTX, BLK, HPD, SP).transpose(0, 2, 1, 3)
    b = input_b.reshape(NCTX, BLK, SN)
    c = input_c.reshape(NCTX, BLK, SN)
    places = jnp.arange(BLK, dtype=jnp.int32)
    causal = places[:, None] >= places[None, :]
    cumulative = jnp.einsum("nhs,ts->nht", decay, causal.astype(F32), precision=HIGHEST)
    gap = jnp.where(causal, cumulative[:, :, :, None] - cumulative[:, :, None, :], -jnp.inf)
    inter = jnp.einsum("ntk,nsk->nts", c, b)
    mixing = inter[:, None] * jnp.exp(gap) * step[:, :, None, :]
    y = jnp.einsum("nhts,nhsp->nhtp", mixing, x)
    last = cumulative[:, :, -1]
    to_end = jnp.exp(last[:, :, None] - cumulative) * step
    local = jnp.einsum("nhsp,nsk->nhpk", x * to_end[..., None], b)
    upto = (order[:, None] >= order[None, :]).astype(F32)
    running = jnp.sum(upto[:, :, None] * last[None], axis=1)
    span = (running - last)[:, None, :] - running[None, :, :]
    earlier = (order[:, None] > order[None, :])[:, :, None]
    weight = jnp.exp(jnp.where(earlier, span, -jnp.inf))
    entering = jnp.einsum("bch,chpk->bhpk", weight, local)
    y = y + jnp.exp(cumulative)[..., None] * jnp.einsum("ntk,nhpk->nhtp", c, entering)
    y = y + d_skip[None, :, None, None] * x
    y = y.transpose(0, 2, 1, 3).reshape(NCTX * BLK, XC)
    return y * jax.nn.silu(gate)


def per_device(
    tokens,
    cotangent,
    gain_attn,
    gain_mlp,
    w_qkv,
    w_o,
    w_zx,
    w_side,
    w_out,
    w_gu,
    w_down,
    conv_w,
    conv_bias,
    a_log,
    dt_bias,
    d_skip,
):
    ctx = lax.axis_index("ctx")
    chip, core = ctx // 2, ctx % 2
    offsets = jnp.arange(NCTX, dtype=jnp.int32)
    order = 2 * ((chip + offsets // 2) % CHIPS) + (core ^ (offsets % 2))
    positions = (order[:, None] * BLK + jnp.arange(BLK, dtype=jnp.int32)[None, :]).reshape(-1)
    previous = (order[:, None] == order[None, :] + 1).astype(F32)
    own_tokens, own_cot = tokens[0], cotangent[0]
    gain_attn, gain_mlp, conv_w, conv_bias = gain_attn[0], gain_mlp[0], conv_w[0], conv_bias[0]
    w_qkv, w_o, w_zx, w_side, w_out, w_gu, w_down = (
        w[0] for w in (w_qkv, w_o, w_zx, w_side, w_out, w_gu, w_down)
    )
    rows = w_qkv.shape[0]

    cut = lambda v: v.reshape(rows, NCTX, -1).transpose(1, 0, 2)
    group = NCTX // 2
    to_all = lambda v: jnp.broadcast_to(v[None], (NCTX,) + v.shape)
    keys = lambda v: jnp.repeat(v.reshape(rows, 2, HEAD_SIZE).transpose(1, 0, 2), group, axis=0)
    hidden_cols = lambda v: (
        v.reshape(rows, NDP, NCTX, HID // NDP).transpose(2, 0, 1, 3).reshape(NCTX, rows, HID)
    )
    columns = jnp.concatenate(
        [
            cut(w_zx[:, :INNER]),
            cut(w_zx[:, INNER:]),
            to_all(w_side[:, : 2 * SN]),
            cut(w_qkv[:, :QUERY_FEATURES]),
            keys(w_qkv[:, QUERY_FEATURES : QUERY_FEATURES + KEY_FEATURES]),
            keys(w_qkv[:, QUERY_FEATURES + KEY_FEATURES :]),
            cut(w_side[:, 2 * SN :]),
            jnp.zeros((NCTX, rows, 64 - HPD), BF16),
            hidden_cols(w_gu[:, :FF]),
            hidden_cols(w_gu[:, FF:]),
        ],
        axis=2,
    )
    small = jnp.concatenate([gain_attn, gain_mlp, conv_bias, conv_w.reshape(-1)])
    small = jnp.pad(small, (0, columns.shape[2] - small.shape[0]))
    columns = jnp.concatenate([columns, jnp.broadcast_to(small, (NCTX, 1, small.shape[0]))], axis=1)
    columns = lax.all_to_all(columns, "ctx", 0, 0)
    weight_part = columns[:, :rows].reshape(NCTX * rows, -1)
    mixers_part = jnp.concatenate([weight_part[:, :GA], columns[:, rows, :GA]], axis=0)
    mixers_all = dp_gather(mixers_part)
    wa = mixers_all[:, : NCTX * rows].reshape(D, GA)
    small = mixers_all[:, NCTX * rows :].reshape(NDP * NCTX, GA).astype(F32)
    per = D // (NDP * NCTX)
    cper = CONV // (NDP * NCTX)
    gain_a = small[:, :per].reshape(D)
    gain_m = small[:, per : 2 * per].reshape(D)
    bias_all = small[:, 2 * per : 2 * per + cper].reshape(CONV)
    taps_all = small[:, 2 * per + cper : 2 * per + 5 * cper].reshape(-1, KW, cper)
    taps_all = taps_all.transpose(1, 0, 2).reshape(KW, CONV)
    mine = lambda v: jnp.concatenate(
        [lax.dynamic_slice_in_dim(v, ctx * XC, XC, v.ndim - 1), v[..., INNER:]], axis=-1
    )
    taps, conv_b = mine(taps_all), mine(bias_all)

    tok = gather_rows(own_tokens).astype(F32)

    swap_pairs = [
        (c, NCTX * (c % NDP) + c // NDP) for c in range(NDP * NCTX)
    ]
    back_pairs = [(t, s) for s, t in swap_pairs]
    mix_rows = lax.ppermute(jnp.concatenate([w_o, w_out], axis=0), ("dp", "ctx"), swap_pairs)
    n_o, n_out, n_down = w_o.shape[0], w_out.shape[0], w_down.shape[0]
    mix_rows = dp_gather(mix_rows)
    w_mix = jnp.concatenate(
        [mix_rows[:, :n_o].reshape(HEAD_SIZE, D), mix_rows[:, n_o:].reshape(XC, D)], axis=0
    )
    gu = dp_gather(weight_part[:, GA:]).reshape(D, 2 * HID)
    down = dp_gather(w_down).reshape(HID, D)
    cot = gather_rows(own_cot)

    normed = (tok * rms_factor(tok) * gain_a[None, :]).astype(BF16)
    proj = mm(normed, wa)
    cosine, sine = rope_tables(positions)
    query = apply_rotary(proj[:, Q0:K0], cosine, sine).astype(BF16)
    key = apply_rotary(proj[:, K0:V0], cosine, sine).astype(BF16)
    value = proj[:, V0:T0].astype(BF16)
    scale = 1.0 / math.sqrt(HEAD_SIZE)
    scores = jnp.where(positions[:, None] >= positions[None, :], mm_nt(query, key) * scale, -jnp.inf)
    peak = jnp.max(scores, axis=1, keepdims=True)
    weights = jnp.exp(scores - peak)
    probs = weights / jnp.sum(weights, axis=1, keepdims=True)
    probs_low = probs.astype(BF16)
    attended = mm(probs_low, value)
    conv_in = proj[:, X0:Q0].astype(BF16).astype(F32)
    activated, pull_conv = jax.vjp(
        lambda v, t, b: conv_act(v, t, b, previous), conv_in, taps, conv_b
    )
    activated = activated.astype(BF16).astype(F32)
    heads = lambda v: lax.dynamic_slice_in_dim(v[0], ctx * HPD, HPD, 0)
    gated, pull_mixer = jax.vjp(
        lambda *v: mixer(*v, order),
        activated[:, :XC],
        activated[:, XC : XC + SN],
        activated[:, XC + SN :],
        proj[:, :XC],
        proj[:, T0 : T0 + HPD],
        heads(a_log),
        heads(dt_bias),
        heads(d_skip),
    )
    mixed = jnp.concatenate([attended.astype(BF16), gated.astype(BF16)], axis=1)
    own_residual = own_tokens.astype(F32)
    middle = own_residual + scatter_rows(mm(mixed, w_mix))

    factor_m = rms_factor(middle)
    normed2 = gather_rows((middle * factor_m * gain_m[None, :]).astype(BF16))
    gate_up = mm(normed2, gu)
    gate_half, up_half = gate_up[:, :HID], gate_up[:, HID:]
    sigmoid_gate = jax.nn.sigmoid(gate_half)
    silu_gate = gate_half * sigmoid_gate
    hidden = (silu_gate * up_half).astype(BF16)
    grad_hidden = mm_nt(cot, down)
    grad_gate_up = jnp.concatenate(
        [
            grad_hidden * up_half * sigmoid_gate * (1.0 + gate_half * (1.0 - sigmoid_gate)),
            grad_hidden * silu_gate,
        ],
        axis=1,
    ).astype(BF16)
    grad_normed2 = scatter_rows(mm_nt(grad_gate_up, gu))
    grad_middle = own_cot.astype(F32) + norm_back(middle, factor_m, gain_m[None, :], grad_normed2)
    middle_low = gather_rows(grad_middle.astype(BF16))
    block_out = middle + scatter_rows(mm(hidden, down))
    grad_gu = mm_tn(normed2, grad_gate_up)
    grad_down = mm_tn(hidden, cot)

    grad_mixed = mm_nt(middle_low, w_mix)
    grad_mix = mm_tn(mixed, middle_low)
    grad_attended = grad_mixed[:, :HEAD_SIZE].astype(BF16)
    grad_probs = mm_nt(grad_attended, value)
    delta = jnp.sum(grad_attended.astype(F32) * attended, axis=1, keepdims=True)
    grad_scores = (scale * probs * (grad_probs - delta)).astype(BF16)
    grad_query = unrotate(mm(grad_scores, key), cosine, sine)
    grad_key = unrotate(mm_tn(grad_scores, query), cosine, sine)
    grad_value = mm_tn(probs_low, grad_attended)
    grad_x, grad_b, grad_c, grad_gate, grad_dt, grad_alog, grad_bias, grad_skip = pull_mixer(
        grad_mixed[:, HEAD_SIZE:]
    )
    grad_conv_in, grad_taps, grad_conv_b = pull_conv(
        jnp.concatenate([grad_x, grad_b, grad_c], axis=1)
    )
    grad_proj = jnp.concatenate(
        [
            grad_gate,
            grad_conv_in,
            grad_query,
            grad_key,
            grad_value,
            grad_dt,
            jnp.zeros((NCTX * BLK, 64 - HPD), F32),
        ],
        axis=1,
    ).astype(BF16)
    grad_normed = scatter_rows(mm_nt(grad_proj, wa))
    grad_tokens = grad_middle + norm_back(
        own_residual, rms_factor(own_residual), gain_a[None, :], grad_normed
    )
    grad_wa = mm_tn(normed, grad_proj)

    place = lambda v, at, size: lax.dynamic_update_slice_in_dim(
        jnp.zeros(v.shape[:-1] + (size,), F32), v, at, v.ndim - 1
    )
    conv_terms = jnp.concatenate([grad_conv_b[None], grad_taps], axis=0)
    conv_terms = jnp.concatenate(
        [place(conv_terms[:, :XC], ctx * XC, INNER), conv_terms[:, XC:]], axis=1
    )
    conv_terms = conv_terms.reshape(KW + 1, NDP * NCTX, cper).transpose(1, 0, 2)
    head_terms = place(jnp.stack([grad_alog, grad_bias, grad_skip]), ctx * HPD, SH)
    n_conv, n_head = (KW + 1) * cper, 3 * SH
    small_terms = jnp.concatenate(
        [
            conv_terms.reshape(NDP * NCTX, n_conv),
            jnp.broadcast_to(head_terms.reshape(1, n_head), (NDP * NCTX, n_head)),
        ],
        axis=1,
    )
    coarse = small_terms.astype(BF16).astype(F32)
    n_small = n_conv + n_head
    small_terms = jnp.concatenate([coarse, small_terms - coarse], axis=1)
    small_terms = jnp.pad(small_terms, ((0, 0), (0, GA - 2 * n_small)))
    sent = jnp.concatenate(
        [
            grad_wa.reshape(NDP, NCTX * rows, GA),
            small_terms.reshape(NDP, NCTX, GA),
        ],
        axis=1,
    )
    sum_gu = dp_sum(grad_gu.reshape(NDP, NCTX * rows, 2 * HID))
    sum_down = dp_sum(grad_down.reshape(NDP, n_down, D))
    sum_mix = dp_sum(
        jnp.concatenate(
            [
                grad_mix[:HEAD_SIZE].reshape(NDP, n_o, D),
                grad_mix[HEAD_SIZE:].reshape(NDP, n_out, D),
            ],
            axis=1,
        )
    )
    sum_mix = lax.ppermute(sum_mix, ("dp", "ctx"), back_pairs)
    got_gu = lax.all_to_all(sum_gu.reshape(NCTX, rows, 2 * HID), "ctx", 0, 0)
    hidden_back = lambda v: (
        v.reshape(NCTX, rows, NDP, HID // NDP).transpose(1, 2, 0, 3).reshape(rows, FF)
    )
    out_gu = jnp.concatenate(
        [hidden_back(got_gu[:, :, :HID]), hidden_back(got_gu[:, :, HID:])], axis=1
    )
    sum_a = dp_sum(sent)
    sum_a = jnp.concatenate(
        [
            sum_a[: NCTX * rows].reshape(NCTX, rows, GA),
            sum_a[NCTX * rows :].reshape(NCTX, 1, GA),
        ],
        axis=1,
    )
    got = lax.all_to_all(sum_a, "ctx", 0, 0)
    small_got = jnp.sum(got[:, rows], axis=0)
    small_got = small_got[:n_small] + small_got[n_small : 2 * n_small]
    got = got[:, :rows]
    uncut = lambda v: v.transpose(1, 0, 2).reshape(rows, -1)
    keys_back = lambda v: uncut(jnp.sum(v.reshape(2, group, rows, HEAD_SIZE), axis=1))
    out_zx = jnp.concatenate([uncut(got[:, :, :X0]), uncut(got[:, :, X0:B0])], axis=1)
    out_side = jnp.concatenate(
        [jnp.sum(got[:, :, B0:Q0], axis=0), uncut(got[:, :, T0 : T0 + HPD])], axis=1
    )
    out_qkv = jnp.concatenate(
        [uncut(got[:, :, Q0:K0]), keys_back(got[:, :, K0:V0]), keys_back(got[:, :, V0:T0])], axis=1
    )
    row_sum = lambda w, g: jnp.sum(w.astype(F32) * g, axis=1)
    out_gain_a = (row_sum(w_qkv, out_qkv) + row_sum(w_zx, out_zx) + row_sum(w_side, out_side)) / (
        gain_attn.astype(F32)
    )
    out_gain_m = row_sum(w_gu, out_gu) / gain_mlp.astype(F32)
    out_conv = small_got[:n_conv].reshape(KW + 1, cper)
    out_heads = small_got[n_conv:].reshape(3, 1, SH)
    return (
        block_out[None],
        grad_tokens[None],
        out_gain_a[None],
        out_gain_m[None],
        out_qkv[None],
        sum_mix[:n_o][None],
        out_zx[None],
        out_side[None],
        sum_mix[n_o:][None],
        out_gu[None],
        sum_down[None],
        out_conv[1:][None],
        out_conv[0][None],
        out_heads[0],
        out_heads[1],
        out_heads[2],
    )


def solution(mesh):
    rows = P("dp", "ctx", None)
    vector = P(None, ("dp", "ctx"))
    matrix = P(None, ("dp", "ctx"), None)
    taps = P(None, None, ("dp", "ctx"))
    weights = (vector, vector) + (matrix,) * 7 + (taps, vector, P(), P(), P())
    return jax.shard_map(
        per_device,
        mesh=mesh,
        in_specs=(rows, rows) + weights,
        out_specs=(rows, rows) + weights,
        check_vma=False,
    )
```

```python
import functools
import math

import jax
import jax.numpy as jnp
from jax import lax
from jax.experimental import pallas as pl
from jax.experimental.pallas import tpu as pltpu
from jax.sharding import PartitionSpec as P

D = 1024
HEAD_SIZE = 64
SH = 24
SP = 64
SN = 128
FF = 2048
KW = 4
BLK = 128
INNER = 1536
CONV = 1792
QUERY_FEATURES = 512
KEY_FEATURES = 128
NDP = 16
NCTX = 8
CHIPS = 4
HPD = SH // NCTX
XC = INNER // NCTX
HID = FF // NCTX
CV = 2 * SN + XC
X0, Z0, Q0 = 2 * SN, CV, CV + XC
K0, V0, T0 = Q0 + HEAD_SIZE, Q0 + 2 * HEAD_SIZE, Q0 + 3 * HEAD_SIZE
GA = Q0 + 4 * HEAD_SIZE

EPSILON = 1e-05
ROPE_BASE = 100000000000.0
F32 = jnp.float32
BF16 = jnp.bfloat16
HIGHEST = lax.Precision.HIGHEST


def dot(a, b, dims):
    return lax.dot_general(a, b, (dims, ((), ())), preferred_element_type=F32)


def mm(a, b):
    return dot(a, b, ((1,), (0,)))


def mm_nt(a, b):
    return dot(a, b, ((1,), (1,)))


def mm_tn(a, b):
    return dot(a, b, ((0,), (0,)))


def chip_shift(array, by):
    return lax.ppermute(array, "ctx", [(i, (i + 2 * by) % NCTX) for i in range(NCTX)])


def core_swap(array):
    return lax.ppermute(array, "ctx", [(i, i ^ 1) for i in range(NCTX)])


def gather_rows(own):
    same = [own, chip_shift(own, -1), None, chip_shift(own, 1)]
    same[2] = chip_shift(own, 2)
    other = [None] * CHIPS
    for k in (0, 1, 3, 2):
        other[k] = core_swap(same[k])
    return [block for pair in zip(same, other) for block in pair]


def scatter_rows(keep, pass_on):
    total = None
    for k in (2, 1, 3, 0):
        both = keep[k] + core_swap(pass_on[k]).astype(F32)
        if k:
            both = chip_shift(both.astype(BF16), k).astype(F32)
        total = both if total is None else total + both
    return total


def dp_gather(own):
    return lax.all_to_all(jnp.broadcast_to(own[None], (NDP,) + own.shape), "dp", 0, 0)


def stacked_halves(v):
    half = v.shape[-1] // 2
    return jnp.concatenate([v[..., :half], v[..., half:]], axis=-2)


def side_halves(v):
    half = v.shape[-2] // 2
    return jnp.concatenate([v[..., :half, :], v[..., half:, :]], axis=-1)


def dp_sum(parts):
    return jnp.sum(lax.all_to_all(parts.astype(BF16), "dp", 0, 0).astype(F32), axis=0)


def after(value, *others):
    return lax.optimization_barrier((value,) + others)[0]


def mlp_kernel(na, nb, ca, cb, gu, down, keep_n, pass_n, keep_d, pass_d, hid, dgu):
    normed2 = jnp.concatenate([na[...], nb[...]], axis=0)
    cot = jnp.concatenate([ca[...], cb[...]], axis=0)
    gate_up = mm(normed2, gu[...])
    gate_half, up_half = gate_up[:, :HID], gate_up[:, HID:]
    sigmoid_gate = 1.0 / (1.0 + jnp.exp(-gate_half))
    silu_gate = gate_half * sigmoid_gate
    hidden = (silu_gate * up_half).astype(BF16)
    grad_hidden = mm_nt(cot, down[...])
    grad_gate = grad_hidden * up_half * (sigmoid_gate + silu_gate * (1.0 - sigmoid_gate))
    grad_gate_up = jnp.concatenate([grad_gate, grad_hidden * silu_gate], axis=1).astype(BF16)
    hid[...] = hidden
    dgu[...] = grad_gate_up
    grad_normed2 = mm_nt(grad_gate_up, gu[...])
    keep_n[...] = grad_normed2[:BLK]
    pass_n[...] = grad_normed2[BLK:].astype(BF16)
    out = mm(hidden, down[...])
    keep_d[...] = out[:BLK]
    pass_d[...] = out[BLK:].astype(BF16)


def mlp(na, nb, ca, cb, gu, down):
    shape = jax.ShapeDtypeStruct
    return pl.pallas_call(
        mlp_kernel,
        out_shape=(
            shape((BLK, D), F32),
            shape((BLK, D), BF16),
            shape((BLK, D), F32),
            shape((BLK, D), BF16),
            shape((2 * BLK, HID), BF16),
            shape((2 * BLK, 2 * HID), BF16),
        ),
        cost_estimate=pl.CostEstimate(
            flops=8 * 2 * BLK * D * HID * 3 // 2, bytes_accessed=5_000_000, transcendentals=0
        ),
        compiler_params=pltpu.CompilerParams(vmem_limit_bytes=40 * 1024 * 1024),
        name="feed_forward",
    )(na, nb, ca, cb, gu, down)


def tn_kernel(n_left, *refs):
    left = jnp.concatenate([r[...] for r in refs[:n_left]], axis=0)
    right = jnp.concatenate([r[...] for r in refs[n_left:-1]], axis=0)
    refs[-1][...] = mm_tn(left, right).astype(BF16)


def tn_sum(left, right):
    n, m = left[0].shape[1], right[0].shape[1]
    return pl.pallas_call(
        functools.partial(tn_kernel, len(left)),
        out_shape=jax.ShapeDtypeStruct((n, m), BF16),
        cost_estimate=pl.CostEstimate(
            flops=2 * n * m * NCTX * BLK, bytes_accessed=6 * n * m, transcendentals=0
        ),
        compiler_params=pltpu.CompilerParams(vmem_limit_bytes=40 * 1024 * 1024),
        name="weight_grad",
    )(*left, *right)


def rms_factor(hidden_in):
    return lax.rsqrt(jnp.mean(hidden_in * hidden_in, axis=-1, keepdims=True) + EPSILON)


def norm_back(hidden_in, factor, gain, upstream):
    scaled = upstream * gain
    inner = jnp.mean(scaled * hidden_in, axis=-1, keepdims=True)
    return factor * scaled - hidden_in * (factor * factor * factor) * inner


def rope_tables():
    exponent = -(2.0 * jnp.arange(HEAD_SIZE // 2, dtype=F32)) / HEAD_SIZE
    inverse = jnp.power(jnp.float32(ROPE_BASE), exponent)
    angles = jnp.arange(NCTX * BLK, dtype=F32)[:, None] * inverse[None, :]
    cosine, sine = jnp.cos(angles), jnp.sin(angles)
    return (
        jnp.concatenate([cosine] * 4, axis=1),
        jnp.concatenate([-sine, sine, -sine, sine], axis=1),
    )


def sigmoid(v):
    return 1.0 / (1.0 + jnp.exp(-v))


def softplus(v):
    return jnp.maximum(v, 0.0) + jnp.log1p(jnp.exp(-jnp.abs(v)))


def exact(a, b, dims):
    return lax.dot_general(a, b, (dims, ((), ())), precision=HIGHEST, preferred_element_type=F32)


def wide(columns):
    return jnp.concatenate([jnp.broadcast_to(c, (BLK, SP)) for c in columns], axis=1)


def tall(scalars):
    return jnp.concatenate([jnp.broadcast_to(c, (SP, SN)) for c in scalars], axis=0)


def head_sums(v):
    return [jnp.sum(v[:, h * SP : (h + 1) * SP], axis=1, keepdims=True) for h in range(HPD)]


def iota(shape, dim):
    return lax.broadcasted_iota(jnp.int32, shape, dim)


def turn(v):
    first = (iota(v.shape, 1) // (HEAD_SIZE // 2)) % 2 == 0
    return jnp.where(
        first, pltpu.roll(v, 2 * HEAD_SIZE - HEAD_SIZE // 2, 1), pltpu.roll(v, HEAD_SIZE // 2, 1)
    )


def rotated(block, cosine, sine):
    both = block[:, Q0:V0]
    return both * cosine + turn(both) * sine


def block_rows(a):
    return pl.ds(a * BLK, BLK)


def held_rows(places, a):
    return pl.ds(pl.multiple_of(places[a] * BLK, BLK), BLK)


def probabilities(query, keys, a):
    scores = mm_nt(query, keys) * (1.0 / math.sqrt(HEAD_SIZE))
    seen = iota(scores.shape, 0) + a * BLK >= iota(scores.shape, 1)
    scores = jnp.where(seen, scores, -jnp.inf)
    weights = jnp.exp(scores - jnp.max(scores, axis=1, keepdims=True))
    return weights / jnp.sum(weights, axis=1, keepdims=True)


class Block:
    def __init__(self, block, tail, taps, conv_b, heads):
        conv_in = block[:, :CV].astype(BF16).astype(F32)
        self.next_tail = conv_in[BLK - 8 :]
        extended = jnp.concatenate([tail, conv_in], axis=0)
        self.shifted = [extended[8 - d : 8 - d + BLK] for d in range(KW)]
        total = conv_b
        for d in range(KW):
            total = total + taps[KW - 1 - d : KW - d] * self.shifted[d]
        self.total = total
        self.sig = sigmoid(total)
        low = (total * self.sig).astype(BF16)
        self.b, self.c, self.x = low[:, :SN], low[:, SN : 2 * SN], low[:, 2 * SN :]
        raw = block[:, V0:] + heads[1:2]
        self.step = softplus(raw)
        self.step_slope = sigmoid(raw)
        self.rate = -jnp.exp(heads[0:1]) * heads[3:4]
        self.decay = self.rate * self.step
        self.tri = (iota((BLK, BLK), 0) >= iota((BLK, BLK), 1)).astype(F32)
        self.cum = exact(self.tri, self.decay, ((1,), (0,)))
        cum_t, step_t = self.cum.T, self.step.T
        lanes = [HEAD_SIZE + h for h in range(HPD)]
        self.cum_cols = [self.cum[:, l : l + 1] for l in lanes]
        self.last = [self.cum[BLK - 1 :, l : l + 1] for l in lanes]
        self.step_cols = [self.step[:, l : l + 1] for l in lanes]
        self.step_rows = [step_t[l : l + 1] for l in lanes]
        causal = iota((BLK, BLK), 0) >= iota((BLK, BLK), 1)
        self.fade = [
            jnp.exp(jnp.where(causal, self.cum_cols[h] - cum_t[l : l + 1], -jnp.inf))
            for h, l in enumerate(lanes)
        ]
        self.inter = mm_nt(self.c, self.b)
        self.to_end = [jnp.exp(self.last[h] - self.cum_cols[h]) for h in range(HPD)]
        self.grown = wide([jnp.exp(v) for v in self.cum_cols])
        self.weight = wide([self.to_end[h] * self.step_cols[h] for h in range(HPD)])
        self.carry = tall([jnp.exp(v) for v in self.last])
        self.skip = wide([heads[2:3, l : l + 1] for l in lanes])
        self.x32 = self.x.astype(F32)

    def head(self, v, h):
        return v[:, h * SP : (h + 1) * SP]


def forward_kernel(
    places, proj, cosine, sine, taps, conv_b, heads, mixed, y_out, states, keys, values
):
    taps, conv_b, heads = taps[...], conv_b[...], heads[...]
    tail = jnp.zeros((8, CV), F32)
    state = jnp.zeros((XC, SN), F32)
    for a in range(NCTX):
        at = held_rows(places, a)
        block = proj[at, :]
        both = rotated(block, cosine[block_rows(a), :], sine[block_rows(a), :]).astype(BF16)
        keys[block_rows(a), :] = both[:, HEAD_SIZE:]
        values[block_rows(a), :] = block[:, V0:T0].astype(BF16)
        seen = pl.ds(0, (a + 1) * BLK)
        probs = probabilities(both[:, :HEAD_SIZE], keys[seen, :], a)
        attended = mm(probs.astype(BF16), values[seen, :])
        now = Block(block, tail, taps, conv_b, heads)
        tail = now.next_tail
        states[a] = state
        y = now.grown * mm_nt(now.c, state.astype(BF16)) + now.skip * now.x32
        inner = [
            mm((now.inter * now.fade[h] * now.step_rows[h]).astype(BF16), now.head(now.x, h))
            for h in range(HPD)
        ]
        y = y + jnp.concatenate(inner, axis=1)
        y_out[block_rows(a), :] = y
        state = now.carry * state + mm_tn((now.x32 * now.weight).astype(BF16), now.b)
        gate = block[:, Z0:Q0]
        gated = y * gate * sigmoid(gate)
        mixed[at, :] = jnp.concatenate([attended, gated], axis=1).astype(BF16)


def backward_kernel(*refs):
    (places, proj, cosine, sine, taps, conv_b, heads, y_in, states, w_mix) = refs[:10]
    middle_low = refs[10 : 10 + NCTX]
    (grad_proj, conv_out, head_out, skip_out) = refs[10 + NCTX : 14 + NCTX]
    (keys, values, grad_mixed, grad_q, grad_k, grad_v) = refs[14 + NCTX :]
    taps, conv_b, heads = taps[...], conv_b[...], heads[...]
    for r in range(NCTX):
        grad_mixed[block_rows(r), :] = mm_nt(middle_low[r][...], w_mix[...])
    queries = []
    for a in range(NCTX):
        block = proj[held_rows(places, a), :]
        both = rotated(block, cosine[block_rows(a), :], sine[block_rows(a), :]).astype(BF16)
        queries.append(both[:, :HEAD_SIZE])
        keys[block_rows(a), :] = both[:, HEAD_SIZE:]
        values[block_rows(a), :] = block[:, V0:T0].astype(BF16)
    for a in reversed(range(NCTX)):
        seen = pl.ds(0, (a + 1) * BLK)
        grad_attended = grad_mixed[held_rows(places, a), :][:, :HEAD_SIZE].astype(BF16)
        probs = probabilities(queries[a], keys[seen, :], a)
        grad_probs = mm_nt(grad_attended, values[seen, :])
        delta = jnp.sum(probs * grad_probs, axis=1, keepdims=True)
        grad_scores = (probs * (grad_probs - delta) * (1.0 / math.sqrt(HEAD_SIZE))).astype(BF16)
        grad_q[block_rows(a), :] = mm(grad_scores, keys[seen, :])
        more_k = mm_tn(grad_scores, queries[a])
        more_v = mm_tn(probs.astype(BF16), grad_attended)
        if a < NCTX - 1:
            more_k = more_k + grad_k[seen, :]
            more_v = more_v + grad_v[seen, :]
        grad_k[seen, :] = more_k
        grad_v[seen, :] = more_v
    adjoint = jnp.zeros((XC, SN), F32)
    later = jnp.zeros((8, CV), F32)
    conv_rows = [jnp.zeros((1, CV), F32) for _ in range(KW + 1)]
    grad_alog = jnp.zeros((1, SN), F32)
    grad_bias = jnp.zeros((1, SN), F32)
    grad_skip = jnp.zeros((1, XC), F32)
    lane = iota((BLK, SN), 1)
    for a in reversed(range(NCTX)):
        at = held_rows(places, a)
        block = proj[at, :]
        if a:
            tail = proj[held_rows(places, a - 1), :][BLK - 8 :, :CV].astype(BF16).astype(F32)
        else:
            tail = jnp.zeros((8, CV), F32)
        now = Block(block, tail, taps, conv_b, heads)
        gate = block[:, Z0:Q0]
        sig = sigmoid(gate)
        grad_gated = grad_mixed[at, :][:, HEAD_SIZE:]
        y = y_in[block_rows(a), :]
        grad_gate = grad_gated * y * (sig + gate * sig * (1.0 - sig))
        grad_y = grad_gated * gate * sig
        grad_skip = grad_skip + jnp.sum(grad_y * now.x32, axis=0, keepdims=True)
        grad_y_low = grad_y.astype(BF16)
        grad_x = now.skip * grad_y
        state = states[a]
        state_low = state.astype(BF16)
        grad_inter = jnp.zeros((BLK, BLK), F32)
        cum_cols, step_cols, inner = [], [], []
        for h in range(HPD):
            gy, x = now.head(grad_y_low, h), now.head(now.x, h)
            grad_mixing = mm_nt(gy, x)
            faded = now.fade[h] * now.step_rows[h]
            grad_inter = grad_inter + grad_mixing * faded
            inner.append(mm_tn((now.inter * faded).astype(BF16), gy))
            product = grad_mixing * now.inter * now.fade[h]
            column = jnp.sum(product.T, axis=1, keepdims=True)
            row = jnp.sum(product * now.step_rows[h], axis=1, keepdims=True)
            step_cols.append(column)
            cum_cols.append(row - column * now.step_cols[h])
        grad_x = grad_x + jnp.concatenate(inner, axis=1)
        grad_inter = grad_inter.astype(BF16)
        grown_y = grad_y * now.grown
        grown_low = grown_y.astype(BF16)
        grad_c = mm(grad_inter, now.b) + mm(grown_low, state_low)
        from_state = head_sums(grown_y * mm_nt(now.c, state_low))
        adjoint_low = adjoint.astype(BF16)
        weighted = (now.x32 * now.weight).astype(BF16)
        grad_b = mm_tn(grad_inter, now.c) + mm(weighted, adjoint_low)
        grad_weighted = mm_nt(now.b, adjoint_low)
        grad_x = grad_x + grad_weighted * now.weight
        grad_weight = head_sums(grad_weighted * now.x32)
        carried = now.carry * adjoint * state
        grad_cum = jnp.zeros((BLK, SN), F32)
        grad_step = jnp.zeros((BLK, SN), F32)
        for h in range(HPD):
            step_col = step_cols[h] + grad_weight[h] * now.to_end[h]
            pulled = grad_weight[h] * now.to_end[h] * now.step_cols[h]
            last = jnp.sum(pulled, axis=0, keepdims=True) + jnp.sum(
                jnp.sum(carried[h * SP : (h + 1) * SP], axis=1, keepdims=True), axis=0, keepdims=True
            )
            cum_col = cum_cols[h] + from_state[h] - pulled
            cum_col = jnp.where(iota((BLK, 1), 0) == BLK - 1, cum_col + last, cum_col)
            here = lane == HEAD_SIZE + h
            grad_cum = jnp.where(here, cum_col, grad_cum)
            grad_step = jnp.where(here, step_col, grad_step)
        adjoint = now.carry * adjoint + mm_tn(grown_low, now.c)
        grad_decay = exact(now.tri, grad_cum, ((0,), (0,)))
        grad_alog = grad_alog + jnp.sum(grad_decay * now.decay, axis=0, keepdims=True)
        grad_dt = (grad_step + grad_decay * now.rate) * now.step_slope
        grad_bias = grad_bias + jnp.sum(grad_dt, axis=0, keepdims=True)
        grad_total = jnp.concatenate([grad_b, grad_c, grad_x], axis=1) * (
            now.sig + now.total * now.sig * (1.0 - now.sig)
        )
        conv_rows[0] = conv_rows[0] + jnp.sum(grad_total, axis=0, keepdims=True)
        extended = jnp.concatenate([grad_total, later], axis=0)
        later = grad_total[:8]
        grad_conv_in = jnp.zeros((BLK, CV), F32)
        for d in range(KW):
            k = KW - 1 - d
            conv_rows[1 + k] = conv_rows[1 + k] + jnp.sum(
                grad_total * now.shifted[d], axis=0, keepdims=True
            )
            grad_conv_in = grad_conv_in + taps[k : k + 1] * extended[d : d + BLK]
        both = jnp.concatenate([grad_q[block_rows(a), :], grad_k[block_rows(a), :]], axis=1)
        both = both * cosine[block_rows(a), :] + turn(both * sine[block_rows(a), :])
        grad_dt = pltpu.roll(grad_dt, HEAD_SIZE, 1)[:, :HEAD_SIZE]
        grad_proj[at, :] = jnp.concatenate(
            [grad_conv_in, grad_gate, both, grad_v[block_rows(a), :], grad_dt], axis=1
        ).astype(BF16)
    conv_out[...] = jnp.concatenate(conv_rows + [jnp.zeros((3, CV), F32)], axis=0)
    head_out[...] = jnp.concatenate([grad_alog, grad_bias, jnp.zeros((6, SN), F32)], axis=0)
    skip_out[...] = jnp.concatenate([grad_skip, jnp.zeros((7, XC), F32)], axis=0)


SMEM = pl.BlockSpec(memory_space=pltpu.SMEM)
VMEM = pl.BlockSpec(memory_space=pltpu.VMEM)
LIMIT = 48 * 1024 * 1024


def mixers_forward(places, proj, cosine, sine, taps, conv_b, heads):
    shape = jax.ShapeDtypeStruct
    rows = NCTX * BLK
    return pl.pallas_call(
        forward_kernel,
        in_specs=[SMEM] + [VMEM] * 6,
        out_specs=[VMEM] * 3,
        out_shape=(
            shape((rows, HEAD_SIZE + XC), BF16),
            shape((rows, XC), F32),
            shape((NCTX, XC, SN), F32),
        ),
        scratch_shapes=[pltpu.VMEM((rows, HEAD_SIZE), BF16)] * 2,
        cost_estimate=pl.CostEstimate(
            flops=2_000_000_000, bytes_accessed=8_000_000, transcendentals=4_000_000
        ),
        compiler_params=pltpu.CompilerParams(vmem_limit_bytes=LIMIT),
        name="mixers_forward",
    )(places, proj, cosine, sine, taps, conv_b, heads)


def mixers_backward(places, proj, cosine, sine, taps, conv_b, heads, y, states, w_mix, middle_low):
    shape = jax.ShapeDtypeStruct
    rows = NCTX * BLK
    return pl.pallas_call(
        backward_kernel,
        in_specs=[SMEM] + [VMEM] * (9 + NCTX),
        out_specs=[VMEM] * 4,
        out_shape=(
            shape((rows, GA), BF16),
            shape((8, CV), F32),
            shape((8, SN), F32),
            shape((8, XC), F32),
        ),
        scratch_shapes=[pltpu.VMEM((rows, HEAD_SIZE), BF16)] * 2
        + [pltpu.VMEM((rows, HEAD_SIZE + XC), F32)]
        + [pltpu.VMEM((rows, HEAD_SIZE), F32)] * 3,
        cost_estimate=pl.CostEstimate(
            flops=8_000_000_000, bytes_accessed=12_000_000, transcendentals=8_000_000
        ),
        compiler_params=pltpu.CompilerParams(vmem_limit_bytes=LIMIT),
        name="mixers_backward",
    )(places, proj, cosine, sine, taps, conv_b, heads, y, states, w_mix, *middle_low)


def per_device(
    tokens,
    cotangent,
    gain_attn,
    gain_mlp,
    w_qkv,
    w_o,
    w_zx,
    w_side,
    w_out,
    w_gu,
    w_down,
    conv_w,
    conv_bias,
    a_log,
    dt_bias,
    d_skip,
):
    ctx = lax.axis_index("ctx")
    chip, core = ctx // 2, ctx % 2
    blocks = jnp.arange(NCTX, dtype=jnp.int32)
    places = 2 * ((blocks // 2 - chip + CHIPS) % CHIPS) + (core ^ (blocks % 2))
    own_tokens, own_cot = tokens[0], cotangent[0]
    gain_attn, gain_mlp, conv_w, conv_bias = gain_attn[0], gain_mlp[0], conv_w[0], conv_bias[0]
    w_qkv, w_o, w_zx, w_side, w_out, w_gu, w_down = (
        w[0] for w in (w_qkv, w_o, w_zx, w_side, w_out, w_gu, w_down)
    )
    rows = w_qkv.shape[0]

    cut = lambda v: v.reshape(rows, NCTX, -1).transpose(1, 0, 2)
    group = NCTX // 2
    to_all = lambda v: jnp.broadcast_to(v[None], (NCTX,) + v.shape)
    keys = lambda v: jnp.repeat(v.reshape(rows, 2, HEAD_SIZE).transpose(1, 0, 2), group, axis=0)
    hidden_cols = lambda v: (
        v.reshape(rows, NDP, NCTX, HID // NDP).transpose(2, 0, 1, 3).reshape(NCTX, rows, HID)
    )
    columns = jnp.concatenate(
        [
            to_all(w_side[:, : 2 * SN]),
            cut(w_zx[:, INNER:]),
            cut(w_zx[:, :INNER]),
            cut(w_qkv[:, :QUERY_FEATURES]),
            keys(w_qkv[:, QUERY_FEATURES : QUERY_FEATURES + KEY_FEATURES]),
            keys(w_qkv[:, QUERY_FEATURES + KEY_FEATURES :]),
            cut(w_side[:, 2 * SN :]),
            jnp.zeros((NCTX, rows, 64 - HPD), BF16),
            hidden_cols(w_gu[:, :FF]),
            hidden_cols(w_gu[:, FF:]),
        ],
        axis=2,
    )
    small = jnp.concatenate([gain_attn, gain_mlp, conv_bias, conv_w.reshape(-1)])
    small = jnp.pad(small, (0, columns.shape[2] - small.shape[0]))
    columns = jnp.concatenate([columns, jnp.broadcast_to(small, (NCTX, 1, small.shape[0]))], axis=1)
    columns = lax.all_to_all(columns, "ctx", 0, 0)
    weight_part = columns[:, :rows].reshape(NCTX * rows, -1)
    mixers_part = jnp.concatenate([weight_part[:, :GA], columns[:, rows, :GA]], axis=0)
    mixers_all = dp_gather(mixers_part)
    wa = mixers_all[:, : NCTX * rows].reshape(D, GA)
    small = mixers_all[:, NCTX * rows :].reshape(NDP * NCTX, GA).astype(F32)
    per = D // (NDP * NCTX)
    cper = CONV // (NDP * NCTX)
    gain_a = small[:, :per].reshape(D)
    gain_m = small[:, per : 2 * per].reshape(D)
    bias_all = small[:, 2 * per : 2 * per + cper].reshape(CONV)
    taps_all = small[:, 2 * per + cper : 2 * per + 5 * cper].reshape(-1, KW, cper)
    taps_all = taps_all.transpose(1, 0, 2).reshape(KW, CONV)
    mine = lambda v: jnp.concatenate(
        [v[..., INNER:], lax.dynamic_slice_in_dim(v, ctx * XC, XC, v.ndim - 1)], axis=-1
    )
    taps, conv_b = mine(taps_all), mine(bias_all)

    tok_low = jnp.concatenate(gather_rows(own_tokens), axis=0)
    tok = tok_low.astype(F32)

    swap_pairs = [
        (c, NCTX * (c % NDP) + c // NDP) for c in range(NDP * NCTX)
    ]
    back_pairs = [(t, s) for s, t in swap_pairs]
    mix_rows = lax.ppermute(jnp.concatenate([w_o, w_out], axis=0), ("dp", "ctx"), swap_pairs)
    n_o, n_out, n_down = w_o.shape[0], w_out.shape[0], w_down.shape[0]
    late = jnp.concatenate(
        [weight_part[:, GA:], stacked_halves(w_down), stacked_halves(mix_rows)], axis=0
    )
    late = dp_gather(after(late, mixers_all))
    n_gu, n_half = NCTX * rows, 2 * n_down
    gu = late[:, :n_gu].reshape(D, 2 * HID)
    down = side_halves(late[:, n_gu : n_gu + n_half]).reshape(HID, D)
    mix_rows = side_halves(late[:, n_gu + n_half :])
    w_mix = jnp.concatenate(
        [mix_rows[:, :n_o].reshape(HEAD_SIZE, D), mix_rows[:, n_o:].reshape(XC, D)], axis=0
    )
    cot = gather_rows(after(own_cot, tok_low))

    normed = (tok * rms_factor(tok) * gain_a[None, :]).astype(BF16)
    proj = mm(normed, wa)
    cosine, sine = rope_tables()
    heads = lambda v: jnp.pad(
        lax.dynamic_slice_in_dim(v[0], ctx * HPD, HPD, 0), (HEAD_SIZE, HEAD_SIZE - HPD)
    )
    head_rows = jnp.stack([heads(a_log), heads(dt_bias), heads(d_skip), heads(jnp.ones_like(a_log))])
    head_rows = jnp.pad(head_rows, ((0, 4), (0, 0)))
    shared = (places, proj, cosine, sine, taps, conv_b[None], head_rows)
    mixed, y, states = mixers_forward(*shared)
    own_residual = own_tokens.astype(F32)
    part = lambda r: mm(mixed[r * BLK : (r + 1) * BLK], w_mix)
    middle = own_residual + scatter_rows(
        [part(2 * k) for k in range(CHIPS)], [part(2 * k + 1).astype(BF16) for k in range(CHIPS)]
    )

    factor_m = rms_factor(middle)
    normed2 = gather_rows((middle * factor_m * gain_m[None, :]).astype(BF16))
    keep_n, pass_n, keep_d, pass_d, hidden, grad_gate_up = zip(
        *[
            mlp(normed2[r], normed2[r + 1], cot[r], cot[r + 1], gu, down)
            for r in range(0, NCTX, 2)
        ]
    )
    grad_normed2 = scatter_rows(keep_n, pass_n)
    grad_middle = own_cot.astype(F32) + norm_back(middle, factor_m, gain_m[None, :], grad_normed2)
    middle_low = gather_rows(grad_middle.astype(BF16))
    grad_gu = tn_sum(normed2, grad_gate_up)
    grad_down = tn_sum(hidden, cot)
    pass_d = [after(v, middle_low[5]) for v in pass_d]
    block_out = middle + scatter_rows(keep_d, pass_d)

    grad_mix = tn_sum([mixed], middle_low)
    grad_proj, conv_terms, head_sum, skip_sum = mixers_backward(
        *shared, y, states, w_mix, middle_low
    )
    back = lambda r: mm_nt(grad_proj[r * BLK : (r + 1) * BLK], wa)
    grad_normed = scatter_rows(
        [back(2 * k) for k in range(CHIPS)], [back(2 * k + 1).astype(BF16) for k in range(CHIPS)]
    )
    grad_tokens = grad_middle + norm_back(
        own_residual, rms_factor(own_residual), gain_a[None, :], grad_normed
    )
    grad_wa = mm_tn(normed, grad_proj)

    place = lambda v, at, size: lax.dynamic_update_slice_in_dim(
        jnp.zeros(v.shape[:-1] + (size,), F32), v, at, v.ndim - 1
    )
    conv_terms = conv_terms[: KW + 1]
    conv_terms = jnp.concatenate(
        [place(conv_terms[:, X0:], ctx * XC, INNER), conv_terms[:, :X0]], axis=1
    )
    conv_terms = conv_terms.reshape(KW + 1, NDP * NCTX, cper).transpose(1, 0, 2)
    skip_terms = jnp.sum(skip_sum[0].reshape(HPD, SP), axis=1)
    head_terms = jnp.stack([*head_sum[:2, HEAD_SIZE : HEAD_SIZE + HPD], skip_terms])
    head_terms = place(head_terms, ctx * HPD, SH)
    n_conv, n_head = (KW + 1) * cper, 3 * SH
    small_terms = jnp.concatenate(
        [
            conv_terms.reshape(NDP * NCTX, n_conv),
            jnp.broadcast_to(head_terms.reshape(1, n_head), (NDP * NCTX, n_head)),
        ],
        axis=1,
    )
    coarse = small_terms.astype(BF16).astype(F32)
    n_small = n_conv + n_head
    small_terms = jnp.concatenate([coarse, small_terms - coarse], axis=1)
    small_terms = jnp.pad(small_terms, ((0, 0), (0, GA - 2 * n_small)))
    sent = jnp.concatenate(
        [
            grad_wa.reshape(NDP, NCTX * rows, GA),
            small_terms.reshape(NDP, NCTX, GA),
        ],
        axis=1,
    )
    mix_terms = jnp.concatenate(
        [
            grad_mix[:HEAD_SIZE].reshape(NDP, n_o, D),
            grad_mix[HEAD_SIZE:].reshape(NDP, n_out, D),
        ],
        axis=1,
    )
    sum_late = dp_sum(
        jnp.concatenate(
            [
                grad_gu.reshape(NDP, n_gu, 2 * HID),
                stacked_halves(grad_down.reshape(NDP, n_down, D)),
                stacked_halves(mix_terms),
            ],
            axis=1,
        )
    )
    sum_gu = sum_late[:n_gu]
    sum_down = side_halves(sum_late[n_gu : n_gu + n_half])
    sum_mix = side_halves(sum_late[n_gu + n_half :])
    sum_mix = lax.ppermute(sum_mix, ("dp", "ctx"), back_pairs)
    got_gu = lax.all_to_all(sum_gu.reshape(NCTX, rows, 2 * HID), "ctx", 0, 0)
    hidden_back = lambda v: (
        v.reshape(NCTX, rows, NDP, HID // NDP).transpose(1, 2, 0, 3).reshape(rows, FF)
    )
    out_gu = jnp.concatenate(
        [hidden_back(got_gu[:, :, :HID]), hidden_back(got_gu[:, :, HID:])], axis=1
    )
    sum_a = dp_sum(sent)
    sum_a = jnp.concatenate(
        [
            sum_a[: NCTX * rows].reshape(NCTX, rows, GA),
            sum_a[NCTX * rows :].reshape(NCTX, 1, GA),
        ],
        axis=1,
    )
    got = lax.all_to_all(sum_a, "ctx", 0, 0)
    small_got = jnp.sum(got[:, rows], axis=0)
    small_got = small_got[:n_small] + small_got[n_small : 2 * n_small]
    got = got[:, :rows]
    uncut = lambda v: v.transpose(1, 0, 2).reshape(rows, -1)
    keys_back = lambda v: uncut(jnp.sum(v.reshape(2, group, rows, HEAD_SIZE), axis=1))
    out_zx = jnp.concatenate([uncut(got[:, :, Z0:Q0]), uncut(got[:, :, X0:Z0])], axis=1)
    out_side = jnp.concatenate(
        [jnp.sum(got[:, :, :X0], axis=0), uncut(got[:, :, T0 : T0 + HPD])], axis=1
    )
    out_qkv = jnp.concatenate(
        [uncut(got[:, :, Q0:K0]), keys_back(got[:, :, K0:V0]), keys_back(got[:, :, V0:T0])], axis=1
    )
    row_sum = lambda w, g: jnp.sum(w.astype(F32) * g, axis=1)
    out_gain_a = (row_sum(w_qkv, out_qkv) + row_sum(w_zx, out_zx) + row_sum(w_side, out_side)) / (
        gain_attn.astype(F32)
    )
    out_gain_m = row_sum(w_gu, out_gu) / gain_mlp.astype(F32)
    out_conv = small_got[:n_conv].reshape(KW + 1, cper)
    out_heads = small_got[n_conv:].reshape(3, 1, SH)
    return (
        block_out[None],
        grad_tokens[None],
        out_gain_a[None],
        out_gain_m[None],
        out_qkv[None],
        sum_mix[:n_o][None],
        out_zx[None],
        out_side[None],
        sum_mix[n_o:][None],
        out_gu[None],
        sum_down[None],
        out_conv[1:][None],
        out_conv[0][None],
        out_heads[0],
        out_heads[1],
        out_heads[2],
    )


def solution(mesh):
    rows = P("dp", "ctx", None)
    vector = P(None, ("dp", "ctx"))
    matrix = P(None, ("dp", "ctx"), None)
    taps = P(None, None, ("dp", "ctx"))
    weights = (vector, vector) + (matrix,) * 7 + (taps, vector, P(), P(), P())
    return jax.shard_map(
        per_device,
        mesh=mesh,
        in_specs=(rows, rows) + weights,
        out_specs=(rows, rows) + weights,
        check_vma=False,
    )
```

```python
import functools
import math

import jax
import jax.numpy as jnp
from jax import lax
from jax.experimental import pallas as pl
from jax.experimental.pallas import tpu as pltpu
from jax.sharding import PartitionSpec as P

D = 1024
HEAD_SIZE = 64
SH = 24
SP = 64
SN = 128
FF = 2048
KW = 4
BLK = 128
INNER = 1536
CONV = 1792
QUERY_FEATURES = 512
KEY_FEATURES = 128
NDP = 16
NCTX = 8
CHIPS = 4
HPD = SH // NCTX
XC = INNER // NCTX
HID = FF // NCTX
CV = 2 * SN + XC
X0, Z0, Q0 = 2 * SN, CV, CV + XC
K0, V0, T0 = Q0 + HEAD_SIZE, Q0 + 2 * HEAD_SIZE, Q0 + 3 * HEAD_SIZE
GA = Q0 + 4 * HEAD_SIZE
SPARE = T0 + HPD
NDEV = NDP * NCTX
CPER = CONV // NDEV
N_SMALL = (KW + 1) * CPER + 3 * SH

EPSILON = 1e-05
ROPE_BASE = 100000000000.0
F32 = jnp.float32
BF16 = jnp.bfloat16
HIGHEST = lax.Precision.HIGHEST


def dot(a, b, dims):
    return lax.dot_general(a, b, (dims, ((), ())), preferred_element_type=F32)


def mm(a, b):
    return dot(a, b, ((1,), (0,)))


def mm_nt(a, b):
    return dot(a, b, ((1,), (1,)))


def mm_tn(a, b):
    return dot(a, b, ((0,), (0,)))


def chip_shift(array, by):
    return lax.ppermute(array, "ctx", [(i, (i + 2 * by) % NCTX) for i in range(NCTX)])


def core_swap(array):
    return lax.ppermute(array, "ctx", [(i, i ^ 1) for i in range(NCTX)])


def gather_rows(own):
    same = [own, chip_shift(own, -1), None, chip_shift(own, 1)]
    same[2] = chip_shift(own, 2)
    other = [None] * CHIPS
    for k in (0, 1, 3, 2):
        other[k] = core_swap(same[k])
    return [block for pair in zip(same, other) for block in pair]


def scatter_rows(keep, pass_on):
    total = None
    for k in (2, 1, 3, 0):
        both = keep[k] + core_swap(pass_on[k]).astype(F32)
        if k:
            both = chip_shift(both.astype(BF16), k).astype(F32)
        total = both if total is None else total + both
    return total


def dp_gather(own):
    return lax.all_to_all(jnp.broadcast_to(own[None], (NDP,) + own.shape), "dp", 0, 0)


def to_owners(parts):
    return lax.all_to_all(parts, ("dp", "ctx"), 0, 0)


def dp_sum(parts):
    return jnp.sum(lax.all_to_all(parts, "dp", 0, 0).astype(F32), axis=0)


SMEM = pl.BlockSpec(memory_space=pltpu.SMEM)
VMEM = pl.BlockSpec(memory_space=pltpu.VMEM)
LIMIT = 48 * 1024 * 1024


def after(value, *others):
    return lax.optimization_barrier((value,) + others)[0]


def mlp_kernel(*refs):
    normed, cot, (gu, down) = refs[:NCTX], refs[NCTX : 2 * NCTX], refs[2 * NCTX : 2 * NCTX + 2]
    outs = refs[2 * NCTX + 2 :]
    keep_n, pass_n, keep_d, pass_d = (outs[CHIPS * m : CHIPS * (m + 1)] for m in range(4))
    hid, dgu = outs[4 * CHIPS :]
    for k in (2, 1, 3, 0):
        normed2 = jnp.concatenate([normed[2 * k][...], normed[2 * k + 1][...]], axis=0)
        upstream = jnp.concatenate([cot[2 * k][...], cot[2 * k + 1][...]], axis=0)
        gate_up = mm(normed2, gu[...])
        gate_half, up_half = gate_up[:, :HID], gate_up[:, HID:]
        sigmoid_gate = sigmoid(gate_half)
        silu_gate = gate_half * sigmoid_gate
        hidden = (silu_gate * up_half).astype(BF16)
        grad_hidden = mm_nt(upstream, down[...])
        grad_gate = grad_hidden * up_half * (sigmoid_gate + silu_gate * (1.0 - sigmoid_gate))
        grad_gate_up = jnp.concatenate([grad_gate, grad_hidden * silu_gate], axis=1).astype(BF16)
        at = pl.ds(2 * k * BLK, 2 * BLK)
        hid[at, :] = hidden
        dgu[at, :] = grad_gate_up
        grad_normed2 = mm_nt(grad_gate_up, gu[...])
        keep_n[k][...] = grad_normed2[:BLK]
        pass_n[k][...] = grad_normed2[BLK:].astype(BF16)
        out = mm(hidden, down[...])
        keep_d[k][...] = out[:BLK]
        pass_d[k][...] = out[BLK:].astype(BF16)


def mlp(normed2, cot, gu, down):
    shape = jax.ShapeDtypeStruct
    keep, passed = [shape((BLK, D), F32)] * CHIPS, [shape((BLK, D), BF16)] * CHIPS
    rows = NCTX * BLK
    outs = pl.pallas_call(
        mlp_kernel,
        out_shape=keep + passed + keep + passed
        + [shape((rows, HID), BF16), shape((rows, 2 * HID), BF16)],
        cost_estimate=pl.CostEstimate(
            flops=2 * rows * D * HID * 6, bytes_accessed=12_000_000, transcendentals=0
        ),
        compiler_params=pltpu.CompilerParams(vmem_limit_bytes=LIMIT),
        name="feed_forward",
    )(*normed2, *cot, gu, down)
    parts = [outs[CHIPS * m : CHIPS * (m + 1)] for m in range(4)]
    return [*parts, *outs[4 * CHIPS :]]


def tn_kernel(n_left, *refs):
    left = jnp.concatenate([r[...] for r in refs[:n_left]], axis=0)
    right = jnp.concatenate([r[...] for r in refs[n_left:-1]], axis=0)
    refs[-1][...] = mm_tn(left, right).astype(BF16)


def mixer_grad_kernel(normed, grad_proj, small, out):
    total = mm_tn(normed[...], grad_proj[...])
    out[:, :V0] = total[:, :V0].astype(BF16)
    out[:, V0:] = (total[:, V0:] + small[...]).astype(BF16)


def mixer_grad(normed, grad_proj, small):
    return pl.pallas_call(
        mixer_grad_kernel,
        out_shape=jax.ShapeDtypeStruct((D, GA), BF16),
        cost_estimate=pl.CostEstimate(
            flops=2 * D * GA * NCTX * BLK, bytes_accessed=8_000_000, transcendentals=0
        ),
        compiler_params=pltpu.CompilerParams(vmem_limit_bytes=LIMIT),
        name="mixer_weight_grad",
    )(normed, grad_proj, small)


def columns_kernel(zx, side, qkv, gu, small, mixers, ff):
    zx, side, qkv, gu, small = (v[...].astype(F32) for v in (zx, side, qkv, gu, small))
    for j in range(NCTX):
        head = j // (NCTX // 2) * HEAD_SIZE
        key = QUERY_FEATURES + head
        value = QUERY_FEATURES + KEY_FEATURES + head
        own = [
            side[:, : 2 * SN],
            zx[:, INNER + j * XC : INNER + (j + 1) * XC],
            zx[:, j * XC : (j + 1) * XC],
            qkv[:, j * HEAD_SIZE : (j + 1) * HEAD_SIZE],
            qkv[:, key : key + HEAD_SIZE],
            qkv[:, value : value + HEAD_SIZE],
            side[:, 2 * SN + j * HPD : 2 * SN + (j + 1) * HPD],
            small,
        ]
        own = jnp.concatenate(own, axis=1).astype(BF16)
        units = [gu[:, j * HID : (j + 1) * HID], gu[:, FF + j * HID : FF + (j + 1) * HID]]
        units = jnp.concatenate(units, axis=1).astype(BF16)
        for i in range(NDP):
            mixers[i * NCTX + j] = own
            ff[i * NCTX + j] = units


def columns_for_all(zx, side, qkv, gu, small):
    rows = zx.shape[0]
    shape = jax.ShapeDtypeStruct
    return pl.pallas_call(
        columns_kernel,
        out_shape=(shape((NDEV, rows, GA), BF16), shape((NDEV, rows, 2 * HID), BF16)),
        cost_estimate=pl.CostEstimate(flops=0, bytes_accessed=3_000_000, transcendentals=0),
        compiler_params=pltpu.CompilerParams(vmem_limit_bytes=LIMIT),
        name="columns",
    )(zx, side, qkv, gu, small)


def source_sum(parts, j):
    total = parts[j].astype(F32)
    for i in range(1, NDP):
        total = total + parts[i * NCTX + j].astype(F32)
    return total


def row_dot(weight, grad):
    total = jnp.sum(weight[...].astype(F32) * grad, axis=1, keepdims=True)
    return jnp.broadcast_to(total, (total.shape[0], SN))


def mixers_owned_kernel(parts, zx, side, qkv, out_zx, out_side, out_qkv, out_gain, out_small):
    got = [source_sum(parts, j) for j in range(NCTX)]
    half = NCTX // 2
    grads = jnp.concatenate([g[:, Z0:Q0] for g in got] + [g[:, X0:Z0] for g in got], axis=1)
    out_zx[...] = grads
    gain = row_dot(zx, grads)
    both = sum(g[:, :X0] for g in got[1:]) + got[0][:, :X0]
    grads = jnp.concatenate([both] + [g[:, T0 : T0 + HPD] for g in got], axis=1)
    out_side[...] = grads
    gain = gain + row_dot(side, grads)
    pairs = [sum(g[:, K0:T0] for g in got[h + 1 : h + half]) + got[h][:, K0:T0] for h in (0, half)]
    grads = jnp.concatenate(
        [g[:, Q0:K0] for g in got]
        + [p[:, :HEAD_SIZE] for p in pairs]
        + [p[:, HEAD_SIZE:] for p in pairs],
        axis=1,
    )
    out_qkv[...] = grads
    out_gain[...] = gain + row_dot(qkv, grads)
    out_small[...] = sum(g[:, V0:] for g in got[1:]) + got[0][:, V0:]


def mixers_owned(parts, zx, side, qkv):
    shape = jax.ShapeDtypeStruct
    rows = zx.shape[0]
    return pl.pallas_call(
        mixers_owned_kernel,
        out_shape=(
            shape(zx.shape, F32),
            shape(side.shape, F32),
            shape(qkv.shape, F32),
            shape((rows, SN), F32),
            shape((rows, SN), F32),
        ),
        cost_estimate=pl.CostEstimate(flops=0, bytes_accessed=3_000_000, transcendentals=0),
        compiler_params=pltpu.CompilerParams(vmem_limit_bytes=LIMIT),
        name="mixers_owned",
    )(parts, zx, side, qkv)


def ff_owned_kernel(parts, gu, out_gu, out_gain):
    got = [source_sum(parts, j) for j in range(NCTX)]
    grads = jnp.concatenate([g[:, :HID] for g in got] + [g[:, HID:] for g in got], axis=1)
    out_gu[...] = grads
    out_gain[...] = row_dot(gu, grads)


def ff_owned(parts, gu):
    shape = jax.ShapeDtypeStruct
    return pl.pallas_call(
        ff_owned_kernel,
        out_shape=(shape(gu.shape, F32), shape((gu.shape[0], SN), F32)),
        cost_estimate=pl.CostEstimate(flops=0, bytes_accessed=2_000_000, transcendentals=0),
        compiler_params=pltpu.CompilerParams(vmem_limit_bytes=LIMIT),
        name="ff_owned",
    )(parts, gu)


def tn_sum(left, right):
    n, m = left[0].shape[1], right[0].shape[1]
    return pl.pallas_call(
        functools.partial(tn_kernel, len(left)),
        out_shape=jax.ShapeDtypeStruct((n, m), BF16),
        cost_estimate=pl.CostEstimate(
            flops=2 * n * m * NCTX * BLK, bytes_accessed=6 * n * m, transcendentals=0
        ),
        compiler_params=pltpu.CompilerParams(vmem_limit_bytes=LIMIT),
        name="weight_grad",
    )(*left, *right)


def rms_factor(hidden_in):
    return lax.rsqrt(jnp.mean(hidden_in * hidden_in, axis=-1, keepdims=True) + EPSILON)


def norm_back(hidden_in, factor, gain, upstream):
    scaled = upstream * gain
    inner = jnp.mean(scaled * hidden_in, axis=-1, keepdims=True)
    return factor * scaled - hidden_in * (factor * factor * factor) * inner


def rope_tables():
    exponent = -(2.0 * jnp.arange(HEAD_SIZE // 2, dtype=F32)) / HEAD_SIZE
    inverse = jnp.power(jnp.float32(ROPE_BASE), exponent)
    angles = jnp.arange(NCTX * BLK, dtype=F32)[:, None] * inverse[None, :]
    cosine, sine = jnp.cos(angles), jnp.sin(angles)
    return (
        jnp.concatenate([cosine] * 4, axis=1),
        jnp.concatenate([-sine, sine, -sine, sine], axis=1),
    )


def sigmoid(v):
    return 1.0 / (1.0 + jnp.exp(-v))


def softplus(v):
    return jnp.maximum(v, 0.0) + jnp.log1p(jnp.exp(-jnp.abs(v)))


def exact(a, b, dims):
    return lax.dot_general(a, b, (dims, ((), ())), precision=HIGHEST, preferred_element_type=F32)


def wide(columns):
    return jnp.concatenate([jnp.broadcast_to(c, (BLK, SP)) for c in columns], axis=1)


def tall(scalars):
    return jnp.concatenate([jnp.broadcast_to(c, (SP, SN)) for c in scalars], axis=0)


def head_sums(v):
    return [jnp.sum(v[:, h * SP : (h + 1) * SP], axis=1, keepdims=True) for h in range(HPD)]


def iota(shape, dim):
    return lax.broadcasted_iota(jnp.int32, shape, dim)


def turn(v):
    first = (iota(v.shape, 1) // (HEAD_SIZE // 2)) % 2 == 0
    return jnp.where(
        first, pltpu.roll(v, 2 * HEAD_SIZE - HEAD_SIZE // 2, 1), pltpu.roll(v, HEAD_SIZE // 2, 1)
    )


def rotated(block, cosine, sine):
    both = block[:, Q0:V0]
    return both * cosine + turn(both) * sine


def block_rows(a):
    return pl.ds(a * BLK, BLK)


def held_rows(places, a):
    return pl.ds(pl.multiple_of(places[a] * BLK, BLK), BLK)


def probabilities(query, keys, a):
    scores = mm_nt(query, keys) * (1.0 / math.sqrt(HEAD_SIZE))
    seen = iota(scores.shape, 0) + a * BLK >= iota(scores.shape, 1)
    scores = jnp.where(seen, scores, -jnp.inf)
    weights = jnp.exp(scores - jnp.max(scores, axis=1, keepdims=True))
    return weights / jnp.sum(weights, axis=1, keepdims=True)


class Block:
    def __init__(self, block, tail, taps, conv_b, heads):
        conv_in = block[:, :CV].astype(BF16).astype(F32)
        self.next_tail = conv_in[BLK - 8 :]
        extended = jnp.concatenate([tail, conv_in], axis=0)
        self.shifted = [extended[8 - d : 8 - d + BLK] for d in range(KW)]
        total = conv_b
        for d in range(KW):
            total = total + taps[KW - 1 - d : KW - d] * self.shifted[d]
        self.total = total
        self.sig = sigmoid(total)
        low = (total * self.sig).astype(BF16)
        self.b, self.c, self.x = low[:, :SN], low[:, SN : 2 * SN], low[:, 2 * SN :]
        raw = block[:, V0:] + heads[1:2]
        self.step = softplus(raw)
        self.step_slope = sigmoid(raw)
        self.rate = -jnp.exp(heads[0:1]) * heads[3:4]
        self.decay = self.rate * self.step
        self.tri = (iota((BLK, BLK), 0) >= iota((BLK, BLK), 1)).astype(F32)
        self.cum = exact(self.tri, self.decay, ((1,), (0,)))
        cum_t, step_t = self.cum.T, self.step.T
        lanes = [HEAD_SIZE + h for h in range(HPD)]
        self.cum_cols = [self.cum[:, l : l + 1] for l in lanes]
        self.last = [self.cum[BLK - 1 :, l : l + 1] for l in lanes]
        self.step_cols = [self.step[:, l : l + 1] for l in lanes]
        self.step_rows = [step_t[l : l + 1] for l in lanes]
        causal = iota((BLK, BLK), 0) >= iota((BLK, BLK), 1)
        self.fade = [
            jnp.exp(jnp.where(causal, self.cum_cols[h] - cum_t[l : l + 1], -jnp.inf))
            for h, l in enumerate(lanes)
        ]
        self.inter = mm_nt(self.c, self.b)
        self.to_end = [jnp.exp(self.last[h] - self.cum_cols[h]) for h in range(HPD)]
        self.grown = wide([jnp.exp(v) for v in self.cum_cols])
        self.weight = wide([self.to_end[h] * self.step_cols[h] for h in range(HPD)])
        self.carry = tall([jnp.exp(v) for v in self.last])
        self.skip = wide([heads[2:3, l : l + 1] for l in lanes])
        self.x32 = self.x.astype(F32)

    def head(self, v, h):
        return v[:, h * SP : (h + 1) * SP]


def forward_kernel(*refs):
    places, proj, cosine, sine, taps, conv_b, heads, w_mix = refs[:8]
    mixed, y_out, states = refs[8:11]
    keep, passed = refs[11 : 11 + CHIPS], refs[11 + CHIPS : 11 + 2 * CHIPS]
    keys, values = refs[11 + 2 * CHIPS :]
    taps, conv_b, heads = taps[...], conv_b[...], heads[...]
    tail = jnp.zeros((8, CV), F32)
    state = jnp.zeros((XC, SN), F32)
    for a in range(NCTX):
        at = held_rows(places, a)
        block = proj[at, :]
        both = rotated(block, cosine[block_rows(a), :], sine[block_rows(a), :]).astype(BF16)
        keys[block_rows(a), :] = both[:, HEAD_SIZE:]
        values[block_rows(a), :] = block[:, V0:T0].astype(BF16)
        seen = pl.ds(0, (a + 1) * BLK)
        probs = probabilities(both[:, :HEAD_SIZE], keys[seen, :], a)
        attended = mm(probs.astype(BF16), values[seen, :])
        now = Block(block, tail, taps, conv_b, heads)
        tail = now.next_tail
        states[a] = state
        y = now.grown * mm_nt(now.c, state.astype(BF16)) + now.skip * now.x32
        inner = [
            mm((now.inter * now.fade[h] * now.step_rows[h]).astype(BF16), now.head(now.x, h))
            for h in range(HPD)
        ]
        y = y + jnp.concatenate(inner, axis=1)
        y_out[block_rows(a), :] = y
        state = now.carry * state + mm_tn((now.x32 * now.weight).astype(BF16), now.b)
        gate = block[:, Z0:Q0]
        gated = y * gate * sigmoid(gate)
        mixed[at, :] = jnp.concatenate([attended, gated], axis=1).astype(BF16)
    for k in range(CHIPS):
        out = mm(mixed[pl.ds(2 * k * BLK, 2 * BLK), :], w_mix[...])
        keep[k][...] = out[:BLK]
        passed[k][...] = out[BLK:].astype(BF16)


def backward_kernel(*refs):
    places, proj, cosine, sine, taps, conv_b, heads, y_in, states, w_mix, wa = refs[:11]
    middle_low, refs = refs[11 : 11 + NCTX], refs[11 + NCTX :]
    grad_proj, conv_out, head_out, skip_out = refs[:4]
    keep, passed = refs[4 : 4 + CHIPS], refs[4 + CHIPS : 4 + 2 * CHIPS]
    keys, values, grad_mixed, grad_q, grad_k, grad_v = refs[4 + 2 * CHIPS :]
    taps, conv_b, heads = taps[...], conv_b[...], heads[...]
    for r in range(NCTX):
        grad_mixed[block_rows(r), :] = mm_nt(middle_low[r][...], w_mix[...])
    queries = []
    for a in range(NCTX):
        block = proj[held_rows(places, a), :]
        both = rotated(block, cosine[block_rows(a), :], sine[block_rows(a), :]).astype(BF16)
        queries.append(both[:, :HEAD_SIZE])
        keys[block_rows(a), :] = both[:, HEAD_SIZE:]
        values[block_rows(a), :] = block[:, V0:T0].astype(BF16)
    for a in reversed(range(NCTX)):
        seen = pl.ds(0, (a + 1) * BLK)
        grad_attended = grad_mixed[held_rows(places, a), :][:, :HEAD_SIZE].astype(BF16)
        probs = probabilities(queries[a], keys[seen, :], a)
        grad_probs = mm_nt(grad_attended, values[seen, :])
        delta = jnp.sum(probs * grad_probs, axis=1, keepdims=True)
        grad_scores = (probs * (grad_probs - delta) * (1.0 / math.sqrt(HEAD_SIZE))).astype(BF16)
        grad_q[block_rows(a), :] = mm(grad_scores, keys[seen, :])
        more_k = mm_tn(grad_scores, queries[a])
        more_v = mm_tn(probs.astype(BF16), grad_attended)
        if a < NCTX - 1:
            more_k = more_k + grad_k[seen, :]
            more_v = more_v + grad_v[seen, :]
        grad_k[seen, :] = more_k
        grad_v[seen, :] = more_v
    adjoint = jnp.zeros((XC, SN), F32)
    later = jnp.zeros((8, CV), F32)
    conv_rows = [jnp.zeros((1, CV), F32) for _ in range(KW + 1)]
    grad_alog = jnp.zeros((1, SN), F32)
    grad_bias = jnp.zeros((1, SN), F32)
    grad_skip = jnp.zeros((1, XC), F32)
    lane = iota((BLK, SN), 1)
    for a in reversed(range(NCTX)):
        at = held_rows(places, a)
        block = proj[at, :]
        if a:
            tail = proj[held_rows(places, a - 1), :][BLK - 8 :, :CV].astype(BF16).astype(F32)
        else:
            tail = jnp.zeros((8, CV), F32)
        now = Block(block, tail, taps, conv_b, heads)
        gate = block[:, Z0:Q0]
        sig = sigmoid(gate)
        grad_gated = grad_mixed[at, :][:, HEAD_SIZE:]
        y = y_in[block_rows(a), :]
        grad_gate = grad_gated * y * (sig + gate * sig * (1.0 - sig))
        grad_y = grad_gated * gate * sig
        grad_skip = grad_skip + jnp.sum(grad_y * now.x32, axis=0, keepdims=True)
        grad_y_low = grad_y.astype(BF16)
        grad_x = now.skip * grad_y
        state = states[a]
        state_low = state.astype(BF16)
        grad_inter = jnp.zeros((BLK, BLK), F32)
        cum_cols, step_cols, inner = [], [], []
        for h in range(HPD):
            gy, x = now.head(grad_y_low, h), now.head(now.x, h)
            grad_mixing = mm_nt(gy, x)
            faded = now.fade[h] * now.step_rows[h]
            grad_inter = grad_inter + grad_mixing * faded
            inner.append(mm_tn((now.inter * faded).astype(BF16), gy))
            product = grad_mixing * now.inter * now.fade[h]
            column = jnp.sum(product.T, axis=1, keepdims=True)
            row = jnp.sum(product * now.step_rows[h], axis=1, keepdims=True)
            step_cols.append(column)
            cum_cols.append(row - column * now.step_cols[h])
        grad_x = grad_x + jnp.concatenate(inner, axis=1)
        grad_inter = grad_inter.astype(BF16)
        grown_y = grad_y * now.grown
        grown_low = grown_y.astype(BF16)
        grad_c = mm(grad_inter, now.b) + mm(grown_low, state_low)
        from_state = head_sums(grown_y * mm_nt(now.c, state_low))
        adjoint_low = adjoint.astype(BF16)
        weighted = (now.x32 * now.weight).astype(BF16)
        grad_b = mm_tn(grad_inter, now.c) + mm(weighted, adjoint_low)
        grad_weighted = mm_nt(now.b, adjoint_low)
        grad_x = grad_x + grad_weighted * now.weight
        grad_weight = head_sums(grad_weighted * now.x32)
        carried = now.carry * adjoint * state
        grad_cum = jnp.zeros((BLK, SN), F32)
        grad_step = jnp.zeros((BLK, SN), F32)
        for h in range(HPD):
            step_col = step_cols[h] + grad_weight[h] * now.to_end[h]
            pulled = grad_weight[h] * now.to_end[h] * now.step_cols[h]
            last = jnp.sum(pulled, axis=0, keepdims=True) + jnp.sum(
                jnp.sum(carried[h * SP : (h + 1) * SP], axis=1, keepdims=True), axis=0, keepdims=True
            )
            cum_col = cum_cols[h] + from_state[h] - pulled
            cum_col = jnp.where(iota((BLK, 1), 0) == BLK - 1, cum_col + last, cum_col)
            here = lane == HEAD_SIZE + h
            grad_cum = jnp.where(here, cum_col, grad_cum)
            grad_step = jnp.where(here, step_col, grad_step)
        adjoint = now.carry * adjoint + mm_tn(grown_low, now.c)
        grad_decay = exact(now.tri, grad_cum, ((0,), (0,)))
        grad_alog = grad_alog + jnp.sum(grad_decay * now.decay, axis=0, keepdims=True)
        grad_dt = (grad_step + grad_decay * now.rate) * now.step_slope
        grad_bias = grad_bias + jnp.sum(grad_dt, axis=0, keepdims=True)
        grad_total = jnp.concatenate([grad_b, grad_c, grad_x], axis=1) * (
            now.sig + now.total * now.sig * (1.0 - now.sig)
        )
        conv_rows[0] = conv_rows[0] + jnp.sum(grad_total, axis=0, keepdims=True)
        extended = jnp.concatenate([grad_total, later], axis=0)
        later = grad_total[:8]
        grad_conv_in = jnp.zeros((BLK, CV), F32)
        for d in range(KW):
            k = KW - 1 - d
            conv_rows[1 + k] = conv_rows[1 + k] + jnp.sum(
                grad_total * now.shifted[d], axis=0, keepdims=True
            )
            grad_conv_in = grad_conv_in + taps[k : k + 1] * extended[d : d + BLK]
        both = jnp.concatenate([grad_q[block_rows(a), :], grad_k[block_rows(a), :]], axis=1)
        both = both * cosine[block_rows(a), :] + turn(both * sine[block_rows(a), :])
        grad_dt = pltpu.roll(grad_dt, HEAD_SIZE, 1)[:, :HEAD_SIZE]
        grad_proj[at, :] = jnp.concatenate(
            [grad_conv_in, grad_gate, both, grad_v[block_rows(a), :], grad_dt], axis=1
        ).astype(BF16)
    for k in (2, 1, 3, 0):
        out = mm_nt(grad_proj[pl.ds(2 * k * BLK, 2 * BLK), :], wa[...])
        keep[k][...] = out[:BLK]
        passed[k][...] = out[BLK:].astype(BF16)
    conv_out[...] = jnp.concatenate(conv_rows + [jnp.zeros((3, CV), F32)], axis=0)
    head_out[...] = jnp.concatenate([grad_alog, grad_bias, jnp.zeros((6, SN), F32)], axis=0)
    skip_out[...] = jnp.concatenate([grad_skip, jnp.zeros((7, XC), F32)], axis=0)


def mixers_forward(places, proj, cosine, sine, taps, conv_b, heads, w_mix):
    shape = jax.ShapeDtypeStruct
    rows = NCTX * BLK
    return pl.pallas_call(
        forward_kernel,
        in_specs=[SMEM] + [VMEM] * 7,
        out_specs=[VMEM] * (3 + 2 * CHIPS),
        out_shape=(
            shape((rows, HEAD_SIZE + XC), BF16),
            shape((rows, XC), F32),
            shape((NCTX, XC, SN), F32),
            *[shape((BLK, D), F32)] * CHIPS,
            *[shape((BLK, D), BF16)] * CHIPS,
        ),
        scratch_shapes=[pltpu.VMEM((rows, HEAD_SIZE), BF16)] * 2,
        cost_estimate=pl.CostEstimate(
            flops=2_000_000_000, bytes_accessed=8_000_000, transcendentals=4_000_000
        ),
        compiler_params=pltpu.CompilerParams(vmem_limit_bytes=LIMIT),
        name="mixers_forward",
    )(places, proj, cosine, sine, taps, conv_b, heads, w_mix)


def mixers_backward(
    places, proj, cosine, sine, taps, conv_b, heads, y, states, w_mix, wa, middle_low
):
    shape = jax.ShapeDtypeStruct
    rows = NCTX * BLK
    return pl.pallas_call(
        backward_kernel,
        in_specs=[SMEM] + [VMEM] * (10 + NCTX),
        out_specs=[VMEM] * (4 + 2 * CHIPS),
        out_shape=(
            shape((rows, GA), BF16),
            shape((8, CV), F32),
            shape((8, SN), F32),
            shape((8, XC), F32),
            *[shape((BLK, D), F32)] * CHIPS,
            *[shape((BLK, D), BF16)] * CHIPS,
        ),
        scratch_shapes=[pltpu.VMEM((rows, HEAD_SIZE), BF16)] * 2
        + [pltpu.VMEM((rows, HEAD_SIZE + XC), F32)]
        + [pltpu.VMEM((rows, HEAD_SIZE), F32)] * 3,
        cost_estimate=pl.CostEstimate(
            flops=8_000_000_000, bytes_accessed=12_000_000, transcendentals=8_000_000
        ),
        compiler_params=pltpu.CompilerParams(vmem_limit_bytes=LIMIT),
        name="mixers_backward",
    )(places, proj, cosine, sine, taps, conv_b, heads, y, states, w_mix, wa, *middle_low)


def per_device(
    tokens,
    cotangent,
    gain_attn,
    gain_mlp,
    w_qkv,
    w_o,
    w_zx,
    w_side,
    w_out,
    w_gu,
    w_down,
    conv_w,
    conv_bias,
    a_log,
    dt_bias,
    d_skip,
):
    ctx = lax.axis_index("ctx")
    chip, core = ctx // 2, ctx % 2
    blocks = jnp.arange(NCTX, dtype=jnp.int32)
    places = 2 * ((blocks // 2 - chip + CHIPS) % CHIPS) + (core ^ (blocks % 2))
    own_tokens, own_cot = tokens[0], cotangent[0]
    gain_attn, gain_mlp, conv_w, conv_bias = gain_attn[0], gain_mlp[0], conv_w[0], conv_bias[0]
    w_qkv, w_o, w_zx, w_side, w_out, w_gu, w_down = (
        w[0] for w in (w_qkv, w_o, w_zx, w_side, w_out, w_gu, w_down)
    )
    rows = w_qkv.shape[0]

    small = jnp.concatenate([gain_attn, gain_mlp, conv_bias, conv_w.reshape(-1)])
    wide_by = -(-small.shape[0] // rows)
    small = jnp.pad(small, (0, rows * wide_by - small.shape[0])).reshape(rows, wide_by)
    small = jnp.pad(small, ((0, 0), (0, GA - SPARE - wide_by)))
    mixers_cols, ff_cols = columns_for_all(w_zx, w_side, w_qkv, w_gu, small)
    wa = to_owners(mixers_cols).reshape(D, GA)
    small = wa[:, SPARE : SPARE + wide_by].reshape(NDEV, rows * wide_by).astype(F32)
    per = D // NDEV
    gain_a = small[:, :per].reshape(D)
    gain_m = small[:, per : 2 * per].reshape(D)
    bias_all = small[:, 2 * per : 2 * per + CPER].reshape(CONV)
    taps_all = small[:, 2 * per + CPER : 2 * per + 5 * CPER].reshape(-1, KW, CPER)
    taps_all = taps_all.transpose(1, 0, 2).reshape(KW, CONV)
    mine = lambda v: jnp.concatenate(
        [v[..., INNER:], lax.dynamic_slice_in_dim(v, ctx * XC, XC, v.ndim - 1)], axis=-1
    )
    taps, conv_b = mine(taps_all), mine(bias_all)

    tok_low = jnp.concatenate(gather_rows(own_tokens), axis=0)
    tok = tok_low.astype(F32)

    swap_pairs = [(c, NCTX * (c % NDP) + c // NDP) for c in range(NDEV)]
    back_pairs = [(t, s) for s, t in swap_pairs]
    n_o, n_out, n_down = w_o.shape[0], w_out.shape[0], w_down.shape[0]
    by_rows = lambda v, at, size: v[:, at : at + size].reshape(NDP * size, D)
    late = lax.ppermute(
        jnp.concatenate([w_o, w_out, w_down], axis=0), ("dp", "ctx"), swap_pairs
    )
    late = dp_gather(after(late, wa))
    w_mix = jnp.concatenate([by_rows(late, 0, n_o), by_rows(late, n_o, n_out)], axis=0)
    down = by_rows(late, n_o + n_out, n_down)
    gu = to_owners(after(ff_cols, late)).reshape(D, 2 * HID)
    cot = gather_rows(after(own_cot, tok_low))

    normed = (tok * rms_factor(tok) * gain_a[None, :]).astype(BF16)
    proj = mm(normed, wa)
    cosine, sine = rope_tables()
    heads = lambda v: jnp.pad(
        lax.dynamic_slice_in_dim(v[0], ctx * HPD, HPD, 0), (HEAD_SIZE, HEAD_SIZE - HPD)
    )
    head_rows = jnp.stack([heads(a_log), heads(dt_bias), heads(d_skip), heads(jnp.ones_like(a_log))])
    head_rows = jnp.pad(head_rows, ((0, 4), (0, 0)))
    shared = (places, proj, cosine, sine, taps, conv_b[None], head_rows)
    mixed, y, states, *parts = mixers_forward(*shared, w_mix)
    own_residual = own_tokens.astype(F32)
    middle = own_residual + scatter_rows(parts[:CHIPS], parts[CHIPS:])

    factor_m = rms_factor(middle)
    normed2 = gather_rows((middle * factor_m * gain_m[None, :]).astype(BF16))
    keep_n, pass_n, keep_d, pass_d, hidden, grad_gate_up = mlp(normed2, cot, gu, down)
    grad_normed2 = scatter_rows(keep_n, pass_n)
    grad_middle = own_cot.astype(F32) + norm_back(middle, factor_m, gain_m[None, :], grad_normed2)
    middle_low = gather_rows(grad_middle.astype(BF16))
    grad_gu = tn_sum(normed2, [grad_gate_up])
    grad_down = tn_sum([hidden], cot)
    pass_d = [after(v, middle_low[5]) for v in pass_d]
    block_out = middle + scatter_rows(keep_d, pass_d)

    grad_mix = tn_sum([mixed], middle_low)
    split = lambda v: v.reshape(NDP, -1, D)
    late_terms = jnp.concatenate(
        [split(grad_mix[:HEAD_SIZE]), split(grad_mix[HEAD_SIZE:]), split(grad_down)], axis=1
    )
    ff_terms = grad_gu.reshape(NDEV, rows, 2 * HID)
    grad_proj, conv_terms, head_sum, skip_sum, *parts = mixers_backward(
        *shared, y, states, after(w_mix, ff_terms, late_terms), wa, middle_low
    )
    grad_normed = scatter_rows(parts[:CHIPS], parts[CHIPS:])
    grad_tokens = grad_middle + norm_back(
        own_residual, rms_factor(own_residual), gain_a[None, :], grad_normed
    )
    place = lambda v, at, size: lax.dynamic_update_slice_in_dim(
        jnp.zeros(v.shape[:-1] + (size,), F32), v, at, v.ndim - 1
    )
    conv_terms = conv_terms[: KW + 1]
    conv_terms = jnp.concatenate(
        [place(conv_terms[:, X0:], ctx * XC, INNER), conv_terms[:, :X0]], axis=1
    )
    conv_terms = conv_terms.reshape(KW + 1, NDEV, CPER).transpose(1, 0, 2)
    skip_terms = jnp.sum(skip_sum[0].reshape(HPD, SP), axis=1)
    head_terms = jnp.stack([*head_sum[:2, HEAD_SIZE : HEAD_SIZE + HPD], skip_terms])
    head_terms = place(head_terms, ctx * HPD, SH).reshape(1, 3 * SH)
    small_terms = jnp.concatenate(
        [conv_terms.reshape(NDEV, -1), jnp.broadcast_to(head_terms, (NDEV, 3 * SH))], axis=1
    )
    coarse = small_terms.astype(BF16).astype(F32)
    small_terms = jnp.concatenate([coarse, small_terms - coarse], axis=1)
    wide_by = -(-2 * N_SMALL // rows)
    small_terms = jnp.pad(small_terms, ((0, 0), (0, rows * wide_by - 2 * N_SMALL)))
    small_terms = small_terms.reshape(D, wide_by)
    small_terms = jnp.pad(
        small_terms, ((0, 0), (SPARE - V0, GA - SPARE - wide_by))
    )
    grad_wa = mixer_grad(normed, grad_proj, small_terms)
    got = to_owners(grad_wa.reshape(NDEV, rows, GA))
    out_zx, out_side, out_qkv, gain_sum, small_got = mixers_owned(got, w_zx, w_side, w_qkv)
    out_gain_a = gain_sum[:, 0] / gain_attn.astype(F32)
    small_got = small_got[:, SPARE - V0 : SPARE - V0 + wide_by].reshape(-1)
    small_got = small_got[:N_SMALL] + small_got[N_SMALL : 2 * N_SMALL]
    out_conv = small_got[: (KW + 1) * CPER].reshape(KW + 1, CPER)
    out_heads = small_got[(KW + 1) * CPER :].reshape(3, 1, SH)
    out_gu, gain_sum = ff_owned(to_owners(ff_terms), w_gu)
    out_gain_m = gain_sum[:, 0] / gain_mlp.astype(F32)
    out_rows = lax.ppermute(dp_sum(late_terms), ("dp", "ctx"), back_pairs)
    return (
        block_out[None],
        grad_tokens[None],
        out_gain_a[None],
        out_gain_m[None],
        out_qkv[None],
        out_rows[:n_o][None],
        out_zx[None],
        out_side[None],
        out_rows[n_o : n_o + n_out][None],
        out_gu[None],
        out_rows[n_o + n_out :][None],
        out_conv[1:][None],
        out_conv[0][None],
        out_heads[0],
        out_heads[1],
        out_heads[2],
    )


def solution(mesh):
    rows = P("dp", "ctx", None)
    vector = P(None, ("dp", "ctx"))
    matrix = P(None, ("dp", "ctx"), None)
    taps = P(None, None, ("dp", "ctx"))
    weights = (vector, vector) + (matrix,) * 7 + (taps, vector, P(), P(), P())
    return jax.shard_map(
        per_device,
        mesh=mesh,
        in_specs=(rows, rows) + weights,
        out_specs=(rows, rows) + weights,
        check_vma=False,
    )
```

```python
import functools
import math

import jax
import jax.numpy as jnp
from jax import lax
from jax.experimental import pallas as pl
from jax.experimental.pallas import tpu as pltpu
from jax.sharding import PartitionSpec as P

D = 1024
HEAD_SIZE = 64
SH = 24
SP = 64
SN = 128
FF = 2048
KW = 4
BLK = 128
INNER = 1536
CONV = 1792
QUERY_FEATURES = 512
KEY_FEATURES = 128
NDP = 16
NCTX = 8
CHIPS = 4
HPD = SH // NCTX
XC = INNER // NCTX
HID = FF // NCTX
CV = 2 * SN + XC
X0, Z0, Q0 = 2 * SN, CV, CV + XC
K0, V0, T0 = Q0 + HEAD_SIZE, Q0 + 2 * HEAD_SIZE, Q0 + 3 * HEAD_SIZE
GA = Q0 + 4 * HEAD_SIZE
SPARE = T0 + HPD
NDEV = NDP * NCTX
CPER = CONV // NDEV
N_SMALL = (KW + 1) * CPER + 3 * SH

EPSILON = 1e-05
ROPE_BASE = 100000000000.0
F32 = jnp.float32
BF16 = jnp.bfloat16
HIGHEST = lax.Precision.HIGHEST


def dot(a, b, dims):
    return lax.dot_general(a, b, (dims, ((), ())), preferred_element_type=F32)


def mm(a, b):
    return dot(a, b, ((1,), (0,)))


def mm_nt(a, b):
    return dot(a, b, ((1,), (1,)))


def mm_tn(a, b):
    return dot(a, b, ((0,), (0,)))


def chip_shift(array, by):
    return lax.ppermute(array, "ctx", [(i, (i + 2 * by) % NCTX) for i in range(NCTX)])


def core_swap(array):
    return lax.ppermute(array, "ctx", [(i, i ^ 1) for i in range(NCTX)])


def gather_rows(own):
    same = [own, chip_shift(own, -1), None, chip_shift(own, 1)]
    same[2] = chip_shift(own, 2)
    other = [None] * CHIPS
    for k in (0, 1, 3, 2):
        other[k] = core_swap(same[k])
    return [block for pair in zip(same, other) for block in pair]


def swap_add(keep, pass_on):
    return {k: keep[k] + core_swap(pass_on[k]).astype(F32) for k in (2, 1, 3, 0)}


def shift_sum(both, shifted):
    total = both[0]
    for k in (1, 3, 2):
        total = total + shifted[k].astype(F32)
    return total


def scatter_rows(keep, pass_on):
    both = swap_add(keep, pass_on)
    return shift_sum(both, {k: chip_shift(both[k].astype(BF16), k) for k in (2, 1, 3)})


def dp_gather(own):
    return lax.all_to_all(jnp.broadcast_to(own[None], (NDP,) + own.shape), "dp", 0, 0)


def to_owners(parts):
    return lax.all_to_all(parts, ("dp", "ctx"), 0, 0)


SMEM = pl.BlockSpec(memory_space=pltpu.SMEM)
VMEM = pl.BlockSpec(memory_space=pltpu.VMEM)
LIMIT = 48 * 1024 * 1024


def after(value, *others):
    return lax.optimization_barrier((value,) + others)[0]


def mlp_kernel(*refs):
    normed, cot, (gu, down) = refs[:NCTX], refs[NCTX : 2 * NCTX], refs[2 * NCTX : 2 * NCTX + 2]
    outs = refs[2 * NCTX + 2 :]
    keep_n, pass_n, keep_d, pass_d = (outs[CHIPS * m : CHIPS * (m + 1)] for m in range(4))
    hid, dgu = outs[4 * CHIPS :]
    for k in (2, 1, 3, 0):
        normed2 = jnp.concatenate([normed[2 * k][...], normed[2 * k + 1][...]], axis=0)
        upstream = jnp.concatenate([cot[2 * k][...], cot[2 * k + 1][...]], axis=0)
        gate_up = mm(normed2, gu[...])
        gate_half, up_half = gate_up[:, :HID], gate_up[:, HID:]
        sigmoid_gate = sigmoid(gate_half)
        silu_gate = gate_half * sigmoid_gate
        hidden = (silu_gate * up_half).astype(BF16)
        grad_hidden = mm_nt(upstream, down[...])
        grad_gate = grad_hidden * up_half * (sigmoid_gate + silu_gate * (1.0 - sigmoid_gate))
        grad_gate_up = jnp.concatenate([grad_gate, grad_hidden * silu_gate], axis=1).astype(BF16)
        at = pl.ds(2 * k * BLK, 2 * BLK)
        hid[at, :] = hidden
        dgu[at, :] = grad_gate_up
        grad_normed2 = mm_nt(grad_gate_up, gu[...])
        keep_n[k][...] = grad_normed2[:BLK]
        pass_n[k][...] = grad_normed2[BLK:].astype(BF16)
        out = mm(hidden, down[...])
        keep_d[k][...] = out[:BLK]
        pass_d[k][...] = out[BLK:].astype(BF16)


def mlp(normed2, cot, gu, down):
    shape = jax.ShapeDtypeStruct
    keep, passed = [shape((BLK, D), F32)] * CHIPS, [shape((BLK, D), BF16)] * CHIPS
    rows = NCTX * BLK
    outs = pl.pallas_call(
        mlp_kernel,
        out_shape=keep + passed + keep + passed
        + [shape((rows, HID), BF16), shape((rows, 2 * HID), BF16)],
        cost_estimate=pl.CostEstimate(
            flops=2 * rows * D * HID * 6, bytes_accessed=12_000_000, transcendentals=0
        ),
        compiler_params=pltpu.CompilerParams(vmem_limit_bytes=LIMIT),
        name="feed_forward",
    )(*normed2, *cot, gu, down)
    parts = [outs[CHIPS * m : CHIPS * (m + 1)] for m in range(4)]
    return [*parts, *outs[4 * CHIPS :]]


def tn_kernel(n_left, *refs):
    left = jnp.concatenate([r[...] for r in refs[:n_left]], axis=0)
    right = jnp.concatenate([r[...] for r in refs[n_left:-1]], axis=0)
    refs[-1][...] = mm_tn(left, right).astype(BF16)


def mixer_grad_kernel(normed, grad_proj, small, out):
    total = mm_tn(normed[...], grad_proj[...])
    out[:, :V0] = total[:, :V0].astype(BF16)
    out[:, V0:] = (total[:, V0:] + small[...]).astype(BF16)


def mixer_grad(normed, grad_proj, small):
    return pl.pallas_call(
        mixer_grad_kernel,
        out_shape=jax.ShapeDtypeStruct((D, GA), BF16),
        cost_estimate=pl.CostEstimate(
            flops=2 * D * GA * NCTX * BLK, bytes_accessed=8_000_000, transcendentals=0
        ),
        compiler_params=pltpu.CompilerParams(vmem_limit_bytes=LIMIT),
        name="mixer_weight_grad",
    )(normed, grad_proj, small)


def columns_kernel(zx, side, qkv, gu, small, mixers, ff):
    zx, side, qkv, gu, small = (v[...].astype(F32) for v in (zx, side, qkv, gu, small))
    for j in range(NCTX):
        head = j // (NCTX // 2) * HEAD_SIZE
        key = QUERY_FEATURES + head
        value = QUERY_FEATURES + KEY_FEATURES + head
        own = [
            side[:, : 2 * SN],
            zx[:, INNER + j * XC : INNER + (j + 1) * XC],
            zx[:, j * XC : (j + 1) * XC],
            qkv[:, j * HEAD_SIZE : (j + 1) * HEAD_SIZE],
            qkv[:, key : key + HEAD_SIZE],
            qkv[:, value : value + HEAD_SIZE],
            side[:, 2 * SN + j * HPD : 2 * SN + (j + 1) * HPD],
            small,
        ]
        own = jnp.concatenate(own, axis=1).astype(BF16)
        units = [gu[:, j * HID : (j + 1) * HID], gu[:, FF + j * HID : FF + (j + 1) * HID]]
        units = jnp.concatenate(units, axis=1).astype(BF16)
        for i in range(NDP):
            mixers[i * NCTX + j] = own
            ff[i * NCTX + j] = units


def columns_for_all(zx, side, qkv, gu, small):
    rows = zx.shape[0]
    shape = jax.ShapeDtypeStruct
    return pl.pallas_call(
        columns_kernel,
        out_shape=(shape((NDEV, rows, GA), BF16), shape((NDEV, rows, 2 * HID), BF16)),
        cost_estimate=pl.CostEstimate(flops=0, bytes_accessed=3_000_000, transcendentals=0),
        compiler_params=pltpu.CompilerParams(vmem_limit_bytes=LIMIT),
        name="columns",
    )(zx, side, qkv, gu, small)


def source_sum(parts, j):
    total = parts[j].astype(F32)
    for i in range(1, NDP):
        total = total + parts[i * NCTX + j].astype(F32)
    return total


def row_dot(weight, grad):
    total = jnp.sum(weight[...].astype(F32) * grad, axis=1, keepdims=True)
    return jnp.broadcast_to(total, (total.shape[0], SN))


def mixers_owned_kernel(parts, zx, side, qkv, out_zx, out_side, out_qkv, out_gain, out_small):
    got = [source_sum(parts, j) for j in range(NCTX)]
    half = NCTX // 2
    grads = jnp.concatenate([g[:, Z0:Q0] for g in got] + [g[:, X0:Z0] for g in got], axis=1)
    out_zx[...] = grads
    gain = row_dot(zx, grads)
    both = sum(g[:, :X0] for g in got[1:]) + got[0][:, :X0]
    grads = jnp.concatenate([both] + [g[:, T0 : T0 + HPD] for g in got], axis=1)
    out_side[...] = grads
    gain = gain + row_dot(side, grads)
    pairs = [sum(g[:, K0:T0] for g in got[h + 1 : h + half]) + got[h][:, K0:T0] for h in (0, half)]
    grads = jnp.concatenate(
        [g[:, Q0:K0] for g in got]
        + [p[:, :HEAD_SIZE] for p in pairs]
        + [p[:, HEAD_SIZE:] for p in pairs],
        axis=1,
    )
    out_qkv[...] = grads
    out_gain[...] = gain + row_dot(qkv, grads)
    out_small[...] = sum(g[:, V0:] for g in got[1:]) + got[0][:, V0:]


def mixers_owned(parts, zx, side, qkv):
    shape = jax.ShapeDtypeStruct
    rows = zx.shape[0]
    return pl.pallas_call(
        mixers_owned_kernel,
        out_shape=(
            shape(zx.shape, F32),
            shape(side.shape, F32),
            shape(qkv.shape, F32),
            shape((rows, SN), F32),
            shape((rows, SN), F32),
        ),
        cost_estimate=pl.CostEstimate(flops=0, bytes_accessed=3_000_000, transcendentals=0),
        compiler_params=pltpu.CompilerParams(vmem_limit_bytes=LIMIT),
        name="mixers_owned",
    )(parts, zx, side, qkv)


def ff_owned_kernel(parts, gu, out_gu, out_gain):
    got = [source_sum(parts, j) for j in range(NCTX)]
    grads = jnp.concatenate([g[:, :HID] for g in got] + [g[:, HID:] for g in got], axis=1)
    out_gu[...] = grads
    out_gain[...] = row_dot(gu, grads)


def ff_owned(parts, gu):
    shape = jax.ShapeDtypeStruct
    return pl.pallas_call(
        ff_owned_kernel,
        out_shape=(shape(gu.shape, F32), shape((gu.shape[0], SN), F32)),
        cost_estimate=pl.CostEstimate(flops=0, bytes_accessed=2_000_000, transcendentals=0),
        compiler_params=pltpu.CompilerParams(vmem_limit_bytes=LIMIT),
        name="ff_owned",
    )(parts, gu)


def tn_sum(left, right):
    n, m = left[0].shape[1], right[0].shape[1]
    return pl.pallas_call(
        functools.partial(tn_kernel, len(left)),
        out_shape=jax.ShapeDtypeStruct((n, m), BF16),
        cost_estimate=pl.CostEstimate(
            flops=2 * n * m * NCTX * BLK, bytes_accessed=6 * n * m, transcendentals=0
        ),
        compiler_params=pltpu.CompilerParams(vmem_limit_bytes=LIMIT),
        name="weight_grad",
    )(*left, *right)


def rms_factor(hidden_in):
    return lax.rsqrt(jnp.mean(hidden_in * hidden_in, axis=-1, keepdims=True) + EPSILON)


def norm_back(hidden_in, factor, gain, upstream):
    scaled = upstream * gain
    inner = jnp.mean(scaled * hidden_in, axis=-1, keepdims=True)
    return factor * scaled - hidden_in * (factor * factor * factor) * inner


def rope_tables():
    exponent = -(2.0 * jnp.arange(HEAD_SIZE // 2, dtype=F32)) / HEAD_SIZE
    inverse = jnp.power(jnp.float32(ROPE_BASE), exponent)
    angles = jnp.arange(NCTX * BLK, dtype=F32)[:, None] * inverse[None, :]
    cosine, sine = jnp.cos(angles), jnp.sin(angles)
    return (
        jnp.concatenate([cosine] * 4, axis=1),
        jnp.concatenate([-sine, sine, -sine, sine], axis=1),
    )


def sigmoid(v):
    return 1.0 / (1.0 + jnp.exp(-v))


def softplus(v):
    return jnp.maximum(v, 0.0) + jnp.log1p(jnp.exp(-jnp.abs(v)))


def exact(a, b, dims):
    return lax.dot_general(a, b, (dims, ((), ())), precision=HIGHEST, preferred_element_type=F32)


def wide(columns):
    return jnp.concatenate([jnp.broadcast_to(c, (BLK, SP)) for c in columns], axis=1)


def tall(scalars):
    return jnp.concatenate([jnp.broadcast_to(c, (SP, SN)) for c in scalars], axis=0)


def head_sums(v):
    return [jnp.sum(v[:, h * SP : (h + 1) * SP], axis=1, keepdims=True) for h in range(HPD)]


def iota(shape, dim):
    return lax.broadcasted_iota(jnp.int32, shape, dim)


def turn(v):
    first = (iota(v.shape, 1) // (HEAD_SIZE // 2)) % 2 == 0
    return jnp.where(
        first, pltpu.roll(v, 2 * HEAD_SIZE - HEAD_SIZE // 2, 1), pltpu.roll(v, HEAD_SIZE // 2, 1)
    )


def rotated(block, cosine, sine):
    both = block[:, Q0:V0]
    return both * cosine + turn(both) * sine


def block_rows(a):
    return pl.ds(a * BLK, BLK)


def held_rows(places, a):
    return pl.ds(pl.multiple_of(places[a] * BLK, BLK), BLK)


def probabilities(query, keys, a):
    scores = mm_nt(query, keys) * (1.0 / math.sqrt(HEAD_SIZE))
    seen = iota(scores.shape, 0) + a * BLK >= iota(scores.shape, 1)
    scores = jnp.where(seen, scores, -jnp.inf)
    weights = jnp.exp(scores - jnp.max(scores, axis=1, keepdims=True))
    return weights / jnp.sum(weights, axis=1, keepdims=True)


class Block:
    def __init__(self, block, tail, taps, conv_b, heads):
        conv_in = block[:, :CV].astype(BF16).astype(F32)
        self.next_tail = conv_in[BLK - 8 :]
        extended = jnp.concatenate([tail, conv_in], axis=0)
        self.shifted = [extended[8 - d : 8 - d + BLK] for d in range(KW)]
        total = conv_b
        for d in range(KW):
            total = total + taps[KW - 1 - d : KW - d] * self.shifted[d]
        self.total = total
        self.sig = sigmoid(total)
        low = (total * self.sig).astype(BF16)
        self.b, self.c, self.x = low[:, :SN], low[:, SN : 2 * SN], low[:, 2 * SN :]
        raw = block[:, V0:] + heads[1:2]
        self.step = softplus(raw)
        self.step_slope = sigmoid(raw)
        self.rate = -jnp.exp(heads[0:1]) * heads[3:4]
        self.decay = self.rate * self.step
        self.tri = (iota((BLK, BLK), 0) >= iota((BLK, BLK), 1)).astype(F32)
        self.cum = exact(self.tri, self.decay, ((1,), (0,)))
        cum_t, step_t = self.cum.T, self.step.T
        lanes = [HEAD_SIZE + h for h in range(HPD)]
        self.cum_cols = [self.cum[:, l : l + 1] for l in lanes]
        self.last = [self.cum[BLK - 1 :, l : l + 1] for l in lanes]
        self.step_cols = [self.step[:, l : l + 1] for l in lanes]
        self.step_rows = [step_t[l : l + 1] for l in lanes]
        causal = iota((BLK, BLK), 0) >= iota((BLK, BLK), 1)
        self.fade = [
            jnp.exp(jnp.where(causal, self.cum_cols[h] - cum_t[l : l + 1], -jnp.inf))
            for h, l in enumerate(lanes)
        ]
        self.inter = mm_nt(self.c, self.b)
        self.to_end = [jnp.exp(self.last[h] - self.cum_cols[h]) for h in range(HPD)]
        self.grown = wide([jnp.exp(v) for v in self.cum_cols])
        self.weight = wide([self.to_end[h] * self.step_cols[h] for h in range(HPD)])
        self.carry = tall([jnp.exp(v) for v in self.last])
        self.skip = wide([heads[2:3, l : l + 1] for l in lanes])
        self.x32 = self.x.astype(F32)

    def head(self, v, h):
        return v[:, h * SP : (h + 1) * SP]


def forward_kernel(*refs):
    places, wa, cosine, sine, taps, conv_b, heads = refs[:7]
    tokens, refs = refs[7 : 7 + NCTX], refs[7 + NCTX :]
    normed, proj, mixed, y_out, states, keys, values = refs
    gain = wa[:, V0:].astype(F32).T[SPARE - V0 : SPARE - V0 + 1]
    for r in range(NCTX):
        token = tokens[r][...].astype(F32)
        low = (token * rms_factor(token) * gain).astype(BF16)
        normed[block_rows(r), :] = low
        proj[block_rows(r), :] = mm(low, wa[...])
    taps, conv_b, heads = taps[...], conv_b[...], heads[...]
    tail = jnp.zeros((8, CV), F32)
    state = jnp.zeros((XC, SN), F32)
    for a in range(NCTX):
        at = held_rows(places, a)
        block = proj[at, :]
        both = rotated(block, cosine[block_rows(a), :], sine[block_rows(a), :]).astype(BF16)
        keys[block_rows(a), :] = both[:, HEAD_SIZE:]
        values[block_rows(a), :] = block[:, V0:T0].astype(BF16)
        seen = pl.ds(0, (a + 1) * BLK)
        probs = probabilities(both[:, :HEAD_SIZE], keys[seen, :], a)
        attended = mm(probs.astype(BF16), values[seen, :])
        now = Block(block, tail, taps, conv_b, heads)
        tail = now.next_tail
        states[a] = state
        y = now.grown * mm_nt(now.c, state.astype(BF16)) + now.skip * now.x32
        inner = [
            mm((now.inter * now.fade[h] * now.step_rows[h]).astype(BF16), now.head(now.x, h))
            for h in range(HPD)
        ]
        y = y + jnp.concatenate(inner, axis=1)
        y_out[block_rows(a), :] = y
        state = now.carry * state + mm_tn((now.x32 * now.weight).astype(BF16), now.b)
        gate = block[:, Z0:Q0]
        gated = y * gate * sigmoid(gate)
        mixed[at, :] = jnp.concatenate([attended, gated], axis=1).astype(BF16)


def mix_kernel(mixed, w_mix, *outs):
    for k in (2, 1, 3, 0):
        out = mm(mixed[pl.ds(2 * k * BLK, 2 * BLK), :], w_mix[...])
        outs[k][...] = out[:BLK]
        outs[CHIPS + k][...] = out[BLK:].astype(BF16)


def mix(mixed, w_mix):
    shape = jax.ShapeDtypeStruct
    return pl.pallas_call(
        mix_kernel,
        out_shape=[shape((BLK, D), F32)] * CHIPS + [shape((BLK, D), BF16)] * CHIPS,
        cost_estimate=pl.CostEstimate(
            flops=2 * NCTX * BLK * D * 256, bytes_accessed=4_000_000, transcendentals=0
        ),
        compiler_params=pltpu.CompilerParams(vmem_limit_bytes=LIMIT),
        name="mix",
    )(mixed, w_mix)


def backward_kernel(*refs):
    places, proj, cosine, sine, taps, conv_b, heads, y_in, states, w_mix, wa = refs[:11]
    middle_low, refs = refs[11 : 11 + NCTX], refs[11 + NCTX :]
    grad_proj, conv_out, head_out, skip_out = refs[:4]
    keep, passed = refs[4 : 4 + CHIPS], refs[4 + CHIPS : 4 + 2 * CHIPS]
    keys, values, grad_mixed, grad_q, grad_k, grad_v = refs[4 + 2 * CHIPS :]
    taps, conv_b, heads = taps[...], conv_b[...], heads[...]
    for r in range(NCTX):
        grad_mixed[block_rows(r), :] = mm_nt(middle_low[r][...], w_mix[...])
    queries = []
    for a in range(NCTX):
        block = proj[held_rows(places, a), :]
        both = rotated(block, cosine[block_rows(a), :], sine[block_rows(a), :]).astype(BF16)
        queries.append(both[:, :HEAD_SIZE])
        keys[block_rows(a), :] = both[:, HEAD_SIZE:]
        values[block_rows(a), :] = block[:, V0:T0].astype(BF16)
    for a in reversed(range(NCTX)):
        seen = pl.ds(0, (a + 1) * BLK)
        grad_attended = grad_mixed[held_rows(places, a), :][:, :HEAD_SIZE].astype(BF16)
        probs = probabilities(queries[a], keys[seen, :], a)
        grad_probs = mm_nt(grad_attended, values[seen, :])
        delta = jnp.sum(probs * grad_probs, axis=1, keepdims=True)
        grad_scores = (probs * (grad_probs - delta) * (1.0 / math.sqrt(HEAD_SIZE))).astype(BF16)
        grad_q[block_rows(a), :] = mm(grad_scores, keys[seen, :])
        more_k = mm_tn(grad_scores, queries[a])
        more_v = mm_tn(probs.astype(BF16), grad_attended)
        if a < NCTX - 1:
            more_k = more_k + grad_k[seen, :]
            more_v = more_v + grad_v[seen, :]
        grad_k[seen, :] = more_k
        grad_v[seen, :] = more_v
    adjoint = jnp.zeros((XC, SN), F32)
    later = jnp.zeros((8, CV), F32)
    conv_rows = [jnp.zeros((1, CV), F32) for _ in range(KW + 1)]
    grad_alog = jnp.zeros((1, SN), F32)
    grad_bias = jnp.zeros((1, SN), F32)
    grad_skip = jnp.zeros((1, XC), F32)
    lane = iota((BLK, SN), 1)
    for a in reversed(range(NCTX)):
        at = held_rows(places, a)
        block = proj[at, :]
        if a:
            tail = proj[held_rows(places, a - 1), :][BLK - 8 :, :CV].astype(BF16).astype(F32)
        else:
            tail = jnp.zeros((8, CV), F32)
        now = Block(block, tail, taps, conv_b, heads)
        gate = block[:, Z0:Q0]
        sig = sigmoid(gate)
        grad_gated = grad_mixed[at, :][:, HEAD_SIZE:]
        y = y_in[block_rows(a), :]
        grad_gate = grad_gated * y * (sig + gate * sig * (1.0 - sig))
        grad_y = grad_gated * gate * sig
        grad_skip = grad_skip + jnp.sum(grad_y * now.x32, axis=0, keepdims=True)
        grad_y_low = grad_y.astype(BF16)
        grad_x = now.skip * grad_y
        state = states[a]
        state_low = state.astype(BF16)
        grad_inter = jnp.zeros((BLK, BLK), F32)
        cum_cols, step_cols, inner = [], [], []
        for h in range(HPD):
            gy, x = now.head(grad_y_low, h), now.head(now.x, h)
            grad_mixing = mm_nt(gy, x)
            faded = now.fade[h] * now.step_rows[h]
            grad_inter = grad_inter + grad_mixing * faded
            inner.append(mm_tn((now.inter * faded).astype(BF16), gy))
            product = grad_mixing * now.inter * now.fade[h]
            column = jnp.sum(product.T, axis=1, keepdims=True)
            row = jnp.sum(product * now.step_rows[h], axis=1, keepdims=True)
            step_cols.append(column)
            cum_cols.append(row - column * now.step_cols[h])
        grad_x = grad_x + jnp.concatenate(inner, axis=1)
        grad_inter = grad_inter.astype(BF16)
        grown_y = grad_y * now.grown
        grown_low = grown_y.astype(BF16)
        grad_c = mm(grad_inter, now.b) + mm(grown_low, state_low)
        from_state = head_sums(grown_y * mm_nt(now.c, state_low))
        adjoint_low = adjoint.astype(BF16)
        weighted = (now.x32 * now.weight).astype(BF16)
        grad_b = mm_tn(grad_inter, now.c) + mm(weighted, adjoint_low)
        grad_weighted = mm_nt(now.b, adjoint_low)
        grad_x = grad_x + grad_weighted * now.weight
        grad_weight = head_sums(grad_weighted * now.x32)
        carried = now.carry * adjoint * state
        grad_cum = jnp.zeros((BLK, SN), F32)
        grad_step = jnp.zeros((BLK, SN), F32)
        for h in range(HPD):
            step_col = step_cols[h] + grad_weight[h] * now.to_end[h]
            pulled = grad_weight[h] * now.to_end[h] * now.step_cols[h]
            last = jnp.sum(pulled, axis=0, keepdims=True) + jnp.sum(
                jnp.sum(carried[h * SP : (h + 1) * SP], axis=1, keepdims=True), axis=0, keepdims=True
            )
            cum_col = cum_cols[h] + from_state[h] - pulled
            cum_col = jnp.where(iota((BLK, 1), 0) == BLK - 1, cum_col + last, cum_col)
            here = lane == HEAD_SIZE + h
            grad_cum = jnp.where(here, cum_col, grad_cum)
            grad_step = jnp.where(here, step_col, grad_step)
        adjoint = now.carry * adjoint + mm_tn(grown_low, now.c)
        grad_decay = exact(now.tri, grad_cum, ((0,), (0,)))
        grad_alog = grad_alog + jnp.sum(grad_decay * now.decay, axis=0, keepdims=True)
        grad_dt = (grad_step + grad_decay * now.rate) * now.step_slope
        grad_bias = grad_bias + jnp.sum(grad_dt, axis=0, keepdims=True)
        grad_total = jnp.concatenate([grad_b, grad_c, grad_x], axis=1) * (
            now.sig + now.total * now.sig * (1.0 - now.sig)
        )
        conv_rows[0] = conv_rows[0] + jnp.sum(grad_total, axis=0, keepdims=True)
        extended = jnp.concatenate([grad_total, later], axis=0)
        later = grad_total[:8]
        grad_conv_in = jnp.zeros((BLK, CV), F32)
        for d in range(KW):
            k = KW - 1 - d
            conv_rows[1 + k] = conv_rows[1 + k] + jnp.sum(
                grad_total * now.shifted[d], axis=0, keepdims=True
            )
            grad_conv_in = grad_conv_in + taps[k : k + 1] * extended[d : d + BLK]
        both = jnp.concatenate([grad_q[block_rows(a), :], grad_k[block_rows(a), :]], axis=1)
        both = both * cosine[block_rows(a), :] + turn(both * sine[block_rows(a), :])
        grad_dt = pltpu.roll(grad_dt, HEAD_SIZE, 1)[:, :HEAD_SIZE]
        grad_proj[at, :] = jnp.concatenate(
            [grad_conv_in, grad_gate, both, grad_v[block_rows(a), :], grad_dt], axis=1
        ).astype(BF16)
    for k in (2, 1, 3, 0):
        out = mm_nt(grad_proj[pl.ds(2 * k * BLK, 2 * BLK), :], wa[...])
        keep[k][...] = out[:BLK]
        passed[k][...] = out[BLK:].astype(BF16)
    conv_out[...] = jnp.concatenate(conv_rows + [jnp.zeros((3, CV), F32)], axis=0)
    head_out[...] = jnp.concatenate([grad_alog, grad_bias, jnp.zeros((6, SN), F32)], axis=0)
    skip_out[...] = jnp.concatenate([grad_skip, jnp.zeros((7, XC), F32)], axis=0)


def mixers_forward(places, wa, cosine, sine, taps, conv_b, heads, tokens):
    shape = jax.ShapeDtypeStruct
    rows = NCTX * BLK
    return pl.pallas_call(
        forward_kernel,
        in_specs=[SMEM] + [VMEM] * (6 + NCTX),
        out_specs=[VMEM] * 5,
        out_shape=(
            shape((rows, D), BF16),
            shape((rows, GA), F32),
            shape((rows, HEAD_SIZE + XC), BF16),
            shape((rows, XC), F32),
            shape((NCTX, XC, SN), F32),
        ),
        scratch_shapes=[pltpu.VMEM((rows, HEAD_SIZE), BF16)] * 2,
        cost_estimate=pl.CostEstimate(
            flops=16_000_000_000, bytes_accessed=16_000_000, transcendentals=4_000_000
        ),
        compiler_params=pltpu.CompilerParams(vmem_limit_bytes=LIMIT),
        name="mixers_forward",
    )(places, wa, cosine, sine, taps, conv_b, heads, *tokens)


def mixers_backward(
    places, proj, cosine, sine, taps, conv_b, heads, y, states, w_mix, wa, middle_low
):
    shape = jax.ShapeDtypeStruct
    rows = NCTX * BLK
    return pl.pallas_call(
        backward_kernel,
        in_specs=[SMEM] + [VMEM] * (10 + NCTX),
        out_specs=[VMEM] * (4 + 2 * CHIPS),
        out_shape=(
            shape((rows, GA), BF16),
            shape((8, CV), F32),
            shape((8, SN), F32),
            shape((8, XC), F32),
            *[shape((BLK, D), F32)] * CHIPS,
            *[shape((BLK, D), BF16)] * CHIPS,
        ),
        scratch_shapes=[pltpu.VMEM((rows, HEAD_SIZE), BF16)] * 2
        + [pltpu.VMEM((rows, HEAD_SIZE + XC), F32)]
        + [pltpu.VMEM((rows, HEAD_SIZE), F32)] * 3,
        cost_estimate=pl.CostEstimate(
            flops=38_000_000_000, bytes_accessed=16_000_000, transcendentals=8_000_000
        ),
        compiler_params=pltpu.CompilerParams(vmem_limit_bytes=LIMIT),
        name="mixers_backward",
    )(places, proj, cosine, sine, taps, conv_b, heads, y, states, w_mix, wa, *middle_low)


def per_device(
    tokens,
    cotangent,
    gain_attn,
    gain_mlp,
    w_qkv,
    w_o,
    w_zx,
    w_side,
    w_out,
    w_gu,
    w_down,
    conv_w,
    conv_bias,
    a_log,
    dt_bias,
    d_skip,
):
    ctx = lax.axis_index("ctx")
    chip, core = ctx // 2, ctx % 2
    blocks = jnp.arange(NCTX, dtype=jnp.int32)
    places = 2 * ((blocks // 2 - chip + CHIPS) % CHIPS) + (core ^ (blocks % 2))
    own_tokens, own_cot = tokens[0], cotangent[0]
    gain_attn, gain_mlp, conv_w, conv_bias = gain_attn[0], gain_mlp[0], conv_w[0], conv_bias[0]
    w_qkv, w_o, w_zx, w_side, w_out, w_gu, w_down = (
        w[0] for w in (w_qkv, w_o, w_zx, w_side, w_out, w_gu, w_down)
    )
    rows = w_qkv.shape[0]

    conv_small = jnp.concatenate([conv_bias, conv_w.reshape(-1)])
    wide_by = -(-conv_small.shape[0] // rows)
    conv_small = jnp.pad(conv_small, (0, rows * wide_by - conv_small.shape[0]))
    small = jnp.concatenate(
        [gain_attn[:, None], gain_mlp[:, None], conv_small.reshape(rows, wide_by)], axis=1
    )
    small = jnp.pad(small, ((0, 0), (0, GA - SPARE - 2 - wide_by)))
    mixers_cols, ff_cols = columns_for_all(w_zx, w_side, w_qkv, w_gu, small)
    wa = to_owners(mixers_cols).reshape(D, GA)
    gain_a = wa[:, SPARE].astype(F32)
    gain_m = wa[:, SPARE + 1].astype(F32)
    small = wa[:, SPARE + 2 : SPARE + 2 + wide_by].reshape(NDEV, rows * wide_by).astype(F32)
    bias_all = small[:, :CPER].reshape(CONV)
    taps_all = small[:, CPER : (KW + 1) * CPER].reshape(-1, KW, CPER)
    taps_all = taps_all.transpose(1, 0, 2).reshape(KW, CONV)
    mine = lambda v: jnp.concatenate(
        [v[..., INNER:], lax.dynamic_slice_in_dim(v, ctx * XC, XC, v.ndim - 1)], axis=-1
    )
    taps, conv_b = mine(taps_all), mine(bias_all)

    tok = gather_rows(own_tokens)
    swap_pairs = [(c, NCTX * (c % NDP) + c // NDP) for c in range(NDEV)]
    back_pairs = [(t, s) for s, t in swap_pairs]
    n_o, n_out, n_down = w_o.shape[0], w_out.shape[0], w_down.shape[0]
    mix_rows = lax.ppermute(
        jnp.concatenate([w_o, w_out, w_down], axis=0), ("dp", "ctx"), swap_pairs
    )
    late = dp_gather(after(mix_rows, wa))
    by_rows = lambda at, size: late[:, at : at + size].reshape(NDP * size, D)
    w_mix = jnp.concatenate([by_rows(0, n_o), by_rows(n_o, n_out)], axis=0)
    down = by_rows(n_o + n_out, n_down)
    gu = to_owners(after(ff_cols, late)).reshape(D, 2 * HID)
    cot = gather_rows(after(own_cot, wa))

    cosine, sine = rope_tables()
    heads = lambda v: jnp.pad(
        lax.dynamic_slice_in_dim(v[0], ctx * HPD, HPD, 0), (HEAD_SIZE, HEAD_SIZE - HPD)
    )
    head_rows = jnp.stack([heads(a_log), heads(dt_bias), heads(d_skip), heads(jnp.ones_like(a_log))])
    head_rows = jnp.pad(head_rows, ((0, 4), (0, 0)))
    shared = (cosine, sine, taps, conv_b[None], head_rows)
    normed, proj, mixed, y, states = mixers_forward(places, wa, *shared, tok)
    parts = [after(v, *cot) for v in mix(mixed, w_mix)]
    own_residual = own_tokens.astype(F32)
    middle = own_residual + scatter_rows(parts[:CHIPS], parts[CHIPS:])

    factor_m = rms_factor(middle)
    normed2 = gather_rows((middle * factor_m * gain_m[None, :]).astype(BF16))
    keep_n, pass_n, keep_d, pass_d, hidden, grad_gate_up = mlp(normed2, cot, gu, down)
    both_n = swap_add(keep_n, pass_n)
    sent_n = {k: both_n[k].astype(BF16) for k in (2, 1, 3)}
    grad_normed2 = shift_sum(both_n, {k: chip_shift(v, k) for k, v in sent_n.items()})
    hidden, grad_gate_up = (after(v, *sent_n.values()) for v in (hidden, grad_gate_up))
    grad_middle = own_cot.astype(F32) + norm_back(middle, factor_m, gain_m[None, :], grad_normed2)
    middle_low = gather_rows(grad_middle.astype(BF16))
    grad_gu = tn_sum(normed2, [grad_gate_up])
    grad_down = tn_sum([hidden], cot)
    both_d = swap_add(keep_d, pass_d)
    sent_d = {k: after(both_d[k].astype(BF16), *middle_low) for k in (2, 1, 3)}

    grad_mix = tn_sum([mixed], middle_low)
    split = lambda v: v.reshape(NDP, -1, D)
    late_terms = jnp.concatenate(
        [split(grad_mix[:HEAD_SIZE]), split(grad_mix[HEAD_SIZE:]), split(grad_down)], axis=1
    )
    ff_terms = grad_gu.reshape(NDEV, rows, 2 * HID)
    got_ff = to_owners(ff_terms)
    grad_proj, conv_terms, head_sum, skip_sum, *parts = mixers_backward(
        places,
        proj,
        *shared,
        y,
        states,
        after(w_mix, got_ff, late_terms, *sent_d.values()),
        wa,
        middle_low,
    )
    got_late = lax.all_to_all(late_terms, "dp", 0, 0)
    got_d = {k: chip_shift(v, k) for k, v in sent_d.items()}
    place = lambda v, at, size: lax.dynamic_update_slice_in_dim(
        jnp.zeros(v.shape[:-1] + (size,), F32), v, at, v.ndim - 1
    )
    conv_terms = conv_terms[: KW + 1]
    conv_terms = jnp.concatenate(
        [place(conv_terms[:, X0:], ctx * XC, INNER), conv_terms[:, :X0]], axis=1
    )
    conv_terms = conv_terms.reshape(KW + 1, NDEV, CPER).transpose(1, 0, 2)
    skip_terms = jnp.sum(skip_sum[0].reshape(HPD, SP), axis=1)
    head_terms = jnp.stack([*head_sum[:2, HEAD_SIZE : HEAD_SIZE + HPD], skip_terms])
    head_terms = place(head_terms, ctx * HPD, SH).reshape(1, 3 * SH)
    small_terms = jnp.concatenate(
        [conv_terms.reshape(NDEV, -1), jnp.broadcast_to(head_terms, (NDEV, 3 * SH))], axis=1
    )
    coarse = small_terms.astype(BF16).astype(F32)
    small_terms = jnp.concatenate([coarse, small_terms - coarse], axis=1)
    wide_by = -(-2 * N_SMALL // rows)
    small_terms = jnp.pad(small_terms, ((0, 0), (0, rows * wide_by - 2 * N_SMALL)))
    small_terms = small_terms.reshape(D, wide_by)
    small_terms = jnp.pad(
        small_terms, ((0, 0), (SPARE - V0, GA - SPARE - wide_by))
    )
    grad_proj = after(grad_proj, got_late, *got_d.values())
    grad_wa = mixer_grad(normed, grad_proj, small_terms)
    parts = [after(v, grad_wa) for v in parts]
    both = swap_add(parts[:CHIPS], parts[CHIPS:])
    grad_normed = shift_sum(both, {k: chip_shift(both[k].astype(BF16), k) for k in (2, 1, 3)})
    grad_tokens = grad_middle + norm_back(
        own_residual, rms_factor(own_residual), gain_a[None, :], grad_normed
    )
    both_d[0] = after(both_d[0], both[3])
    block_out = middle + shift_sum(both_d, got_d)
    got = to_owners(grad_wa.reshape(NDEV, rows, GA))
    out_zx, out_side, out_qkv, gain_sum, small_got = mixers_owned(got, w_zx, w_side, w_qkv)
    out_gain_a = gain_sum[:, 0] / gain_attn.astype(F32)
    small_got = small_got[:, SPARE - V0 : SPARE - V0 + wide_by].reshape(-1)
    small_got = small_got[:N_SMALL] + small_got[N_SMALL : 2 * N_SMALL]
    out_conv = small_got[: (KW + 1) * CPER].reshape(KW + 1, CPER)
    out_heads = small_got[(KW + 1) * CPER :].reshape(3, 1, SH)
    out_gu, gain_sum = ff_owned(got_ff, w_gu)
    out_gain_m = gain_sum[:, 0] / gain_mlp.astype(F32)
    late_sums = jnp.sum(got_late.astype(F32), axis=0)
    out_rows = lax.ppermute(late_sums, ("dp", "ctx"), back_pairs)
    return (
        block_out[None],
        grad_tokens[None],
        out_gain_a[None],
        out_gain_m[None],
        out_qkv[None],
        out_rows[:n_o][None],
        out_zx[None],
        out_side[None],
        out_rows[n_o : n_o + n_out][None],
        out_gu[None],
        out_rows[n_o + n_out :][None],
        out_conv[1:][None],
        out_conv[0][None],
        out_heads[0],
        out_heads[1],
        out_heads[2],
    )


def solution(mesh):
    rows = P("dp", "ctx", None)
    vector = P(None, ("dp", "ctx"))
    matrix = P(None, ("dp", "ctx"), None)
    taps = P(None, None, ("dp", "ctx"))
    weights = (vector, vector) + (matrix,) * 7 + (taps, vector, P(), P(), P())
    return jax.shard_map(
        per_device,
        mesh=mesh,
        in_specs=(rows, rows) + weights,
        out_specs=(rows, rows) + weights,
        check_vma=False,
    )
```

```python
import functools
import math

import jax
import jax.numpy as jnp
from jax import lax
from jax.experimental import pallas as pl
from jax.experimental.pallas import tpu as pltpu
from jax.sharding import PartitionSpec as P

D = 1024
HEAD_SIZE = 64
SH = 24
SP = 64
SN = 128
FF = 2048
KW = 4
BLK = 128
INNER = 1536
CONV = 1792
QUERY_FEATURES = 512
KEY_FEATURES = 128
NDP = 16
NCTX = 8
CHIPS = 4
HPD = SH // NCTX
XC = INNER // NCTX
HID = FF // NCTX
CV = 2 * SN + XC
X0, Z0, Q0 = 2 * SN, CV, CV + XC
K0, V0, T0 = Q0 + HEAD_SIZE, Q0 + 2 * HEAD_SIZE, Q0 + 3 * HEAD_SIZE
GA = Q0 + 4 * HEAD_SIZE
SPARE = T0 + HPD
NDEV = NDP * NCTX
CPER = CONV // NDEV
N_SMALL = (KW + 1) * CPER + 3 * SH

EPSILON = 1e-05
ROPE_BASE = 100000000000.0
F32 = jnp.float32
BF16 = jnp.bfloat16
HIGHEST = lax.Precision.HIGHEST


def dot(a, b, dims):
    return lax.dot_general(a, b, (dims, ((), ())), preferred_element_type=F32)


def mm(a, b):
    return dot(a, b, ((1,), (0,)))


def mm_nt(a, b):
    return dot(a, b, ((1,), (1,)))


def mm_tn(a, b):
    return dot(a, b, ((0,), (0,)))


def chip_shift(array, by):
    return lax.ppermute(array, "ctx", [(i, (i + 2 * by) % NCTX) for i in range(NCTX)])


def core_swap(array):
    return lax.ppermute(array, "ctx", [(i, i ^ 1) for i in range(NCTX)])


def gather_rows(own):
    same = [own, chip_shift(own, -1), None, chip_shift(own, 1)]
    same[2] = chip_shift(own, 2)
    other = [None] * CHIPS
    for k in (0, 1, 3, 2):
        other[k] = core_swap(same[k])
    return [block for pair in zip(same, other) for block in pair]


def swap_add(keep, pass_on):
    return {k: keep[k] + core_swap(pass_on[k]).astype(F32) for k in (2, 1, 3, 0)}


def shift_sum(both, shifted):
    total = both[0]
    for k in (1, 3, 2):
        total = total + shifted[k].astype(F32)
    return total


def scatter_rows(keep, pass_on):
    both = swap_add(keep, pass_on)
    return shift_sum(both, {k: chip_shift(both[k].astype(BF16), k) for k in (2, 1, 3)})


def dp_gather(own):
    return lax.all_to_all(jnp.broadcast_to(own[None], (NDP,) + own.shape), "dp", 0, 0)


def to_owners(parts):
    return lax.all_to_all(parts, ("dp", "ctx"), 0, 0)


SMEM = pl.BlockSpec(memory_space=pltpu.SMEM)
VMEM = pl.BlockSpec(memory_space=pltpu.VMEM)
LIMIT = 48 * 1024 * 1024


def after(value, *others):
    return lax.optimization_barrier((value,) + others)[0]


def mlp_kernel(*refs):
    normed, cot, (gu, down) = refs[:NCTX], refs[NCTX : 2 * NCTX], refs[2 * NCTX : 2 * NCTX + 2]
    outs = refs[2 * NCTX + 2 :]
    keep_n, pass_n, keep_d, pass_d = (outs[CHIPS * m : CHIPS * (m + 1)] for m in range(4))
    hid, dgu = outs[4 * CHIPS :]
    for k in (2, 1, 3, 0):
        normed2 = jnp.concatenate([normed[2 * k][...], normed[2 * k + 1][...]], axis=0)
        upstream = jnp.concatenate([cot[2 * k][...], cot[2 * k + 1][...]], axis=0)
        gate_up = mm(normed2, gu[...])
        gate_half, up_half = gate_up[:, :HID], gate_up[:, HID:]
        sigmoid_gate = sigmoid(gate_half)
        silu_gate = gate_half * sigmoid_gate
        hidden = (silu_gate * up_half).astype(BF16)
        grad_hidden = mm_nt(upstream, down[...])
        grad_gate = grad_hidden * up_half * (sigmoid_gate + silu_gate * (1.0 - sigmoid_gate))
        grad_gate_up = jnp.concatenate([grad_gate, grad_hidden * silu_gate], axis=1).astype(BF16)
        at = pl.ds(2 * k * BLK, 2 * BLK)
        hid[at, :] = hidden
        dgu[at, :] = grad_gate_up
        grad_normed2 = mm_nt(grad_gate_up, gu[...])
        keep_n[k][...] = grad_normed2[:BLK]
        pass_n[k][...] = grad_normed2[BLK:].astype(BF16)
        out = mm(hidden, down[...])
        keep_d[k][...] = out[:BLK]
        pass_d[k][...] = out[BLK:].astype(BF16)


def mlp(normed2, cot, gu, down):
    shape = jax.ShapeDtypeStruct
    keep, passed = [shape((BLK, D), F32)] * CHIPS, [shape((BLK, D), BF16)] * CHIPS
    rows = NCTX * BLK
    outs = pl.pallas_call(
        mlp_kernel,
        out_shape=keep + passed + keep + passed
        + [shape((rows, HID), BF16), shape((rows, 2 * HID), BF16)],
        cost_estimate=pl.CostEstimate(
            flops=2 * rows * D * HID * 6, bytes_accessed=12_000_000, transcendentals=0
        ),
        compiler_params=pltpu.CompilerParams(vmem_limit_bytes=LIMIT),
        name="feed_forward",
    )(*normed2, *cot, gu, down)
    parts = [outs[CHIPS * m : CHIPS * (m + 1)] for m in range(4)]
    return [*parts, *outs[4 * CHIPS :]]


def tn_kernel(n_left, *refs):
    left = jnp.concatenate([r[...] for r in refs[:n_left]], axis=0)
    right = jnp.concatenate([r[...] for r in refs[n_left:-1]], axis=0)
    refs[-1][...] = mm_tn(left, right).astype(BF16)


def mixed_back_kernel(mixed, w_mix, grad_down, *refs):
    middle_low, (late, grad_mixed) = refs[:NCTX], refs[NCTX:]
    for r in range(NCTX):
        grad_mixed[pl.ds(r * BLK, BLK), :] = mm_nt(middle_low[r][...], w_mix[...])
    middle = jnp.concatenate([r[...] for r in middle_low], axis=0)
    grad_mix = mm_tn(mixed[...], middle)
    down = grad_down[...].astype(F32)
    n_o, n_out, n_down = HEAD_SIZE // NDP, XC // NDP, HID // NDP
    for i in range(NDP):
        at = HEAD_SIZE + i * n_out
        rows = [
            grad_mix[i * n_o : (i + 1) * n_o],
            grad_mix[at : at + n_out],
            down[i * n_down : (i + 1) * n_down],
        ]
        late[i] = jnp.concatenate(rows, axis=0).astype(BF16)


def mixed_back(mixed, w_mix, grad_down, middle_low):
    shape = jax.ShapeDtypeStruct
    return pl.pallas_call(
        mixed_back_kernel,
        out_shape=(
            shape((NDP, (HEAD_SIZE + XC + HID) // NDP, D), BF16),
            shape((NCTX * BLK, HEAD_SIZE + XC), F32),
        ),
        cost_estimate=pl.CostEstimate(
            flops=4_000_000_000, bytes_accessed=6_000_000, transcendentals=0
        ),
        compiler_params=pltpu.CompilerParams(vmem_limit_bytes=LIMIT),
        name="mixed_back",
    )(mixed, w_mix, grad_down, *middle_low)


def mixer_grad_kernel(normed, grad_proj, small, out):
    total = mm_tn(normed[...], grad_proj[...])
    out[:, :V0] = total[:, :V0].astype(BF16)
    out[:, V0:] = (total[:, V0:] + small[...]).astype(BF16)


def mixer_grad(normed, grad_proj, small):
    return pl.pallas_call(
        mixer_grad_kernel,
        out_shape=jax.ShapeDtypeStruct((D, GA), BF16),
        cost_estimate=pl.CostEstimate(
            flops=2 * D * GA * NCTX * BLK, bytes_accessed=8_000_000, transcendentals=0
        ),
        compiler_params=pltpu.CompilerParams(vmem_limit_bytes=LIMIT),
        name="mixer_weight_grad",
    )(normed, grad_proj, small)


def columns_kernel(zx, side, qkv, gu, small, mixers, ff):
    zx, side, qkv, gu, small = (v[...].astype(F32) for v in (zx, side, qkv, gu, small))
    for j in range(NCTX):
        head = j // (NCTX // 2) * HEAD_SIZE
        key = QUERY_FEATURES + head
        value = QUERY_FEATURES + KEY_FEATURES + head
        own = [
            side[:, : 2 * SN],
            zx[:, INNER + j * XC : INNER + (j + 1) * XC],
            zx[:, j * XC : (j + 1) * XC],
            qkv[:, j * HEAD_SIZE : (j + 1) * HEAD_SIZE],
            qkv[:, key : key + HEAD_SIZE],
            qkv[:, value : value + HEAD_SIZE],
            side[:, 2 * SN + j * HPD : 2 * SN + (j + 1) * HPD],
            small,
        ]
        own = jnp.concatenate(own, axis=1).astype(BF16)
        units = [gu[:, j * HID : (j + 1) * HID], gu[:, FF + j * HID : FF + (j + 1) * HID]]
        units = jnp.concatenate(units, axis=1).astype(BF16)
        for i in range(NDP):
            mixers[i * NCTX + j] = own
            ff[i * NCTX + j] = units


def columns_for_all(zx, side, qkv, gu, small):
    rows = zx.shape[0]
    shape = jax.ShapeDtypeStruct
    return pl.pallas_call(
        columns_kernel,
        out_shape=(shape((NDEV, rows, GA), BF16), shape((NDEV, rows, 2 * HID), BF16)),
        cost_estimate=pl.CostEstimate(flops=0, bytes_accessed=3_000_000, transcendentals=0),
        compiler_params=pltpu.CompilerParams(vmem_limit_bytes=LIMIT),
        name="columns",
    )(zx, side, qkv, gu, small)


def source_sum(parts, j):
    total = parts[j].astype(F32)
    for i in range(1, NDP):
        total = total + parts[i * NCTX + j].astype(F32)
    return total


def row_dot(weight, grad):
    total = jnp.sum(weight[...].astype(F32) * grad, axis=1, keepdims=True)
    return jnp.broadcast_to(total, (total.shape[0], SN))


def mixers_owned_kernel(parts, zx, side, qkv, out_zx, out_side, out_qkv, out_gain, out_small):
    got = [source_sum(parts, j) for j in range(NCTX)]
    half = NCTX // 2
    grads = jnp.concatenate([g[:, Z0:Q0] for g in got] + [g[:, X0:Z0] for g in got], axis=1)
    out_zx[...] = grads
    gain = row_dot(zx, grads)
    both = sum(g[:, :X0] for g in got[1:]) + got[0][:, :X0]
    grads = jnp.concatenate([both] + [g[:, T0 : T0 + HPD] for g in got], axis=1)
    out_side[...] = grads
    gain = gain + row_dot(side, grads)
    pairs = [sum(g[:, K0:T0] for g in got[h + 1 : h + half]) + got[h][:, K0:T0] for h in (0, half)]
    grads = jnp.concatenate(
        [g[:, Q0:K0] for g in got]
        + [p[:, :HEAD_SIZE] for p in pairs]
        + [p[:, HEAD_SIZE:] for p in pairs],
        axis=1,
    )
    out_qkv[...] = grads
    out_gain[...] = gain + row_dot(qkv, grads)
    out_small[...] = sum(g[:, V0:] for g in got[1:]) + got[0][:, V0:]


def mixers_owned(parts, zx, side, qkv):
    shape = jax.ShapeDtypeStruct
    rows = zx.shape[0]
    return pl.pallas_call(
        mixers_owned_kernel,
        out_shape=(
            shape(zx.shape, F32),
            shape(side.shape, F32),
            shape(qkv.shape, F32),
            shape((rows, SN), F32),
            shape((rows, SN), F32),
        ),
        cost_estimate=pl.CostEstimate(flops=0, bytes_accessed=3_000_000, transcendentals=0),
        compiler_params=pltpu.CompilerParams(vmem_limit_bytes=LIMIT),
        name="mixers_owned",
    )(parts, zx, side, qkv)


def ff_owned_kernel(parts, gu, out_gu, out_gain):
    got = [source_sum(parts, j) for j in range(NCTX)]
    grads = jnp.concatenate([g[:, :HID] for g in got] + [g[:, HID:] for g in got], axis=1)
    out_gu[...] = grads
    out_gain[...] = row_dot(gu, grads)


def ff_owned(parts, gu):
    shape = jax.ShapeDtypeStruct
    return pl.pallas_call(
        ff_owned_kernel,
        out_shape=(shape(gu.shape, F32), shape((gu.shape[0], SN), F32)),
        cost_estimate=pl.CostEstimate(flops=0, bytes_accessed=2_000_000, transcendentals=0),
        compiler_params=pltpu.CompilerParams(vmem_limit_bytes=LIMIT),
        name="ff_owned",
    )(parts, gu)


def tn_sum(left, right):
    n, m = left[0].shape[1], right[0].shape[1]
    return pl.pallas_call(
        functools.partial(tn_kernel, len(left)),
        out_shape=jax.ShapeDtypeStruct((n, m), BF16),
        cost_estimate=pl.CostEstimate(
            flops=2 * n * m * NCTX * BLK, bytes_accessed=6 * n * m, transcendentals=0
        ),
        compiler_params=pltpu.CompilerParams(vmem_limit_bytes=LIMIT),
        name="weight_grad",
    )(*left, *right)


def rms_factor(hidden_in):
    return lax.rsqrt(jnp.mean(hidden_in * hidden_in, axis=-1, keepdims=True) + EPSILON)


def norm_back(hidden_in, factor, gain, upstream):
    scaled = upstream * gain
    inner = jnp.mean(scaled * hidden_in, axis=-1, keepdims=True)
    return factor * scaled - hidden_in * (factor * factor * factor) * inner


def rope_tables():
    exponent = -(2.0 * jnp.arange(HEAD_SIZE // 2, dtype=F32)) / HEAD_SIZE
    inverse = jnp.power(jnp.float32(ROPE_BASE), exponent)
    angles = jnp.arange(NCTX * BLK, dtype=F32)[:, None] * inverse[None, :]
    cosine, sine = jnp.cos(angles), jnp.sin(angles)
    return (
        jnp.concatenate([cosine] * 4, axis=1),
        jnp.concatenate([-sine, sine, -sine, sine], axis=1),
    )


def sigmoid(v):
    return 1.0 / (1.0 + jnp.exp(-v))


def softplus(v):
    return jnp.maximum(v, 0.0) + jnp.log1p(jnp.exp(-jnp.abs(v)))


def exact(a, b, dims):
    return lax.dot_general(a, b, (dims, ((), ())), precision=HIGHEST, preferred_element_type=F32)


def wide(columns):
    return jnp.concatenate([jnp.broadcast_to(c, (BLK, SP)) for c in columns], axis=1)


def tall(scalars):
    return jnp.concatenate([jnp.broadcast_to(c, (SP, SN)) for c in scalars], axis=0)


def head_sums(v):
    return [jnp.sum(v[:, h * SP : (h + 1) * SP], axis=1, keepdims=True) for h in range(HPD)]


def iota(shape, dim):
    return lax.broadcasted_iota(jnp.int32, shape, dim)


def turn(v):
    first = (iota(v.shape, 1) // (HEAD_SIZE // 2)) % 2 == 0
    return jnp.where(
        first, pltpu.roll(v, 2 * HEAD_SIZE - HEAD_SIZE // 2, 1), pltpu.roll(v, HEAD_SIZE // 2, 1)
    )


def rotated(block, cosine, sine):
    both = block[:, Q0:V0]
    return both * cosine + turn(both) * sine


def block_rows(a):
    return pl.ds(a * BLK, BLK)


def held_rows(places, a):
    return pl.ds(pl.multiple_of(places[a] * BLK, BLK), BLK)


def probabilities(query, keys, a):
    scores = mm_nt(query, keys) * (1.0 / math.sqrt(HEAD_SIZE))
    seen = iota(scores.shape, 0) + a * BLK >= iota(scores.shape, 1)
    scores = jnp.where(seen, scores, -jnp.inf)
    weights = jnp.exp(scores - jnp.max(scores, axis=1, keepdims=True))
    return weights / jnp.sum(weights, axis=1, keepdims=True)


class Block:
    def __init__(self, block, tail, taps, conv_b, heads):
        conv_in = block[:, :CV].astype(BF16).astype(F32)
        self.next_tail = conv_in[BLK - 8 :]
        extended = jnp.concatenate([tail, conv_in], axis=0)
        self.shifted = [extended[8 - d : 8 - d + BLK] for d in range(KW)]
        total = conv_b
        for d in range(KW):
            total = total + taps[KW - 1 - d : KW - d] * self.shifted[d]
        self.total = total
        self.sig = sigmoid(total)
        low = (total * self.sig).astype(BF16)
        self.b, self.c, self.x = low[:, :SN], low[:, SN : 2 * SN], low[:, 2 * SN :]
        raw = block[:, V0:] + heads[1:2]
        self.step = softplus(raw)
        self.step_slope = sigmoid(raw)
        self.rate = -jnp.exp(heads[0:1]) * heads[3:4]
        self.decay = self.rate * self.step
        self.tri = (iota((BLK, BLK), 0) >= iota((BLK, BLK), 1)).astype(F32)
        self.cum = exact(self.tri, self.decay, ((1,), (0,)))
        cum_t, step_t = self.cum.T, self.step.T
        lanes = [HEAD_SIZE + h for h in range(HPD)]
        self.cum_cols = [self.cum[:, l : l + 1] for l in lanes]
        self.last = [self.cum[BLK - 1 :, l : l + 1] for l in lanes]
        self.step_cols = [self.step[:, l : l + 1] for l in lanes]
        self.step_rows = [step_t[l : l + 1] for l in lanes]
        causal = iota((BLK, BLK), 0) >= iota((BLK, BLK), 1)
        self.fade = [
            jnp.exp(jnp.where(causal, self.cum_cols[h] - cum_t[l : l + 1], -jnp.inf))
            for h, l in enumerate(lanes)
        ]
        self.inter = mm_nt(self.c, self.b)
        self.to_end = [jnp.exp(self.last[h] - self.cum_cols[h]) for h in range(HPD)]
        self.grown = wide([jnp.exp(v) for v in self.cum_cols])
        self.weight = wide([self.to_end[h] * self.step_cols[h] for h in range(HPD)])
        self.carry = tall([jnp.exp(v) for v in self.last])
        self.skip = wide([heads[2:3, l : l + 1] for l in lanes])
        self.x32 = self.x.astype(F32)

    def head(self, v, h):
        return v[:, h * SP : (h + 1) * SP]


def forward_kernel(*refs):
    places, wa, cosine, sine, taps, conv_b, heads = refs[:7]
    tokens, refs = refs[7 : 7 + NCTX], refs[7 + NCTX :]
    normed, proj, mixed, y_out, states, keys, values = refs
    gain = wa[:, V0:].astype(F32).T[SPARE - V0 : SPARE - V0 + 1]
    for r in range(NCTX):
        token = tokens[r][...].astype(F32)
        low = (token * rms_factor(token) * gain).astype(BF16)
        normed[block_rows(r), :] = low
        proj[block_rows(r), :] = mm(low, wa[...])
    taps, conv_b, heads = taps[...], conv_b[...], heads[...]
    tail = jnp.zeros((8, CV), F32)
    state = jnp.zeros((XC, SN), F32)
    for a in range(NCTX):
        at = held_rows(places, a)
        block = proj[at, :]
        both = rotated(block, cosine[block_rows(a), :], sine[block_rows(a), :]).astype(BF16)
        keys[block_rows(a), :] = both[:, HEAD_SIZE:]
        values[block_rows(a), :] = block[:, V0:T0].astype(BF16)
        seen = pl.ds(0, (a + 1) * BLK)
        probs = probabilities(both[:, :HEAD_SIZE], keys[seen, :], a)
        attended = mm(probs.astype(BF16), values[seen, :])
        now = Block(block, tail, taps, conv_b, heads)
        tail = now.next_tail
        states[a] = state
        y = now.grown * mm_nt(now.c, state.astype(BF16)) + now.skip * now.x32
        inner = [
            mm((now.inter * now.fade[h] * now.step_rows[h]).astype(BF16), now.head(now.x, h))
            for h in range(HPD)
        ]
        y = y + jnp.concatenate(inner, axis=1)
        y_out[block_rows(a), :] = y
        state = now.carry * state + mm_tn((now.x32 * now.weight).astype(BF16), now.b)
        gate = block[:, Z0:Q0]
        gated = y * gate * sigmoid(gate)
        mixed[at, :] = jnp.concatenate([attended, gated], axis=1).astype(BF16)


def mix_kernel(mixed, w_mix, *outs):
    for k in (2, 1, 3, 0):
        out = mm(mixed[pl.ds(2 * k * BLK, 2 * BLK), :], w_mix[...])
        outs[k][...] = out[:BLK]
        outs[CHIPS + k][...] = out[BLK:].astype(BF16)


def mix(mixed, w_mix):
    shape = jax.ShapeDtypeStruct
    return pl.pallas_call(
        mix_kernel,
        out_shape=[shape((BLK, D), F32)] * CHIPS + [shape((BLK, D), BF16)] * CHIPS,
        cost_estimate=pl.CostEstimate(
            flops=2 * NCTX * BLK * D * 256, bytes_accessed=4_000_000, transcendentals=0
        ),
        compiler_params=pltpu.CompilerParams(vmem_limit_bytes=LIMIT),
        name="mix",
    )(mixed, w_mix)


def backward_kernel(*refs):
    places, proj, cosine, sine, taps, conv_b, heads, y_in, states, wa, grad_mixed = refs[:11]
    refs = refs[11:]
    grad_proj, conv_out, head_out, skip_out = refs[:4]
    keep, passed = refs[4 : 4 + CHIPS], refs[4 + CHIPS : 4 + 2 * CHIPS]
    keys, values, grad_q, grad_k, grad_v = refs[4 + 2 * CHIPS :]
    taps, conv_b, heads = taps[...], conv_b[...], heads[...]
    queries = []
    for a in range(NCTX):
        block = proj[held_rows(places, a), :]
        both = rotated(block, cosine[block_rows(a), :], sine[block_rows(a), :]).astype(BF16)
        queries.append(both[:, :HEAD_SIZE])
        keys[block_rows(a), :] = both[:, HEAD_SIZE:]
        values[block_rows(a), :] = block[:, V0:T0].astype(BF16)
    for a in reversed(range(NCTX)):
        seen = pl.ds(0, (a + 1) * BLK)
        grad_attended = grad_mixed[held_rows(places, a), :][:, :HEAD_SIZE].astype(BF16)
        probs = probabilities(queries[a], keys[seen, :], a)
        grad_probs = mm_nt(grad_attended, values[seen, :])
        delta = jnp.sum(probs * grad_probs, axis=1, keepdims=True)
        grad_scores = (probs * (grad_probs - delta) * (1.0 / math.sqrt(HEAD_SIZE))).astype(BF16)
        grad_q[block_rows(a), :] = mm(grad_scores, keys[seen, :])
        more_k = mm_tn(grad_scores, queries[a])
        more_v = mm_tn(probs.astype(BF16), grad_attended)
        if a < NCTX - 1:
            more_k = more_k + grad_k[seen, :]
            more_v = more_v + grad_v[seen, :]
        grad_k[seen, :] = more_k
        grad_v[seen, :] = more_v
    adjoint = jnp.zeros((XC, SN), F32)
    later = jnp.zeros((8, CV), F32)
    conv_rows = [jnp.zeros((1, CV), F32) for _ in range(KW + 1)]
    grad_alog = jnp.zeros((1, SN), F32)
    grad_bias = jnp.zeros((1, SN), F32)
    grad_skip = jnp.zeros((1, XC), F32)
    lane = iota((BLK, SN), 1)
    for a in reversed(range(NCTX)):
        at = held_rows(places, a)
        block = proj[at, :]
        if a:
            tail = proj[held_rows(places, a - 1), :][BLK - 8 :, :CV].astype(BF16).astype(F32)
        else:
            tail = jnp.zeros((8, CV), F32)
        now = Block(block, tail, taps, conv_b, heads)
        gate = block[:, Z0:Q0]
        sig = sigmoid(gate)
        grad_gated = grad_mixed[at, :][:, HEAD_SIZE:]
        y = y_in[block_rows(a), :]
        grad_gate = grad_gated * y * (sig + gate * sig * (1.0 - sig))
        grad_y = grad_gated * gate * sig
        grad_skip = grad_skip + jnp.sum(grad_y * now.x32, axis=0, keepdims=True)
        grad_y_low = grad_y.astype(BF16)
        grad_x = now.skip * grad_y
        state = states[a]
        state_low = state.astype(BF16)
        grad_inter = jnp.zeros((BLK, BLK), F32)
        cum_cols, step_cols, inner = [], [], []
        for h in range(HPD):
            gy, x = now.head(grad_y_low, h), now.head(now.x, h)
            grad_mixing = mm_nt(gy, x)
            faded = now.fade[h] * now.step_rows[h]
            grad_inter = grad_inter + grad_mixing * faded
            inner.append(mm_tn((now.inter * faded).astype(BF16), gy))
            product = grad_mixing * now.inter * now.fade[h]
            column = jnp.sum(product.T, axis=1, keepdims=True)
            row = jnp.sum(product * now.step_rows[h], axis=1, keepdims=True)
            step_cols.append(column)
            cum_cols.append(row - column * now.step_cols[h])
        grad_x = grad_x + jnp.concatenate(inner, axis=1)
        grad_inter = grad_inter.astype(BF16)
        grown_y = grad_y * now.grown
        grown_low = grown_y.astype(BF16)
        grad_c = mm(grad_inter, now.b) + mm(grown_low, state_low)
        from_state = head_sums(grown_y * mm_nt(now.c, state_low))
        adjoint_low = adjoint.astype(BF16)
        weighted = (now.x32 * now.weight).astype(BF16)
        grad_b = mm_tn(grad_inter, now.c) + mm(weighted, adjoint_low)
        grad_weighted = mm_nt(now.b, adjoint_low)
        grad_x = grad_x + grad_weighted * now.weight
        grad_weight = head_sums(grad_weighted * now.x32)
        carried = now.carry * adjoint * state
        grad_cum = jnp.zeros((BLK, SN), F32)
        grad_step = jnp.zeros((BLK, SN), F32)
        for h in range(HPD):
            step_col = step_cols[h] + grad_weight[h] * now.to_end[h]
            pulled = grad_weight[h] * now.to_end[h] * now.step_cols[h]
            last = jnp.sum(pulled, axis=0, keepdims=True) + jnp.sum(
                jnp.sum(carried[h * SP : (h + 1) * SP], axis=1, keepdims=True), axis=0, keepdims=True
            )
            cum_col = cum_cols[h] + from_state[h] - pulled
            cum_col = jnp.where(iota((BLK, 1), 0) == BLK - 1, cum_col + last, cum_col)
            here = lane == HEAD_SIZE + h
            grad_cum = jnp.where(here, cum_col, grad_cum)
            grad_step = jnp.where(here, step_col, grad_step)
        adjoint = now.carry * adjoint + mm_tn(grown_low, now.c)
        grad_decay = exact(now.tri, grad_cum, ((0,), (0,)))
        grad_alog = grad_alog + jnp.sum(grad_decay * now.decay, axis=0, keepdims=True)
        grad_dt = (grad_step + grad_decay * now.rate) * now.step_slope
        grad_bias = grad_bias + jnp.sum(grad_dt, axis=0, keepdims=True)
        grad_total = jnp.concatenate([grad_b, grad_c, grad_x], axis=1) * (
            now.sig + now.total * now.sig * (1.0 - now.sig)
        )
        conv_rows[0] = conv_rows[0] + jnp.sum(grad_total, axis=0, keepdims=True)
        extended = jnp.concatenate([grad_total, later], axis=0)
        later = grad_total[:8]
        grad_conv_in = jnp.zeros((BLK, CV), F32)
        for d in range(KW):
            k = KW - 1 - d
            conv_rows[1 + k] = conv_rows[1 + k] + jnp.sum(
                grad_total * now.shifted[d], axis=0, keepdims=True
            )
            grad_conv_in = grad_conv_in + taps[k : k + 1] * extended[d : d + BLK]
        both = jnp.concatenate([grad_q[block_rows(a), :], grad_k[block_rows(a), :]], axis=1)
        both = both * cosine[block_rows(a), :] + turn(both * sine[block_rows(a), :])
        grad_dt = pltpu.roll(grad_dt, HEAD_SIZE, 1)[:, :HEAD_SIZE]
        grad_proj[at, :] = jnp.concatenate(
            [grad_conv_in, grad_gate, both, grad_v[block_rows(a), :], grad_dt], axis=1
        ).astype(BF16)
    for k in (2, 1, 3, 0):
        out = mm_nt(grad_proj[pl.ds(2 * k * BLK, 2 * BLK), :], wa[...])
        keep[k][...] = out[:BLK]
        passed[k][...] = out[BLK:].astype(BF16)
    conv_out[...] = jnp.concatenate(conv_rows + [jnp.zeros((3, CV), F32)], axis=0)
    head_out[...] = jnp.concatenate([grad_alog, grad_bias, jnp.zeros((6, SN), F32)], axis=0)
    skip_out[...] = jnp.concatenate([grad_skip, jnp.zeros((7, XC), F32)], axis=0)


def mixers_forward(places, wa, cosine, sine, taps, conv_b, heads, tokens):
    shape = jax.ShapeDtypeStruct
    rows = NCTX * BLK
    return pl.pallas_call(
        forward_kernel,
        in_specs=[SMEM] + [VMEM] * (6 + NCTX),
        out_specs=[VMEM] * 5,
        out_shape=(
            shape((rows, D), BF16),
            shape((rows, GA), F32),
            shape((rows, HEAD_SIZE + XC), BF16),
            shape((rows, XC), F32),
            shape((NCTX, XC, SN), F32),
        ),
        scratch_shapes=[pltpu.VMEM((rows, HEAD_SIZE), BF16)] * 2,
        cost_estimate=pl.CostEstimate(
            flops=16_000_000_000, bytes_accessed=16_000_000, transcendentals=4_000_000
        ),
        compiler_params=pltpu.CompilerParams(vmem_limit_bytes=LIMIT),
        name="mixers_forward",
    )(places, wa, cosine, sine, taps, conv_b, heads, *tokens)


def mixers_backward(
    places, proj, cosine, sine, taps, conv_b, heads, y, states, wa, grad_mixed
):
    shape = jax.ShapeDtypeStruct
    rows = NCTX * BLK
    return pl.pallas_call(
        backward_kernel,
        in_specs=[SMEM] + [VMEM] * 10,
        out_specs=[VMEM] * (4 + 2 * CHIPS),
        out_shape=(
            shape((rows, GA), BF16),
            shape((8, CV), F32),
            shape((8, SN), F32),
            shape((8, XC), F32),
            *[shape((BLK, D), F32)] * CHIPS,
            *[shape((BLK, D), BF16)] * CHIPS,
        ),
        scratch_shapes=[pltpu.VMEM((rows, HEAD_SIZE), BF16)] * 2
        + [pltpu.VMEM((rows, HEAD_SIZE), F32)] * 3,
        cost_estimate=pl.CostEstimate(
            flops=38_000_000_000, bytes_accessed=16_000_000, transcendentals=8_000_000
        ),
        compiler_params=pltpu.CompilerParams(vmem_limit_bytes=LIMIT),
        name="mixers_backward",
    )(places, proj, cosine, sine, taps, conv_b, heads, y, states, wa, grad_mixed)


def per_device(
    tokens,
    cotangent,
    gain_attn,
    gain_mlp,
    w_qkv,
    w_o,
    w_zx,
    w_side,
    w_out,
    w_gu,
    w_down,
    conv_w,
    conv_bias,
    a_log,
    dt_bias,
    d_skip,
):
    ctx = lax.axis_index("ctx")
    chip, core = ctx // 2, ctx % 2
    blocks = jnp.arange(NCTX, dtype=jnp.int32)
    places = 2 * ((blocks // 2 - chip + CHIPS) % CHIPS) + (core ^ (blocks % 2))
    own_tokens, own_cot = tokens[0], cotangent[0]
    gain_attn, gain_mlp, conv_w, conv_bias = gain_attn[0], gain_mlp[0], conv_w[0], conv_bias[0]
    w_qkv, w_o, w_zx, w_side, w_out, w_gu, w_down = (
        w[0] for w in (w_qkv, w_o, w_zx, w_side, w_out, w_gu, w_down)
    )
    rows = w_qkv.shape[0]

    conv_small = jnp.concatenate([conv_bias, conv_w.reshape(-1)])
    wide_by = -(-conv_small.shape[0] // rows)
    conv_small = jnp.pad(conv_small, (0, rows * wide_by - conv_small.shape[0]))
    small = jnp.concatenate(
        [gain_attn[:, None], gain_mlp[:, None], conv_small.reshape(rows, wide_by)], axis=1
    )
    small = jnp.pad(small, ((0, 0), (0, GA - SPARE - 2 - wide_by)))
    mixers_cols, ff_cols = columns_for_all(w_zx, w_side, w_qkv, w_gu, small)
    wa = to_owners(mixers_cols).reshape(D, GA)
    gain_a = wa[:, SPARE].astype(F32)
    gain_m = wa[:, SPARE + 1].astype(F32)
    small = wa[:, SPARE + 2 : SPARE + 2 + wide_by].reshape(NDEV, rows * wide_by).astype(F32)
    bias_all = small[:, :CPER].reshape(CONV)
    taps_all = small[:, CPER : (KW + 1) * CPER].reshape(-1, KW, CPER)
    taps_all = taps_all.transpose(1, 0, 2).reshape(KW, CONV)
    mine = lambda v: jnp.concatenate(
        [v[..., INNER:], lax.dynamic_slice_in_dim(v, ctx * XC, XC, v.ndim - 1)], axis=-1
    )
    taps, conv_b = mine(taps_all), mine(bias_all)

    tok = gather_rows(own_tokens)
    swap_pairs = [(c, NCTX * (c % NDP) + c // NDP) for c in range(NDEV)]
    back_pairs = [(t, s) for s, t in swap_pairs]
    n_o, n_out, n_down = w_o.shape[0], w_out.shape[0], w_down.shape[0]
    mix_rows = lax.ppermute(
        jnp.concatenate([w_o, w_out, w_down], axis=0), ("dp", "ctx"), swap_pairs
    )
    late = dp_gather(after(mix_rows, wa))
    by_rows = lambda at, size: late[:, at : at + size].reshape(NDP * size, D)
    w_mix = jnp.concatenate([by_rows(0, n_o), by_rows(n_o, n_out)], axis=0)
    down = by_rows(n_o + n_out, n_down)
    gu = to_owners(after(ff_cols, late)).reshape(D, 2 * HID)
    cot = gather_rows(after(own_cot, wa))

    cosine, sine = rope_tables()
    heads = lambda v: jnp.pad(
        lax.dynamic_slice_in_dim(v[0], ctx * HPD, HPD, 0), (HEAD_SIZE, HEAD_SIZE - HPD)
    )
    head_rows = jnp.stack([heads(a_log), heads(dt_bias), heads(d_skip), heads(jnp.ones_like(a_log))])
    head_rows = jnp.pad(head_rows, ((0, 4), (0, 0)))
    shared = (cosine, sine, taps, conv_b[None], head_rows)
    normed, proj, mixed, y, states = mixers_forward(places, wa, *shared, tok)
    parts = [after(v, *cot) for v in mix(mixed, w_mix)]
    own_residual = own_tokens.astype(F32)
    middle = own_residual + scatter_rows(parts[:CHIPS], parts[CHIPS:])

    factor_m = rms_factor(middle)
    normed2 = gather_rows((middle * factor_m * gain_m[None, :]).astype(BF16))
    keep_n, pass_n, keep_d, pass_d, hidden, grad_gate_up = mlp(normed2, cot, gu, down)
    both_n = swap_add(keep_n, pass_n)
    sent_n = {k: both_n[k].astype(BF16) for k in (2, 1, 3)}
    grad_normed2 = shift_sum(both_n, {k: chip_shift(v, k) for k, v in sent_n.items()})
    hidden, grad_gate_up = (after(v, *sent_n.values()) for v in (hidden, grad_gate_up))
    grad_middle = own_cot.astype(F32) + norm_back(middle, factor_m, gain_m[None, :], grad_normed2)
    middle_low = gather_rows(grad_middle.astype(BF16))
    grad_gu = tn_sum(normed2, [grad_gate_up])
    grad_down = tn_sum([hidden], cot)
    both_d = swap_add(keep_d, pass_d)
    sent_d = {k: after(both_d[k].astype(BF16), *middle_low) for k in (2, 1, 3)}

    late_terms, grad_mixed = mixed_back(mixed, w_mix, grad_down, middle_low)
    ff_terms = grad_gu.reshape(NDEV, rows, 2 * HID)
    got_ff = to_owners(ff_terms)
    grad_proj, conv_terms, head_sum, skip_sum, *parts = mixers_backward(
        places,
        proj,
        *shared,
        y,
        states,
        wa,
        after(grad_mixed, got_ff, late_terms, *sent_d.values()),
    )
    got_late = lax.all_to_all(late_terms, "dp", 0, 0)
    got_d = {k: chip_shift(v, k) for k, v in sent_d.items()}
    place = lambda v, at, size: lax.dynamic_update_slice_in_dim(
        jnp.zeros(v.shape[:-1] + (size,), F32), v, at, v.ndim - 1
    )
    conv_terms = conv_terms[: KW + 1]
    conv_terms = jnp.concatenate(
        [place(conv_terms[:, X0:], ctx * XC, INNER), conv_terms[:, :X0]], axis=1
    )
    conv_terms = conv_terms.reshape(KW + 1, NDEV, CPER).transpose(1, 0, 2)
    skip_terms = jnp.sum(skip_sum[0].reshape(HPD, SP), axis=1)
    head_terms = jnp.stack([*head_sum[:2, HEAD_SIZE : HEAD_SIZE + HPD], skip_terms])
    head_terms = place(head_terms, ctx * HPD, SH).reshape(1, 3 * SH)
    small_terms = jnp.concatenate(
        [conv_terms.reshape(NDEV, -1), jnp.broadcast_to(head_terms, (NDEV, 3 * SH))], axis=1
    )
    coarse = small_terms.astype(BF16).astype(F32)
    small_terms = jnp.concatenate([coarse, small_terms - coarse], axis=1)
    wide_by = -(-2 * N_SMALL // rows)
    small_terms = jnp.pad(small_terms, ((0, 0), (0, rows * wide_by - 2 * N_SMALL)))
    small_terms = small_terms.reshape(D, wide_by)
    small_terms = jnp.pad(
        small_terms, ((0, 0), (SPARE - V0, GA - SPARE - wide_by))
    )
    grad_proj = after(grad_proj, got_late, *got_d.values())
    grad_wa = mixer_grad(normed, grad_proj, small_terms)
    parts = [after(v, grad_wa) for v in parts]
    both = swap_add(parts[:CHIPS], parts[CHIPS:])
    grad_normed = shift_sum(both, {k: chip_shift(both[k].astype(BF16), k) for k in (2, 1, 3)})
    grad_tokens = grad_middle + norm_back(
        own_residual, rms_factor(own_residual), gain_a[None, :], grad_normed
    )
    both_d[0] = after(both_d[0], both[3])
    block_out = middle + shift_sum(both_d, got_d)
    got = to_owners(grad_wa.reshape(NDEV, rows, GA))
    out_zx, out_side, out_qkv, gain_sum, small_got = mixers_owned(got, w_zx, w_side, w_qkv)
    out_gain_a = gain_sum[:, 0] / gain_attn.astype(F32)
    small_got = small_got[:, SPARE - V0 : SPARE - V0 + wide_by].reshape(-1)
    small_got = small_got[:N_SMALL] + small_got[N_SMALL : 2 * N_SMALL]
    out_conv = small_got[: (KW + 1) * CPER].reshape(KW + 1, CPER)
    out_heads = small_got[(KW + 1) * CPER :].reshape(3, 1, SH)
    out_gu, gain_sum = ff_owned(after(got_ff, both[3]), w_gu)
    out_gain_m = gain_sum[:, 0] / gain_mlp.astype(F32)
    late_sums = jnp.sum(after(got_late, both[3]).astype(F32), axis=0)
    out_rows = lax.ppermute(late_sums, ("dp", "ctx"), back_pairs)
    return (
        block_out[None],
        grad_tokens[None],
        out_gain_a[None],
        out_gain_m[None],
        out_qkv[None],
        out_rows[:n_o][None],
        out_zx[None],
        out_side[None],
        out_rows[n_o : n_o + n_out][None],
        out_gu[None],
        out_rows[n_o + n_out :][None],
        out_conv[1:][None],
        out_conv[0][None],
        out_heads[0],
        out_heads[1],
        out_heads[2],
    )


def solution(mesh):
    rows = P("dp", "ctx", None)
    vector = P(None, ("dp", "ctx"))
    matrix = P(None, ("dp", "ctx"), None)
    taps = P(None, None, ("dp", "ctx"))
    weights = (vector, vector) + (matrix,) * 7 + (taps, vector, P(), P(), P())
    return jax.shard_map(
        per_device,
        mesh=mesh,
        in_specs=(rows, rows) + weights,
        out_specs=(rows, rows) + weights,
        check_vma=False,
    )
```

```python
import functools
import math

import jax
import jax.numpy as jnp
from jax import lax
from jax.experimental import pallas as pl
from jax.experimental.pallas import tpu as pltpu
from jax.sharding import PartitionSpec as P

D = 1024
HEAD_SIZE = 64
SH = 24
SP = 64
SN = 128
FF = 2048
KW = 4
BLK = 128
INNER = 1536
CONV = 1792
QUERY_FEATURES = 512
KEY_FEATURES = 128
NDP = 16
NCTX = 8
CHIPS = 4
HPD = SH // NCTX
XC = INNER // NCTX
HID = FF // NCTX
CV = 2 * SN + XC
X0, Z0, Q0 = 2 * SN, CV, CV + XC
K0, V0, T0 = Q0 + HEAD_SIZE, Q0 + 2 * HEAD_SIZE, Q0 + 3 * HEAD_SIZE
GA = Q0 + 4 * HEAD_SIZE
SPARE = T0 + HPD
NDEV = NDP * NCTX
CPER = CONV // NDEV
N_SMALL = (KW + 1) * CPER + 3 * SH

EPSILON = 1e-05
ROPE_BASE = 100000000000.0
F32 = jnp.float32
BF16 = jnp.bfloat16
HIGHEST = lax.Precision.HIGHEST


def dot(a, b, dims):
    return lax.dot_general(a, b, (dims, ((), ())), preferred_element_type=F32)


def mm(a, b):
    return dot(a, b, ((1,), (0,)))


def mm_nt(a, b):
    return dot(a, b, ((1,), (1,)))


def mm_tn(a, b):
    return dot(a, b, ((0,), (0,)))


def chip_shift(array, by):
    return lax.ppermute(array, "ctx", [(i, (i + 2 * by) % NCTX) for i in range(NCTX)])


def core_swap(array):
    return lax.ppermute(array, "ctx", [(i, i ^ 1) for i in range(NCTX)])


def gather_rows(own):
    same = [own, chip_shift(own, -1), None, chip_shift(own, 1)]
    same[2] = chip_shift(own, 2)
    other = [None] * CHIPS
    for k in (0, 1, 3, 2):
        other[k] = core_swap(same[k])
    return [block for pair in zip(same, other) for block in pair]


def swap_add(keep, pass_on):
    return {k: keep[k] + core_swap(pass_on[k]).astype(F32) for k in (2, 1, 3, 0)}


def shift_sum(both, shifted):
    total = both[0]
    for k in (1, 3, 2):
        total = total + shifted[k].astype(F32)
    return total


def scatter_rows(keep, pass_on):
    both = swap_add(keep, pass_on)
    return shift_sum(both, {k: chip_shift(both[k].astype(BF16), k) for k in (2, 1, 3)})


def to_owners(parts):
    return lax.all_to_all(parts, ("dp", "ctx"), 0, 0)


SMEM = pl.BlockSpec(memory_space=pltpu.SMEM)
VMEM = pl.BlockSpec(memory_space=pltpu.VMEM)
LIMIT = 32 * 1024 * 1024


def after(value, *others):
    return lax.optimization_barrier((value,) + others)[0]


def mlp_kernel(*refs):
    normed, cot, (gu, down) = refs[:NCTX], refs[NCTX : 2 * NCTX], refs[2 * NCTX : 2 * NCTX + 2]
    outs = refs[2 * NCTX + 2 :]
    keep_n, pass_n, keep_d, pass_d = (outs[CHIPS * m : CHIPS * (m + 1)] for m in range(4))
    hid, dgu = outs[4 * CHIPS :]
    for k in (2, 1, 3, 0):
        normed2 = jnp.concatenate([normed[2 * k][...], normed[2 * k + 1][...]], axis=0)
        upstream = jnp.concatenate([cot[2 * k][...], cot[2 * k + 1][...]], axis=0)
        gate_up = mm(normed2, gu[...])
        gate_half, up_half = gate_up[:, :HID], gate_up[:, HID:]
        sigmoid_gate = sigmoid(gate_half)
        silu_gate = gate_half * sigmoid_gate
        hidden = (silu_gate * up_half).astype(BF16)
        grad_hidden = mm_nt(upstream, down[...])
        grad_gate = grad_hidden * up_half * (sigmoid_gate + silu_gate * (1.0 - sigmoid_gate))
        grad_gate_up = jnp.concatenate([grad_gate, grad_hidden * silu_gate], axis=1).astype(BF16)
        at = pl.ds(2 * k * BLK, 2 * BLK)
        hid[at, :] = hidden
        dgu[at, :] = grad_gate_up
        grad_normed2 = mm_nt(grad_gate_up, gu[...])
        keep_n[k][...] = grad_normed2[:BLK]
        pass_n[k][...] = grad_normed2[BLK:].astype(BF16)
        out = mm(hidden, down[...])
        keep_d[k][...] = out[:BLK]
        pass_d[k][...] = out[BLK:].astype(BF16)


def mlp(normed2, cot, gu, down):
    shape = jax.ShapeDtypeStruct
    keep, passed = [shape((BLK, D), F32)] * CHIPS, [shape((BLK, D), BF16)] * CHIPS
    rows = NCTX * BLK
    outs = pl.pallas_call(
        mlp_kernel,
        out_shape=keep + passed + keep + passed
        + [shape((rows, HID), BF16), shape((rows, 2 * HID), BF16)],
        cost_estimate=pl.CostEstimate(
            flops=2 * rows * D * HID * 6, bytes_accessed=12_000_000, transcendentals=0
        ),
        compiler_params=pltpu.CompilerParams(vmem_limit_bytes=LIMIT),
        name="feed_forward",
    )(*normed2, *cot, gu, down)
    parts = [outs[CHIPS * m : CHIPS * (m + 1)] for m in range(4)]
    return [*parts, *outs[4 * CHIPS :]]


def tn_kernel(n_left, *refs):
    left = jnp.concatenate([r[...] for r in refs[:n_left]], axis=0)
    right = jnp.concatenate([r[...] for r in refs[n_left:-1]], axis=0)
    refs[-1][...] = mm_tn(left, right).astype(BF16)


def mixed_back_kernel(mixed, w_mix, grad_down, *refs):
    middle_low, (late, grad_mixed) = refs[:NCTX], refs[NCTX:]
    for r in range(NCTX):
        grad_mixed[pl.ds(r * BLK, BLK), :] = mm_nt(middle_low[r][...], w_mix[...])
    middle = jnp.concatenate([r[...] for r in middle_low], axis=0)
    grad_mix = mm_tn(mixed[...], middle)
    down = grad_down[...].astype(F32)
    n_o, n_out, n_down = HEAD_SIZE // NDP, XC // NDP, HID // NDP
    for i in range(NDP):
        at = HEAD_SIZE + i * n_out
        rows = [
            grad_mix[i * n_o : (i + 1) * n_o],
            grad_mix[at : at + n_out],
            down[i * n_down : (i + 1) * n_down],
        ]
        late[i] = jnp.concatenate(rows, axis=0).astype(BF16)


def mixed_back(mixed, w_mix, grad_down, middle_low):
    shape = jax.ShapeDtypeStruct
    return pl.pallas_call(
        mixed_back_kernel,
        out_shape=(
            shape((NDP, (HEAD_SIZE + XC + HID) // NDP, D), BF16),
            shape((NCTX * BLK, HEAD_SIZE + XC), F32),
        ),
        cost_estimate=pl.CostEstimate(
            flops=4_000_000_000, bytes_accessed=6_000_000, transcendentals=0
        ),
        compiler_params=pltpu.CompilerParams(vmem_limit_bytes=LIMIT),
        name="mixed_back",
    )(mixed, w_mix, grad_down, *middle_low)


def mixer_grad_kernel(normed, grad_proj, small, out):
    total = mm_tn(normed[...], grad_proj[...])
    out[:, :V0] = total[:, :V0].astype(BF16)
    out[:, V0:] = (total[:, V0:] + small[...]).astype(BF16)


def mixer_grad(normed, grad_proj, small):
    return pl.pallas_call(
        mixer_grad_kernel,
        out_shape=jax.ShapeDtypeStruct((D, GA), BF16),
        cost_estimate=pl.CostEstimate(
            flops=2 * D * GA * NCTX * BLK, bytes_accessed=8_000_000, transcendentals=0
        ),
        compiler_params=pltpu.CompilerParams(vmem_limit_bytes=LIMIT),
        name="mixer_weight_grad",
    )(normed, grad_proj, small)


def columns_kernel(zx, side, qkv, gu, small, mixers, ff):
    zx, side, qkv, gu, small = (v[...].astype(F32) for v in (zx, side, qkv, gu, small))
    for j in range(NCTX):
        head = j // (NCTX // 2) * HEAD_SIZE
        key = QUERY_FEATURES + head
        value = QUERY_FEATURES + KEY_FEATURES + head
        own = [
            side[:, : 2 * SN],
            zx[:, INNER + j * XC : INNER + (j + 1) * XC],
            zx[:, j * XC : (j + 1) * XC],
            qkv[:, j * HEAD_SIZE : (j + 1) * HEAD_SIZE],
            qkv[:, key : key + HEAD_SIZE],
            qkv[:, value : value + HEAD_SIZE],
            side[:, 2 * SN + j * HPD : 2 * SN + (j + 1) * HPD],
            small,
        ]
        own = jnp.concatenate(own, axis=1).astype(BF16)
        units = [gu[:, j * HID : (j + 1) * HID], gu[:, FF + j * HID : FF + (j + 1) * HID]]
        units = jnp.concatenate(units, axis=1).astype(BF16)
        for i in range(NDP):
            mixers[i * NCTX + j] = own
            ff[i * NCTX + j] = units


def columns_for_all(zx, side, qkv, gu, small):
    rows = zx.shape[0]
    shape = jax.ShapeDtypeStruct
    return pl.pallas_call(
        columns_kernel,
        out_shape=(shape((NDEV, rows, GA), BF16), shape((NDEV, rows, 2 * HID), BF16)),
        cost_estimate=pl.CostEstimate(flops=0, bytes_accessed=3_000_000, transcendentals=0),
        compiler_params=pltpu.CompilerParams(vmem_limit_bytes=LIMIT),
        name="columns",
    )(zx, side, qkv, gu, small)


def source_sum(parts, j):
    total = parts[j].astype(F32)
    for i in range(1, NDP):
        total = total + parts[i * NCTX + j].astype(F32)
    return total


def row_dot(weight, grad):
    total = jnp.sum(weight[...].astype(F32) * grad, axis=1, keepdims=True)
    return jnp.broadcast_to(total, (total.shape[0], SN))


def mixers_owned_kernel(parts, zx, side, qkv, out_zx, out_side, out_qkv, out_gain, out_small):
    got = [source_sum(parts, j) for j in range(NCTX)]
    half = NCTX // 2
    grads = jnp.concatenate([g[:, Z0:Q0] for g in got] + [g[:, X0:Z0] for g in got], axis=1)
    out_zx[...] = grads
    gain = row_dot(zx, grads)
    both = sum(g[:, :X0] for g in got[1:]) + got[0][:, :X0]
    grads = jnp.concatenate([both] + [g[:, T0 : T0 + HPD] for g in got], axis=1)
    out_side[...] = grads
    gain = gain + row_dot(side, grads)
    pairs = [sum(g[:, K0:T0] for g in got[h + 1 : h + half]) + got[h][:, K0:T0] for h in (0, half)]
    grads = jnp.concatenate(
        [g[:, Q0:K0] for g in got]
        + [p[:, :HEAD_SIZE] for p in pairs]
        + [p[:, HEAD_SIZE:] for p in pairs],
        axis=1,
    )
    out_qkv[...] = grads
    out_gain[...] = gain + row_dot(qkv, grads)
    out_small[...] = sum(g[:, V0:] for g in got[1:]) + got[0][:, V0:]


def mixers_owned(parts, zx, side, qkv):
    shape = jax.ShapeDtypeStruct
    rows = zx.shape[0]
    return pl.pallas_call(
        mixers_owned_kernel,
        out_shape=(
            shape(zx.shape, F32),
            shape(side.shape, F32),
            shape(qkv.shape, F32),
            shape((rows, SN), F32),
            shape((rows, SN), F32),
        ),
        cost_estimate=pl.CostEstimate(flops=0, bytes_accessed=3_000_000, transcendentals=0),
        compiler_params=pltpu.CompilerParams(vmem_limit_bytes=LIMIT),
        name="mixers_owned",
    )(parts, zx, side, qkv)


def ff_owned_kernel(parts, gu, out_gu, out_gain):
    got = [source_sum(parts, j) for j in range(NCTX)]
    grads = jnp.concatenate([g[:, :HID] for g in got] + [g[:, HID:] for g in got], axis=1)
    out_gu[...] = grads
    out_gain[...] = row_dot(gu, grads)


def ff_owned(parts, gu):
    shape = jax.ShapeDtypeStruct
    return pl.pallas_call(
        ff_owned_kernel,
        out_shape=(shape(gu.shape, F32), shape((gu.shape[0], SN), F32)),
        cost_estimate=pl.CostEstimate(flops=0, bytes_accessed=2_000_000, transcendentals=0),
        compiler_params=pltpu.CompilerParams(vmem_limit_bytes=LIMIT),
        name="ff_owned",
    )(parts, gu)


def tn_sum(left, right):
    n, m = left[0].shape[1], right[0].shape[1]
    return pl.pallas_call(
        functools.partial(tn_kernel, len(left)),
        out_shape=jax.ShapeDtypeStruct((n, m), BF16),
        cost_estimate=pl.CostEstimate(
            flops=2 * n * m * NCTX * BLK, bytes_accessed=6 * n * m, transcendentals=0
        ),
        compiler_params=pltpu.CompilerParams(vmem_limit_bytes=LIMIT),
        name="weight_grad",
    )(*left, *right)


def rms_factor(hidden_in):
    return lax.rsqrt(jnp.mean(hidden_in * hidden_in, axis=-1, keepdims=True) + EPSILON)


def norm_back(hidden_in, factor, gain, upstream):
    scaled = upstream * gain
    inner = jnp.mean(scaled * hidden_in, axis=-1, keepdims=True)
    return factor * scaled - hidden_in * (factor * factor * factor) * inner


def rope_tables():
    exponent = -(2.0 * jnp.arange(HEAD_SIZE // 2, dtype=F32)) / HEAD_SIZE
    inverse = jnp.power(jnp.float32(ROPE_BASE), exponent)
    angles = jnp.arange(NCTX * BLK, dtype=F32)[:, None] * inverse[None, :]
    cosine, sine = jnp.cos(angles), jnp.sin(angles)
    return (
        jnp.concatenate([cosine] * 4, axis=1),
        jnp.concatenate([-sine, sine, -sine, sine], axis=1),
    )


def sigmoid(v):
    return 1.0 / (1.0 + jnp.exp(-v))


def softplus(v):
    return jnp.maximum(v, 0.0) + jnp.log1p(jnp.exp(-jnp.abs(v)))


def exact(a, b, dims):
    return lax.dot_general(a, b, (dims, ((), ())), precision=HIGHEST, preferred_element_type=F32)


def wide(columns):
    return jnp.concatenate([jnp.broadcast_to(c, (BLK, SP)) for c in columns], axis=1)


def tall(scalars):
    return jnp.concatenate([jnp.broadcast_to(c, (SP, SN)) for c in scalars], axis=0)


def head_sums(v):
    return [jnp.sum(v[:, h * SP : (h + 1) * SP], axis=1, keepdims=True) for h in range(HPD)]


def iota(shape, dim):
    return lax.broadcasted_iota(jnp.int32, shape, dim)


def turn(v):
    first = (iota(v.shape, 1) // (HEAD_SIZE // 2)) % 2 == 0
    return jnp.where(
        first, pltpu.roll(v, 2 * HEAD_SIZE - HEAD_SIZE // 2, 1), pltpu.roll(v, HEAD_SIZE // 2, 1)
    )


def rotated(block, cosine, sine):
    both = block[:, Q0:V0]
    return both * cosine + turn(both) * sine


def block_rows(a):
    return pl.ds(a * BLK, BLK)


def held_rows(places, a):
    return pl.ds(pl.multiple_of(places[a] * BLK, BLK), BLK)


def probabilities(query, keys, a):
    scores = mm_nt(query, keys) * (1.0 / math.sqrt(HEAD_SIZE))
    seen = iota(scores.shape, 0) + a * BLK >= iota(scores.shape, 1)
    scores = jnp.where(seen, scores, -jnp.inf)
    weights = jnp.exp(scores - jnp.max(scores, axis=1, keepdims=True))
    return weights / jnp.sum(weights, axis=1, keepdims=True)


class Block:
    def __init__(self, block, tail, taps, conv_b, heads):
        conv_in = block[:, :CV].astype(BF16).astype(F32)
        self.next_tail = conv_in[BLK - 8 :]
        extended = jnp.concatenate([tail, conv_in], axis=0)
        self.shifted = [extended[8 - d : 8 - d + BLK] for d in range(KW)]
        total = conv_b
        for d in range(KW):
            total = total + taps[KW - 1 - d : KW - d] * self.shifted[d]
        self.total = total
        self.sig = sigmoid(total)
        low = (total * self.sig).astype(BF16)
        self.b, self.c, self.x = low[:, :SN], low[:, SN : 2 * SN], low[:, 2 * SN :]
        raw = block[:, V0:] + heads[1:2]
        self.step = softplus(raw)
        self.step_slope = sigmoid(raw)
        self.rate = -jnp.exp(heads[0:1]) * heads[3:4]
        self.decay = self.rate * self.step
        self.tri = (iota((BLK, BLK), 0) >= iota((BLK, BLK), 1)).astype(F32)
        self.cum = exact(self.tri, self.decay, ((1,), (0,)))
        cum_t, step_t = self.cum.T, self.step.T
        lanes = [HEAD_SIZE + h for h in range(HPD)]
        self.cum_cols = [self.cum[:, l : l + 1] for l in lanes]
        self.last = [self.cum[BLK - 1 :, l : l + 1] for l in lanes]
        self.step_cols = [self.step[:, l : l + 1] for l in lanes]
        self.step_rows = [step_t[l : l + 1] for l in lanes]
        causal = iota((BLK, BLK), 0) >= iota((BLK, BLK), 1)
        self.fade = [
            jnp.exp(jnp.where(causal, self.cum_cols[h] - cum_t[l : l + 1], -jnp.inf))
            for h, l in enumerate(lanes)
        ]
        self.inter = mm_nt(self.c, self.b)
        self.to_end = [jnp.exp(self.last[h] - self.cum_cols[h]) for h in range(HPD)]
        self.grown = wide([jnp.exp(v) for v in self.cum_cols])
        self.weight = wide([self.to_end[h] * self.step_cols[h] for h in range(HPD)])
        self.carry = tall([jnp.exp(v) for v in self.last])
        self.skip = wide([heads[2:3, l : l + 1] for l in lanes])
        self.x32 = self.x.astype(F32)

    def head(self, v, h):
        return v[:, h * SP : (h + 1) * SP]


def forward_kernel(*refs):
    places, wa, cosine, sine, taps, conv_b, heads = refs[:7]
    tokens, refs = refs[7 : 7 + NCTX], refs[7 + NCTX :]
    normed, proj, mixed, y_out, states, keys, values = refs
    gain = wa[:, V0:].astype(F32).T[SPARE - V0 : SPARE - V0 + 1]
    for r in range(NCTX):
        token = tokens[r][...].astype(F32)
        low = (token * rms_factor(token) * gain).astype(BF16)
        normed[block_rows(r), :] = low
        proj[block_rows(r), :] = mm(low, wa[...])
    taps, conv_b, heads = taps[...], conv_b[...], heads[...]
    tail = jnp.zeros((8, CV), F32)
    state = jnp.zeros((XC, SN), F32)
    for a in range(NCTX):
        at = held_rows(places, a)
        block = proj[at, :]
        both = rotated(block, cosine[block_rows(a), :], sine[block_rows(a), :]).astype(BF16)
        keys[block_rows(a), :] = both[:, HEAD_SIZE:]
        values[block_rows(a), :] = block[:, V0:T0].astype(BF16)
        seen = pl.ds(0, (a + 1) * BLK)
        probs = probabilities(both[:, :HEAD_SIZE], keys[seen, :], a)
        attended = mm(probs.astype(BF16), values[seen, :])
        now = Block(block, tail, taps, conv_b, heads)
        tail = now.next_tail
        states[a] = state
        y = now.grown * mm_nt(now.c, state.astype(BF16)) + now.skip * now.x32
        inner = [
            mm((now.inter * now.fade[h] * now.step_rows[h]).astype(BF16), now.head(now.x, h))
            for h in range(HPD)
        ]
        y = y + jnp.concatenate(inner, axis=1)
        y_out[block_rows(a), :] = y
        state = now.carry * state + mm_tn((now.x32 * now.weight).astype(BF16), now.b)
        gate = block[:, Z0:Q0]
        gated = y * gate * sigmoid(gate)
        mixed[at, :] = jnp.concatenate([attended, gated], axis=1).astype(BF16)


def mix_kernel(mixed, w_mix, *outs):
    for k in (2, 1, 3, 0):
        out = mm(mixed[pl.ds(2 * k * BLK, 2 * BLK), :], w_mix[...])
        outs[k][...] = out[:BLK]
        outs[CHIPS + k][...] = out[BLK:].astype(BF16)


def mix(mixed, w_mix):
    shape = jax.ShapeDtypeStruct
    return pl.pallas_call(
        mix_kernel,
        out_shape=[shape((BLK, D), F32)] * CHIPS + [shape((BLK, D), BF16)] * CHIPS,
        cost_estimate=pl.CostEstimate(
            flops=2 * NCTX * BLK * D * 256, bytes_accessed=4_000_000, transcendentals=0
        ),
        compiler_params=pltpu.CompilerParams(vmem_limit_bytes=LIMIT),
        name="mix",
    )(mixed, w_mix)


def backward_kernel(*refs):
    places, proj, cosine, sine, taps, conv_b, heads, y_in, states, wa, grad_mixed = refs[:11]
    refs = refs[11:]
    grad_proj, conv_out, head_out, skip_out = refs[:4]
    keep, passed = refs[4 : 4 + CHIPS], refs[4 + CHIPS : 4 + 2 * CHIPS]
    keys, values, grad_q, grad_k, grad_v = refs[4 + 2 * CHIPS :]
    taps, conv_b, heads = taps[...], conv_b[...], heads[...]
    queries = []
    for a in range(NCTX):
        block = proj[held_rows(places, a), :]
        both = rotated(block, cosine[block_rows(a), :], sine[block_rows(a), :]).astype(BF16)
        queries.append(both[:, :HEAD_SIZE])
        keys[block_rows(a), :] = both[:, HEAD_SIZE:]
        values[block_rows(a), :] = block[:, V0:T0].astype(BF16)
    for a in reversed(range(NCTX)):
        seen = pl.ds(0, (a + 1) * BLK)
        grad_attended = grad_mixed[held_rows(places, a), :][:, :HEAD_SIZE].astype(BF16)
        probs = probabilities(queries[a], keys[seen, :], a)
        grad_probs = mm_nt(grad_attended, values[seen, :])
        delta = jnp.sum(probs * grad_probs, axis=1, keepdims=True)
        grad_scores = (probs * (grad_probs - delta) * (1.0 / math.sqrt(HEAD_SIZE))).astype(BF16)
        grad_q[block_rows(a), :] = mm(grad_scores, keys[seen, :])
        more_k = mm_tn(grad_scores, queries[a])
        more_v = mm_tn(probs.astype(BF16), grad_attended)
        if a < NCTX - 1:
            more_k = more_k + grad_k[seen, :]
            more_v = more_v + grad_v[seen, :]
        grad_k[seen, :] = more_k
        grad_v[seen, :] = more_v
    adjoint = jnp.zeros((XC, SN), F32)
    later = jnp.zeros((8, CV), F32)
    conv_rows = [jnp.zeros((1, CV), F32) for _ in range(KW + 1)]
    grad_alog = jnp.zeros((1, SN), F32)
    grad_bias = jnp.zeros((1, SN), F32)
    grad_skip = jnp.zeros((1, XC), F32)
    lane = iota((BLK, SN), 1)
    for a in reversed(range(NCTX)):
        at = held_rows(places, a)
        block = proj[at, :]
        if a:
            tail = proj[held_rows(places, a - 1), :][BLK - 8 :, :CV].astype(BF16).astype(F32)
        else:
            tail = jnp.zeros((8, CV), F32)
        now = Block(block, tail, taps, conv_b, heads)
        gate = block[:, Z0:Q0]
        sig = sigmoid(gate)
        grad_gated = grad_mixed[at, :][:, HEAD_SIZE:]
        y = y_in[block_rows(a), :]
        grad_gate = grad_gated * y * (sig + gate * sig * (1.0 - sig))
        grad_y = grad_gated * gate * sig
        grad_skip = grad_skip + jnp.sum(grad_y * now.x32, axis=0, keepdims=True)
        grad_y_low = grad_y.astype(BF16)
        grad_x = now.skip * grad_y
        state = states[a]
        state_low = state.astype(BF16)
        grad_inter = jnp.zeros((BLK, BLK), F32)
        cum_cols, step_cols, inner = [], [], []
        for h in range(HPD):
            gy, x = now.head(grad_y_low, h), now.head(now.x, h)
            grad_mixing = mm_nt(gy, x)
            faded = now.fade[h] * now.step_rows[h]
            grad_inter = grad_inter + grad_mixing * faded
            inner.append(mm_tn((now.inter * faded).astype(BF16), gy))
            product = grad_mixing * now.inter * now.fade[h]
            column = jnp.sum(product.T, axis=1, keepdims=True)
            row = jnp.sum(product * now.step_rows[h], axis=1, keepdims=True)
            step_cols.append(column)
            cum_cols.append(row - column * now.step_cols[h])
        grad_x = grad_x + jnp.concatenate(inner, axis=1)
        grad_inter = grad_inter.astype(BF16)
        grown_y = grad_y * now.grown
        grown_low = grown_y.astype(BF16)
        grad_c = mm(grad_inter, now.b) + mm(grown_low, state_low)
        from_state = head_sums(grown_y * mm_nt(now.c, state_low))
        adjoint_low = adjoint.astype(BF16)
        weighted = (now.x32 * now.weight).astype(BF16)
        grad_b = mm_tn(grad_inter, now.c) + mm(weighted, adjoint_low)
        grad_weighted = mm_nt(now.b, adjoint_low)
        grad_x = grad_x + grad_weighted * now.weight
        grad_weight = head_sums(grad_weighted * now.x32)
        carried = now.carry * adjoint * state
        grad_cum = jnp.zeros((BLK, SN), F32)
        grad_step = jnp.zeros((BLK, SN), F32)
        for h in range(HPD):
            step_col = step_cols[h] + grad_weight[h] * now.to_end[h]
            pulled = grad_weight[h] * now.to_end[h] * now.step_cols[h]
            last = jnp.sum(pulled, axis=0, keepdims=True) + jnp.sum(
                jnp.sum(carried[h * SP : (h + 1) * SP], axis=1, keepdims=True), axis=0, keepdims=True
            )
            cum_col = cum_cols[h] + from_state[h] - pulled
            cum_col = jnp.where(iota((BLK, 1), 0) == BLK - 1, cum_col + last, cum_col)
            here = lane == HEAD_SIZE + h
            grad_cum = jnp.where(here, cum_col, grad_cum)
            grad_step = jnp.where(here, step_col, grad_step)
        adjoint = now.carry * adjoint + mm_tn(grown_low, now.c)
        grad_decay = exact(now.tri, grad_cum, ((0,), (0,)))
        grad_alog = grad_alog + jnp.sum(grad_decay * now.decay, axis=0, keepdims=True)
        grad_dt = (grad_step + grad_decay * now.rate) * now.step_slope
        grad_bias = grad_bias + jnp.sum(grad_dt, axis=0, keepdims=True)
        grad_total = jnp.concatenate([grad_b, grad_c, grad_x], axis=1) * (
            now.sig + now.total * now.sig * (1.0 - now.sig)
        )
        conv_rows[0] = conv_rows[0] + jnp.sum(grad_total, axis=0, keepdims=True)
        extended = jnp.concatenate([grad_total, later], axis=0)
        later = grad_total[:8]
        grad_conv_in = jnp.zeros((BLK, CV), F32)
        for d in range(KW):
            k = KW - 1 - d
            conv_rows[1 + k] = conv_rows[1 + k] + jnp.sum(
                grad_total * now.shifted[d], axis=0, keepdims=True
            )
            grad_conv_in = grad_conv_in + taps[k : k + 1] * extended[d : d + BLK]
        both = jnp.concatenate([grad_q[block_rows(a), :], grad_k[block_rows(a), :]], axis=1)
        both = both * cosine[block_rows(a), :] + turn(both * sine[block_rows(a), :])
        grad_dt = pltpu.roll(grad_dt, HEAD_SIZE, 1)[:, :HEAD_SIZE]
        grad_proj[at, :] = jnp.concatenate(
            [grad_conv_in, grad_gate, both, grad_v[block_rows(a), :], grad_dt], axis=1
        ).astype(BF16)
    for k in (2, 1, 3, 0):
        out = mm_nt(grad_proj[pl.ds(2 * k * BLK, 2 * BLK), :], wa[...])
        keep[k][...] = out[:BLK]
        passed[k][...] = out[BLK:].astype(BF16)
    conv_out[...] = jnp.concatenate(conv_rows + [jnp.zeros((3, CV), F32)], axis=0)
    head_out[...] = jnp.concatenate([grad_alog, grad_bias, jnp.zeros((6, SN), F32)], axis=0)
    skip_out[...] = jnp.concatenate([grad_skip, jnp.zeros((7, XC), F32)], axis=0)


def mixers_forward(places, wa, cosine, sine, taps, conv_b, heads, tokens):
    shape = jax.ShapeDtypeStruct
    rows = NCTX * BLK
    return pl.pallas_call(
        forward_kernel,
        in_specs=[SMEM] + [VMEM] * (6 + NCTX),
        out_specs=[VMEM] * 5,
        out_shape=(
            shape((rows, D), BF16),
            shape((rows, GA), F32),
            shape((rows, HEAD_SIZE + XC), BF16),
            shape((rows, XC), F32),
            shape((NCTX, XC, SN), F32),
        ),
        scratch_shapes=[pltpu.VMEM((rows, HEAD_SIZE), BF16)] * 2,
        cost_estimate=pl.CostEstimate(
            flops=16_000_000_000, bytes_accessed=16_000_000, transcendentals=4_000_000
        ),
        compiler_params=pltpu.CompilerParams(vmem_limit_bytes=LIMIT),
        name="mixers_forward",
    )(places, wa, cosine, sine, taps, conv_b, heads, *tokens)


def mixers_backward(
    places, proj, cosine, sine, taps, conv_b, heads, y, states, wa, grad_mixed
):
    shape = jax.ShapeDtypeStruct
    rows = NCTX * BLK
    return pl.pallas_call(
        backward_kernel,
        in_specs=[SMEM] + [VMEM] * 10,
        out_specs=[VMEM] * (4 + 2 * CHIPS),
        out_shape=(
            shape((rows, GA), BF16),
            shape((8, CV), F32),
            shape((8, SN), F32),
            shape((8, XC), F32),
            *[shape((BLK, D), F32)] * CHIPS,
            *[shape((BLK, D), BF16)] * CHIPS,
        ),
        scratch_shapes=[pltpu.VMEM((rows, HEAD_SIZE), BF16)] * 2
        + [pltpu.VMEM((rows, HEAD_SIZE), F32)] * 3,
        cost_estimate=pl.CostEstimate(
            flops=38_000_000_000, bytes_accessed=16_000_000, transcendentals=8_000_000
        ),
        compiler_params=pltpu.CompilerParams(vmem_limit_bytes=LIMIT),
        name="mixers_backward",
    )(places, proj, cosine, sine, taps, conv_b, heads, y, states, wa, grad_mixed)


def per_device(
    tokens,
    cotangent,
    gain_attn,
    gain_mlp,
    w_qkv,
    w_o,
    w_zx,
    w_side,
    w_out,
    w_gu,
    w_down,
    conv_w,
    conv_bias,
    a_log,
    dt_bias,
    d_skip,
):
    ctx = lax.axis_index("ctx")
    chip, core = ctx // 2, ctx % 2
    blocks = jnp.arange(NCTX, dtype=jnp.int32)
    places = 2 * ((blocks // 2 - chip + CHIPS) % CHIPS) + (core ^ (blocks % 2))
    own_tokens, own_cot = tokens[0], cotangent[0]
    gain_attn, gain_mlp, conv_w, conv_bias = gain_attn[0], gain_mlp[0], conv_w[0], conv_bias[0]
    w_qkv, w_o, w_zx, w_side, w_out, w_gu, w_down = (
        w[0] for w in (w_qkv, w_o, w_zx, w_side, w_out, w_gu, w_down)
    )
    rows = w_qkv.shape[0]

    conv_small = jnp.concatenate([conv_bias, conv_w.reshape(-1)])
    wide_by = -(-conv_small.shape[0] // rows)
    conv_small = jnp.pad(conv_small, (0, rows * wide_by - conv_small.shape[0]))
    small = jnp.concatenate(
        [gain_attn[:, None], gain_mlp[:, None], conv_small.reshape(rows, wide_by)], axis=1
    )
    small = jnp.pad(small, ((0, 0), (0, GA - SPARE - 2 - wide_by)))
    mixers_cols, ff_cols = columns_for_all(w_zx, w_side, w_qkv, w_gu, small)
    wa = to_owners(mixers_cols).reshape(D, GA)
    gain_a = wa[:, SPARE].astype(F32)
    gain_m = wa[:, SPARE + 1].astype(F32)
    small = wa[:, SPARE + 2 : SPARE + 2 + wide_by].reshape(NDEV, rows * wide_by).astype(F32)
    bias_all = small[:, :CPER].reshape(CONV)
    taps_all = small[:, CPER : (KW + 1) * CPER].reshape(-1, KW, CPER)
    taps_all = taps_all.transpose(1, 0, 2).reshape(KW, CONV)
    mine = lambda v: jnp.concatenate(
        [v[..., INNER:], lax.dynamic_slice_in_dim(v, ctx * XC, XC, v.ndim - 1)], axis=-1
    )
    taps, conv_b = mine(taps_all), mine(bias_all)

    tok = gather_rows(own_tokens)
    swap_pairs = [(c, NCTX * (c % NDP) + c // NDP) for c in range(NDEV)]
    back_pairs = [(t, s) for s, t in swap_pairs]
    n_o, n_out, n_down = w_o.shape[0], w_out.shape[0], w_down.shape[0]
    mix_rows = lax.ppermute(
        jnp.concatenate([w_o, w_out, w_down], axis=0), ("dp", "ctx"), swap_pairs
    )
    late = jnp.broadcast_to(mix_rows[None], (NDP,) + mix_rows.shape)
    late = lax.all_to_all(after(late, wa), "dp", 0, 0)
    by_rows = lambda at, size: late[:, at : at + size].reshape(NDP * size, D)
    w_mix = jnp.concatenate([by_rows(0, n_o), by_rows(n_o, n_out)], axis=0)
    down = by_rows(n_o + n_out, n_down)
    gu = to_owners(after(ff_cols, late)).reshape(D, 2 * HID)
    cot = gather_rows(after(own_cot, wa))

    cosine, sine = rope_tables()
    heads = lambda v: jnp.pad(
        lax.dynamic_slice_in_dim(v[0], ctx * HPD, HPD, 0), (HEAD_SIZE, HEAD_SIZE - HPD)
    )
    head_rows = jnp.stack([heads(a_log), heads(dt_bias), heads(d_skip), heads(jnp.ones_like(a_log))])
    head_rows = jnp.pad(head_rows, ((0, 4), (0, 0)))
    shared = (cosine, sine, taps, conv_b[None], head_rows)
    normed, proj, mixed, y, states = mixers_forward(places, wa, *shared, tok)
    parts = [after(v, *cot) for v in mix(mixed, w_mix)]
    own_residual = own_tokens.astype(F32)
    middle = own_residual + scatter_rows(parts[:CHIPS], parts[CHIPS:])

    factor_m = rms_factor(middle)
    normed2 = gather_rows((middle * factor_m * gain_m[None, :]).astype(BF16))
    keep_n, pass_n, keep_d, pass_d, hidden, grad_gate_up = mlp(normed2, cot, gu, down)
    both_n = swap_add(keep_n, pass_n)
    sent_n = {k: both_n[k].astype(BF16) for k in (2, 1, 3)}
    grad_normed2 = shift_sum(both_n, {k: chip_shift(v, k) for k, v in sent_n.items()})
    hidden, grad_gate_up = (after(v, *sent_n.values()) for v in (hidden, grad_gate_up))
    grad_middle = own_cot.astype(F32) + norm_back(middle, factor_m, gain_m[None, :], grad_normed2)
    middle_low = gather_rows(grad_middle.astype(BF16))
    grad_gu = tn_sum(normed2, [grad_gate_up])
    grad_down = tn_sum([hidden], cot)
    both_d = swap_add(keep_d, pass_d)
    sent_d = {k: after(both_d[k].astype(BF16), *middle_low) for k in (2, 1, 3)}

    late_terms, grad_mixed = mixed_back(mixed, w_mix, grad_down, middle_low)
    ff_terms = grad_gu.reshape(NDEV, rows, 2 * HID)
    got_ff = to_owners(ff_terms)
    grad_proj, conv_terms, head_sum, skip_sum, *parts = mixers_backward(
        places,
        proj,
        *shared,
        y,
        states,
        wa,
        after(grad_mixed, got_ff, late_terms, *sent_d.values()),
    )
    got_late = lax.all_to_all(late_terms, "dp", 0, 0)
    got_d = {k: chip_shift(v, k) for k, v in sent_d.items()}
    place = lambda v, at, size: lax.dynamic_update_slice_in_dim(
        jnp.zeros(v.shape[:-1] + (size,), F32), v, at, v.ndim - 1
    )
    conv_terms = conv_terms[: KW + 1]
    conv_terms = jnp.concatenate(
        [place(conv_terms[:, X0:], ctx * XC, INNER), conv_terms[:, :X0]], axis=1
    )
    conv_terms = conv_terms.reshape(KW + 1, NDEV, CPER).transpose(1, 0, 2)
    skip_terms = jnp.sum(skip_sum[0].reshape(HPD, SP), axis=1)
    head_terms = jnp.stack([*head_sum[:2, HEAD_SIZE : HEAD_SIZE + HPD], skip_terms])
    head_terms = place(head_terms, ctx * HPD, SH).reshape(1, 3 * SH)
    small_terms = jnp.concatenate(
        [conv_terms.reshape(NDEV, -1), jnp.broadcast_to(head_terms, (NDEV, 3 * SH))], axis=1
    )
    coarse = small_terms.astype(BF16).astype(F32)
    small_terms = jnp.concatenate([coarse, small_terms - coarse], axis=1)
    wide_by = -(-2 * N_SMALL // rows)
    small_terms = jnp.pad(small_terms, ((0, 0), (0, rows * wide_by - 2 * N_SMALL)))
    small_terms = small_terms.reshape(D, wide_by)
    small_terms = jnp.pad(
        small_terms, ((0, 0), (SPARE - V0, GA - SPARE - wide_by))
    )
    grad_proj = after(grad_proj, got_late, *got_d.values())
    grad_wa = mixer_grad(normed, grad_proj, small_terms)
    parts = [after(v, grad_wa) for v in parts]
    both = swap_add(parts[:CHIPS], parts[CHIPS:])
    grad_normed = shift_sum(both, {k: chip_shift(both[k].astype(BF16), k) for k in (2, 1, 3)})
    grad_tokens = grad_middle + norm_back(
        own_residual, rms_factor(own_residual), gain_a[None, :], grad_normed
    )
    both_d[0] = after(both_d[0], both[3])
    block_out = middle + shift_sum(both_d, got_d)
    got = to_owners(grad_wa.reshape(NDEV, rows, GA))
    out_zx, out_side, out_qkv, gain_sum, small_got = mixers_owned(got, w_zx, w_side, w_qkv)
    out_gain_a = gain_sum[:, 0] / gain_attn.astype(F32)
    small_got = small_got[:, SPARE - V0 : SPARE - V0 + wide_by].reshape(-1)
    small_got = small_got[:N_SMALL] + small_got[N_SMALL : 2 * N_SMALL]
    out_conv = small_got[: (KW + 1) * CPER].reshape(KW + 1, CPER)
    out_heads = small_got[(KW + 1) * CPER :].reshape(3, 1, SH)
    out_gu, gain_sum = ff_owned(after(got_ff, both[3]), w_gu)
    out_gain_m = gain_sum[:, 0] / gain_mlp.astype(F32)
    late_sums = jnp.sum(after(got_late, both[3]).astype(F32), axis=0)
    out_rows = lax.ppermute(late_sums, ("dp", "ctx"), back_pairs)
    return (
        block_out[None],
        grad_tokens[None],
        out_gain_a[None],
        out_gain_m[None],
        out_qkv[None],
        out_rows[:n_o][None],
        out_zx[None],
        out_side[None],
        out_rows[n_o : n_o + n_out][None],
        out_gu[None],
        out_rows[n_o + n_out :][None],
        out_conv[1:][None],
        out_conv[0][None],
        out_heads[0],
        out_heads[1],
        out_heads[2],
    )


def solution(mesh):
    rows = P("dp", "ctx", None)
    vector = P(None, ("dp", "ctx"))
    matrix = P(None, ("dp", "ctx"), None)
    taps = P(None, None, ("dp", "ctx"))
    weights = (vector, vector) + (matrix,) * 7 + (taps, vector, P(), P(), P())
    return jax.shard_map(
        per_device,
        mesh=mesh,
        in_specs=(rows, rows) + weights,
        out_specs=(rows, rows) + weights,
        check_vma=False,
    )
```
